128 devices in a mesh: sample: 4 (over x_lo, core), space: 4 (over y), chan: 8 (over x_hi, z).
Axes of the slice: x: 4 (x_hi: 2, x_lo: 2; x = x_hi * 2 + x_lo), y: 4, z: 4, core: 2. Of those that a mesh axis runs over, the one named last changes fastest.
Arguments:
- volume: bfloat16 [16, 32, 32, 64, 128], P(None, 'sample', 'space', 'chan'), may hold values from -6 to 6
- fine_kernel: bfloat16 [3, 3, 3, 128, 256], replicated, may hold values from -0.109375 to 0.109375
- fine_bias: float32 [256], replicated, may hold values from -3 to 3
- deep_kernel: bfloat16 [3, 3, 3, 256, 256], replicated, may hold values from -0.078125 to 0.078125
- deep_bias: float32 [256], replicated, may hold values from -3 to 3
Outputs:
- deep_out: bfloat16 [16, 256, 16, 512], P(('sample', 'space'), 'chan')
The draws below stay inside these ranges and needn't reach their ends.
All inputs are finite; a program needn't handle non-finite values.
Results may differ from the reference program's by a relative error of at most 0.0048.
Values may be sent and summed in bfloat16 or wider, within the bound.
No kernel may reach another device: no remote copies, remote signals or barrier semaphores. Data moves between devices by JAX's collectives and lax.ppermute only.
A program may use at most 256 MiB of HBM per device.

```python
import jax
import jax.numpy as jnp
from jax import lax

CIN = 128
C2 = 256
BATCH = 16
NZ = 32
NX = 32
NY = 64


def block_levels(key, shape, shards, low, largest):
    def one(position, blocks):
        steps = jax.random.uniform(jax.random.fold_in(jax.random.fold_in(key, 6), position), (blocks,), jnp.float32, low / len(shards), largest / len(shards))
        return jnp.repeat(jnp.exp(steps), shape[position] // blocks).reshape((-1,) + (1,) * (len(shape) - position - 1))

    loudness = one(*shards[0])
    for cut in shards[1:]:
        loudness = loudness * one(*cut)
    return loudness


def gaussian(own_key, extent, deviation, limit, cuts=(), held_as=jnp.bfloat16):
    array = jax.random.normal(own_key, extent, jnp.float32) * deviation
    if len(cuts) > 0:
        array = block_levels(own_key, extent, cuts, -0.22, 0.18) * array
    return jnp.clip(array, min=-limit, max=limit).astype(held_as)


def setup_inputs(seed: int = 0) -> dict:
    seeds = jax.random.split(jax.random.key(seed), 6)
    return {
        "volume": gaussian(seeds[0], (BATCH, NZ, NX, NY, CIN), 1.0, 6.0, ((1, 4), (2, 4), (3, 8))),
        "fine_kernel": gaussian(seeds[1], (3, 3, 3, CIN, C2), (27 * CIN) ** -0.5, 0.109375),
        "fine_bias": gaussian(seeds[2], (C2,), 0.5, 3.0, (), jnp.float32),
        "deep_kernel": gaussian(seeds[3], (3, 3, 3, C2, C2), (27 * C2) ** -0.5, 0.078125),
        "deep_bias": gaussian(seeds[4], (C2,), 0.5, 3.0, (), jnp.float32),
    }


def conv_block(padded, kernel):
    depth = padded.shape[1] - 2
    rows = padded.shape[2] - 2
    cols = padded.shape[3] - 2
    total = None
    for dz in range(3):
        pieces = [padded[:, dz:dz + depth, dx:dx + rows, dy:dy + cols, :] for dx in range(3) for dy in range(3)]
        stacked = jnp.concatenate(pieces, axis=-1)
        flat = kernel[dz].reshape(9 * kernel.shape[3], kernel.shape[4])
        term = lax.dot_general(stacked, flat, (((4,), (0,)), ((), ())), preferred_element_type=jnp.float32)
        total = term if total is None else total + term
    return total


def leaky(value):
    return jnp.where(value >= 0, value, 0.3 * value)


def pool_cells(value):
    s, z, x, y, c = value.shape
    return value.reshape(s, z // 2, 2, x // 2, 2, y // 2, 2, c).max(axis=(2, 4, 6))


def wrap_pad(value):
    return jnp.pad(value, ((0, 0), (1, 1), (1, 1), (1, 1), (0, 0)), mode="wrap")


def reference(volume, fine_kernel, fine_bias, deep_kernel, deep_bias):
    def fine_layer(sample):
        conv = conv_block(wrap_pad(sample[None]), fine_kernel) + fine_bias
        return pool_cells(leaky(conv)).astype(jnp.bfloat16)[0]

    pooled = lax.map(fine_layer, volume)

    def deep_layer(sample):
        conv = conv_block(wrap_pad(sample[None]), deep_kernel) + deep_bias
        deep = leaky(conv).astype(jnp.bfloat16)[0]
        return deep.transpose(3, 0, 1, 2).reshape(deep.shape[3], deep.shape[0], deep.shape[1] * deep.shape[2])

    return lax.map(deep_layer, pooled)
```

```python
import jax
import jax.numpy as jnp
import numpy as np
from jax import lax
from jax.experimental import pallas as pl
from jax.experimental.pallas import tpu as pltpu
from jax.sharding import PartitionSpec as P

MIB = 1 << 20
BF16 = jnp.bfloat16
F32 = jnp.float32
VMEM = pl.BlockSpec(memory_space=pltpu.VMEM)
ANY = pl.BlockSpec(memory_space=pl.ANY)


def swap_matrix():
    m = np.zeros((256, 256), np.float32)
    for r in range(16):
        for s in range(16):
            m[r * 16 + s, s * 16 + r] = 1
    return m


def row_matrix():
    m = np.zeros((256, 256), np.float32)
    for o in range(16):
        for big in range(4):
            for z in range(4):
                m[(o * 4 + big) * 4 + z, (z * 4 + big) * 16 + o] = 1
    return m


def lane_matrix():
    src = np.arange(1024).reshape(8, 8, 4, 4)
    dst = src.transpose(1, 2, 0, 3).reshape(-1)
    m = np.zeros((1024, 1024), np.float32)
    m[dst, np.arange(1024)] = 1
    return m


def params(mib):
    return pltpu.CompilerParams(vmem_limit_bytes=mib * MIB)


def cost(flops, moved):
    return pl.CostEstimate(flops=flops, bytes_accessed=moved, transcendentals=0)


def leaky(value):
    return jnp.where(value >= 0, value, 0.3 * value)


def dot(a, b):
    return jnp.dot(a, b, preferred_element_type=F32)


def shift(value, axis, step):
    n = lax.axis_size(axis)
    return lax.ppermute(value, axis, [(i, (i + step) % n) for i in range(n)])


def swap_pairs(value, axis, odd):
    n = lax.axis_size(axis)
    pairs = []
    for i in range(n):
        up = (i % 2 == 1) if odd else (i % 2 == 0)
        pairs.append((i, (i + 1) % n if up else (i - 1) % n))
    return lax.ppermute(value, axis, pairs)


def turn(p, slab, put):
    for j in (0, 2):
        halves = [slab[:, (j + k) * 16 : (j + k) * 16 + 16].reshape(256, 128) for k in (0, 1)]
        turned = dot(p, jnp.concatenate(halves, -1)).astype(BF16)
        for k in (0, 1):
            put(2 * (j + k), turned[:, k * 128 : (k + 1) * 128].reshape(2, 128, 128))


def turn_faces_kernel(vol, p_ref, lo, hi, buf, sem):
    copies = [pltpu.make_async_copy(vol.at[:, z], buf.at[i], sem.at[i]) for i, z in ((0, 0), (1, 7))]
    for c in copies:
        c.start()
    for i, out in ((0, lo), (1, hi)):
        copies[i].wait()

        def put(x, value, out=out):
            out[x : x + 2] = value

        turn(p_ref[...], buf[i], put)


def turn_faces(vol, p):
    return pl.pallas_call(
        turn_faces_kernel,
        out_shape=[jax.ShapeDtypeStruct((8, 128, 128), BF16)] * 2,
        in_specs=[ANY, VMEM],
        out_specs=[VMEM, VMEM],
        scratch_shapes=[pltpu.VMEM((2, 16, 64, 128), BF16), pltpu.SemaphoreType.DMA((2,))],
        compiler_params=params(8),
        cost_estimate=cost(2 * 2048 * 256 * 256, 1 << 20),
        name="turn_faces",
    )(vol, p)


def turn_rest_kernel(vol, p_ref, out):
    def put(x, value):
        out[0, x : x + 2] = value

    turn(p_ref[...], vol[:, 0], put)


def turn_rest(vol, p):
    return pl.pallas_call(
        turn_rest_kernel,
        grid=(6,),
        out_shape=jax.ShapeDtypeStruct((6, 8, 128, 128), BF16),
        in_specs=[
            pl.BlockSpec((16, 1, 64, 128), lambda i: (0, i + 1, 0, 0)),
            pl.BlockSpec((256, 256), lambda i: (0, 0)),
        ],
        out_specs=pl.BlockSpec((1, 8, 128, 128), lambda i: (i, 0, 0, 0)),
        compiler_params=params(8),
        cost_estimate=cost(2 * 6144 * 256 * 256, 3 << 20),
        name="turn_rest",
    )(vol, p)


def fine_kernel_body(t1, tlo, thi, zlo, zhi, xlo, xhi, w, mid, eacc, epool, b, xs, sem):
    copies = [
        pltpu.make_async_copy(src, dst, sem.at[i])
        for i, (src, dst) in enumerate(
            (
                (t1, xs.at[2:8, 1:9]),
                (tlo, xs.at[1, 1:9]),
                (thi, xs.at[8, 1:9]),
                (zlo, xs.at[0, 1:9]),
                (zhi, xs.at[9, 1:9]),
                (xlo, xs.at[:, 0]),
                (xhi, xs.at[:, 9]),
            )
        )
    ]
    for c in copies:
        c.start()
    for c in copies:
        c.wait()

    def step(i, carry):
        taps = [
            xs[pl.ds(2 * i + dz, 2), dx : dx + 8, dy * 16 : dy * 16 + 96].reshape(1536, 128)
            for dz in range(3)
            for dx in range(3)
            for dy in range(3)
        ]
        acc = dot(jnp.concatenate(taps, -1), w[...])
        acc = acc.reshape(2, 4, 2, 6, 16, 256).max(axis=(0, 2))
        epool[0, pl.ds(i, 1)] = acc[None, :, 0]
        epool[1, pl.ds(i, 1)] = acc[None, :, 5]
        inner = acc[:, 1:5].reshape(4, 2, 2, 16, 256).max(axis=2)
        mid[pl.ds(i, 1)] = leaky(inner + b[...])[None].astype(BF16)
        return carry

    lax.fori_loop(0, 4, step, 0)
    for e in (0, 1):
        taps = [
            xs[dz : dz + 8, dx : dx + 8, (6 * e + k) * 16 : (6 * e + k + 1) * 16].reshape(1024, 128)
            for dz in range(3)
            for dx in range(3)
            for k in (0, 1)
        ]
        rows = [w[t * 384 + 128 * (1 - e) : t * 384 + 128 * (1 - e) + 256] for t in range(9)]
        acc = dot(jnp.concatenate(taps, -1), jnp.concatenate(rows, 0))
        eacc[e] = acc.reshape(8, 8, 16, 256)


def fine_first(t1, tlo, thi, zlo, zhi, xlo, xhi, w, b):
    def body(t1, tlo, thi, zlo, zhi, xlo, xhi, w, b, mid, eacc, epool, xs, sem):
        fine_kernel_body(t1, tlo, thi, zlo, zhi, xlo, xhi, w, mid, eacc, epool, b, xs, sem)

    return pl.pallas_call(
        body,
        out_shape=[
            jax.ShapeDtypeStruct((4, 4, 2, 16, 256), BF16),
            jax.ShapeDtypeStruct((2, 8, 8, 16, 256), F32),
            jax.ShapeDtypeStruct((2, 4, 4, 16, 256), F32),
        ],
        in_specs=[ANY] * 7 + [VMEM, VMEM],
        out_specs=[VMEM] * 3,
        scratch_shapes=[pltpu.VMEM((10, 10, 128, 128), BF16), pltpu.SemaphoreType.DMA((7,))],
        compiler_params=params(48),
        cost_estimate=cost(2 * 8192 * 3456 * 256, 8 << 20),
        name="fine_first",
    )(t1, tlo, thi, zlo, zhi, xlo, xhi, w, b)


def fine_last_kernel(odd, got_a, got_b, w, b, mid, eacc, epool, pooled, f0, f3, ys, sem):
    flag = odd[0]

    def copies(first, second):
        return [
            pltpu.make_async_copy(first, ys.at[0], sem.at[0]),
            pltpu.make_async_copy(second, ys.at[1], sem.at[1]),
        ]

    @pl.when(flag == 1)
    def _():
        for c in copies(got_b, got_a):
            c.start()

    @pl.when(flag == 0)
    def _():
        for c in copies(got_a, got_b):
            c.start()

    for c in copies(got_a, got_b):
        c.wait()
    pooled[:, :, 1:3] = mid[...]
    for e in (0, 1):
        taps = [
            ys[e, dz : dz + 8, dx : dx + 8].reshape(1024, 128) for dz in range(3) for dx in range(3)
        ]
        acc = dot(jnp.concatenate(taps, -1), w[:, 2 * e].reshape(1152, 256))
        acc = acc.reshape(8, 8, 16, 256) + eacc[e]
        acc = acc.reshape(4, 2, 4, 2, 16, 256).max(axis=(1, 3))
        acc = jnp.maximum(acc, epool[e])
        pooled[:, :, 3 * e] = leaky(acc + b[...]).astype(BF16)
    f0[...] = pooled[0]
    f3[...] = pooled[3]


def fine_last(odd, got_a, got_b, w, b, mid, eacc, epool):
    return pl.pallas_call(
        fine_last_kernel,
        out_shape=[
            jax.ShapeDtypeStruct((4, 4, 4, 16, 256), BF16),
            jax.ShapeDtypeStruct((4, 4, 16, 256), BF16),
            jax.ShapeDtypeStruct((4, 4, 16, 256), BF16),
        ],
        in_specs=[pl.BlockSpec(memory_space=pltpu.SMEM), ANY, ANY] + [VMEM] * 5,
        out_specs=[VMEM] * 3,
        scratch_shapes=[pltpu.VMEM((2, 10, 10, 16, 128), BF16), pltpu.SemaphoreType.DMA((2,))],
        compiler_params=params(32),
        cost_estimate=cost(2 * 2048 * 1152 * 256, 6 << 20),
        name="fine_last",
    )(odd, got_a, got_b, w, b, mid, eacc, epool)


def deep_first_kernel(own, zlo, zhi, xlo, xhi, w, out, xs, sem):
    copies = [
        pltpu.make_async_copy(src, dst, sem.at[i])
        for i, (src, dst) in enumerate(
            (
                (own, xs.at[1:5, 1:5]),
                (zlo, xs.at[0, 1:5]),
                (zhi, xs.at[5, 1:5]),
                (xlo, xs.at[:, 0]),
                (xhi, xs.at[:, 5]),
            )
        )
    ]
    for c in copies:
        c.start()
    for c in copies:
        c.wait()
    inner = None
    for first, size, dys in ((1, 2, (0, 1, 2)), (0, 1, (1, 2)), (3, 1, (0, 1))):
        taps = [
            xs[dz : dz + 4, dx : dx + 4, first + dy - 1 : first + dy - 1 + size].reshape(16 * size * 16, 256)
            for dz in range(3)
            for dx in range(3)
            for dy in dys
        ]
        rows = [w[t * 3 + dy] for t in range(9) for dy in dys]
        acc = dot(jnp.concatenate(taps, -1), jnp.concatenate(rows, 0))
        out[:, :, first : first + size] = acc.reshape(4, 4, size, 16, 256)


def deep_first(own, zlo, zhi, xlo, xhi, w):
    return pl.pallas_call(
        deep_first_kernel,
        out_shape=jax.ShapeDtypeStruct((4, 4, 4, 16, 256), F32),
        in_specs=[ANY] * 5 + [VMEM],
        out_specs=VMEM,
        scratch_shapes=[pltpu.VMEM((6, 6, 4, 16, 256), BF16), pltpu.SemaphoreType.DMA((5,))],
        compiler_params=params(48),
        cost_estimate=cost(2 * 1024 * 6912 * 256, 6 << 20),
        name="deep_first",
    )(own, zlo, zhi, xlo, xhi, w)


def deep_last_kernel(odd, got_a, got_b, w, b, acc_in, p_ref, out, ys, full, sem):
    flag = odd[0]

    def copies(first, second):
        return [
            pltpu.make_async_copy(first, ys.at[0], sem.at[0]),
            pltpu.make_async_copy(second, ys.at[1], sem.at[1]),
        ]

    @pl.when(flag == 1)
    def _():
        for c in copies(got_b, got_a):
            c.start()

    @pl.when(flag == 0)
    def _():
        for c in copies(got_a, got_b):
            c.start()

    for c in copies(got_a, got_b):
        c.wait()
    full[:, :, 1:3] = leaky(acc_in[:, :, 1:3] + b[...]).astype(BF16)
    for e in (0, 1):
        taps = [
            ys[e, dz : dz + 4, dx : dx + 4].reshape(256, 256) for dz in range(3) for dx in range(3)
        ]
        acc = dot(jnp.concatenate(taps, -1), w[:, 2 * e].reshape(2304, 256))
        acc = acc.reshape(4, 4, 16, 256) + acc_in[:, :, 3 * e]
        full[:, :, 3 * e] = leaky(acc + b[...]).astype(BF16)
    planes = [dot(p_ref[...], full[z].reshape(256, 256)).reshape(16, 16, 256) for z in range(4)]
    lane = lax.broadcasted_iota(jnp.int32, (128, 128), 1)
    for pair in range(8):
        rows = jnp.concatenate(
            [planes[z][2 * pair + k] for k in (0, 1) for z in range(4)], 0
        )
        turned = rows.T.reshape(8, 2, 16, 128)
        low = turned[:, 0].reshape(128, 128)
        high = turned[:, 1].reshape(128, 128)
        first = jnp.where(lane < 64, low, pltpu.roll(high, 64, 1))
        second = jnp.where(lane < 64, pltpu.roll(low, 64, 1), high)
        out[2 * pair] = first.astype(BF16).reshape(8, 16, 128)
        out[2 * pair + 1] = second.astype(BF16).reshape(8, 16, 128)


def deep_last(odd, got_a, got_b, w, b, acc, p):
    return pl.pallas_call(
        deep_last_kernel,
        out_shape=jax.ShapeDtypeStruct((16, 8, 16, 128), BF16),
        in_specs=[pl.BlockSpec(memory_space=pltpu.SMEM), ANY, ANY] + [VMEM] * 4,
        out_specs=VMEM,
        scratch_shapes=[
            pltpu.VMEM((2, 6, 6, 16, 256), BF16),
            pltpu.VMEM((4, 4, 4, 16, 256), BF16),
            pltpu.SemaphoreType.DMA((2,)),
        ],
        compiler_params=params(32),
        cost_estimate=cost(2 * 512 * 2304 * 256, 6 << 20),
        name="deep_last",
    )(odd, got_a, got_b, w, b, acc, p)


def arrange_kernel(got, lanes, rows, out, first, second):
    for s in range(4):
        for p in range(4):
            for c in range(8):
                first[(p * 4 + s) * 16 : (p * 4 + s) * 16 + 16, c * 128 : (c + 1) * 128] = got[(s * 4 + p) * 8 + c]
    spread = dot(first[...], lanes[...]).astype(BF16)
    for p in range(4):
        for z in range(4):
            for h in range(2):
                second[z * 64 : (z + 1) * 64, (p * 2 + h) * 128 : (p * 2 + h + 1) * 128] = spread[
                    p * 64 : (p + 1) * 64, (h * 4 + z) * 128 : (h * 4 + z + 1) * 128
                ]
    last = dot(rows[...], second[...]).astype(BF16)
    for p in range(4):
        for h in range(2):
            out[0, h * 16 : (h + 1) * 16, :, p * 128 : (p + 1) * 128] = last[
                :, (p * 2 + h) * 128 : (p * 2 + h + 1) * 128
            ].reshape(16, 16, 128)


def arrange(got, lanes, rows):
    return pl.pallas_call(
        arrange_kernel,
        out_shape=jax.ShapeDtypeStruct((1, 32, 16, 512), BF16),
        in_specs=[VMEM] * 3,
        out_specs=VMEM,
        scratch_shapes=[pltpu.VMEM((256, 1024), BF16), pltpu.VMEM((256, 1024), BF16)],
        compiler_params=params(24),
        cost_estimate=cost(2 * 256 * 1280 * 1024, 3 << 20),
        name="arrange",
    )(got, lanes, rows)


def on_device(volume, fine_kernel, fine_bias, deep_kernel, deep_bias):
    p = jnp.asarray(swap_matrix(), BF16)
    odd = lax.axis_index("chan") % 2
    is_odd = odd == 1
    flag = odd.astype(jnp.int32).reshape(1)
    vol = volume.reshape(16, 8, 64, 128)

    def y_exchange(head, tail):
        got_a = swap_pairs(jnp.where(is_odd, tail, head), "chan", True)
        got_b = swap_pairs(jnp.where(is_odd, head, tail), "chan", False)
        return got_a, got_b

    tlo, thi = turn_faces(vol, p)
    zlo, zhi = shift(thi, "sample", 1), shift(tlo, "sample", -1)
    t1 = turn_rest(vol, p)

    def x_face(x):
        return jnp.concatenate([zlo[None, x], tlo[None, x], t1[:, x], thi[None, x], zhi[None, x]], 0)

    xlo, xhi = shift(x_face(7), "space", 1), shift(x_face(0), "space", -1)

    def y_face(y):
        own = jnp.concatenate([zlo[None], tlo[None], t1, thi[None], zhi[None]], 0)
        return jnp.concatenate([xlo[:, None], own, xhi[:, None]], 1)[:, :, y * 16 : y * 16 + 16]

    got_a, got_b = y_exchange(y_face(0), y_face(7))
    w = fine_kernel.reshape(3456, 256)
    b = fine_bias.reshape(1, 256)
    mid, eacc, epool = fine_first(t1, tlo, thi, zlo, zhi, xlo, xhi, w, b)
    pooled, f0, f3 = fine_last(
        flag, got_a, got_b, fine_kernel.reshape(9, 3, 128, 256), b, mid, eacc, epool
    )

    zlo, zhi = shift(f3, "sample", 1), shift(f0, "sample", -1)

    def deep_x_face(x):
        return jnp.concatenate([zlo[None, x], pooled[:, x], zhi[None, x]], 0)

    xlo, xhi = shift(deep_x_face(3), "space", 1), shift(deep_x_face(0), "space", -1)

    def deep_y_face(y):
        own = jnp.concatenate([zlo[None, :, y], pooled[:, :, y], zhi[None, :, y]], 0)
        return jnp.concatenate([xlo[:, None, y], own, xhi[:, None, y]], 1)

    got_a, got_b = y_exchange(deep_y_face(0), deep_y_face(3))
    acc = deep_first(pooled, zlo, zhi, xlo, xhi, deep_kernel.reshape(27, 256, 256))
    send = deep_last(
        flag, got_a, got_b, deep_kernel.reshape(9, 3, 256, 256), deep_bias.reshape(1, 256), acc, p
    )
    got = lax.all_to_all(
        send.reshape(128, 16, 128), ("sample", "space", "chan"), split_axis=0, concat_axis=0, tiled=True
    )
    return arrange(got, jnp.asarray(lane_matrix(), BF16), jnp.asarray(row_matrix(), BF16))


def solution(mesh):
    placed = (P(None, "sample", "space", "chan", None), P(), P(), P(), P())
    return jax.shard_map(
        on_device,
        mesh=mesh,
        in_specs=placed,
        out_specs=P(("sample", "space"), "chan", None, None),
        check_vma=False,
    )
```

```python
import jax
import jax.numpy as jnp
import numpy as np
from jax import lax
from jax.experimental import pallas as pl
from jax.experimental.pallas import tpu as pltpu
from jax.sharding import PartitionSpec as P

MIB = 1 << 20
FINE_MIB = 36
BF16 = jnp.bfloat16
F32 = jnp.float32
VMEM = pl.BlockSpec(memory_space=pltpu.VMEM)
ANY = pl.BlockSpec(memory_space=pl.ANY)


def lane_matrix():
    src = np.arange(1024).reshape(8, 8, 4, 4)
    dst = src.transpose(1, 2, 0, 3).reshape(-1)
    m = np.zeros((1024, 1024), np.float32)
    m[dst, np.arange(1024)] = 1
    return m


def pad_matrix():
    m = np.zeros((6, 6, 16, 256), np.float32)
    for i in range(6):
        for j in range(6):
            for big in range(4):
                for p in range(4):
                    z, x = (4 * big + i - 1) % 16, (4 * p + j - 1) % 16
                    m[i, j, big * 4 + p, ((z // 4) * 4 + x // 4) * 16 + (z % 4) * 4 + x % 4] = 1
    return m.reshape(576, 256)


def params(mib):
    return pltpu.CompilerParams(vmem_limit_bytes=mib * MIB)


def cost(flops, moved):
    return pl.CostEstimate(flops=flops, bytes_accessed=moved, transcendentals=0)


def leaky(value):
    return jnp.where(value >= 0, value, 0.3 * value)


def dot(a, b):
    return jnp.dot(a, b, preferred_element_type=F32)


def swap_rows():
    i = lax.broadcasted_iota(jnp.int32, (256, 256), 0)
    j = lax.broadcasted_iota(jnp.int32, (256, 256), 1)
    hit = ((i >> 4) == (j & 15)) & ((i & 15) == (j >> 4))
    return jnp.where(hit, 1.0, 0.0).astype(BF16)


def shift(value, axis, step):
    n = lax.axis_size(axis)
    return lax.ppermute(value, axis, [(i, (i + step) % n) for i in range(n)])


def swap_pairs(value, axis, odd):
    n = lax.axis_size(axis)
    pairs = []
    for i in range(n):
        up = (i % 2 == 1) if odd else (i % 2 == 0)
        pairs.append((i, (i + 1) % n if up else (i - 1) % n))
    return lax.ppermute(value, axis, pairs)


def turn(p, slab, put):
    for j in (0, 2):
        halves = [slab[:, (j + k) * 16 : (j + k) * 16 + 16].reshape(256, 128) for k in (0, 1)]
        turned = dot(p, jnp.concatenate(halves, -1)).astype(BF16)
        for k in (0, 1):
            put(2 * (j + k), turned[:, k * 128 : (k + 1) * 128].reshape(2, 128, 128))


def turn_faces_kernel(vol, lo, hi, buf, sem):
    copies = [pltpu.make_async_copy(vol.at[:, z], buf.at[i], sem.at[i]) for i, z in ((0, 0), (1, 7))]
    for c in copies:
        c.start()
    p = swap_rows()
    for i, out in ((0, lo), (1, hi)):
        copies[i].wait()

        def put(x, value, out=out):
            out[x : x + 2] = value

        turn(p, buf[i], put)


def turn_faces(vol):
    return pl.pallas_call(
        turn_faces_kernel,
        out_shape=[jax.ShapeDtypeStruct((8, 128, 128), BF16)] * 2,
        in_specs=[ANY],
        out_specs=[VMEM, VMEM],
        scratch_shapes=[pltpu.VMEM((2, 16, 64, 128), BF16), pltpu.SemaphoreType.DMA((2,))],
        compiler_params=params(60),
        cost_estimate=cost(2 * 2048 * 256 * 256, 1 << 20),
        name="turn_faces",
    )(vol)


def turn_rest_kernel(vol, out):
    def put(x, value):
        out[0, x : x + 2] = value

    turn(swap_rows(), vol[:, 0], put)


def turn_rest(vol):
    return pl.pallas_call(
        turn_rest_kernel,
        grid=(6,),
        out_shape=jax.ShapeDtypeStruct((6, 8, 128, 128), BF16),
        in_specs=[pl.BlockSpec((16, 1, 64, 128), lambda i: (0, i + 1, 0, 0))],
        out_specs=pl.BlockSpec((1, 8, 128, 128), lambda i: (i, 0, 0, 0)),
        compiler_params=params(8),
        cost_estimate=cost(2 * 6144 * 256 * 256, 3 << 20),
        name="turn_rest",
    )(vol)


def edge_rows(w, e):
    first = 128 * (1 - e)
    return jnp.concatenate([w[t * 384 + first : t * 384 + first + 256] for t in range(9)], 0)


def fine_middle_kernel(own, w, b, mid, eacc, epool):
    def step(i, carry):
        taps = [
            own[pl.ds(4 * i + dz, 4), 1 + dx : 5 + dx, dy * 16 : dy * 16 + 96].reshape(1536, 128)
            for dz in range(3)
            for dx in range(3)
            for dy in range(3)
        ]
        acc = dot(jnp.concatenate(taps, -1), w[...])
        acc = acc.reshape(2, 2, 2, 2, 6, 16, 256).max(axis=(1, 3))
        epool[0, pl.ds(2 * i, 2)] = acc[:, :, 0]
        epool[1, pl.ds(2 * i, 2)] = acc[:, :, 5]
        for y in (0, 1):
            inner = jnp.maximum(acc[:, :, 1 + 2 * y], acc[:, :, 2 + 2 * y])
            mid[y, pl.ds(2 * i, 2)] = leaky(inner + b[...]).astype(BF16)
        return carry

    lax.fori_loop(0, 2, step, 0)
    for e in (0, 1):
        taps = [
            own[dz : dz + 8, 1 + dx : 5 + dx, (6 * e + k) * 16 : (6 * e + k + 1) * 16].reshape(512, 128)
            for dz in range(3)
            for dx in range(3)
            for k in (0, 1)
        ]
        eacc[e] = dot(jnp.concatenate(taps, -1), edge_rows(w, e)).reshape(8, 4, 16, 256)


def fine_middle(own, w, b):
    return pl.pallas_call(
        fine_middle_kernel,
        out_shape=[
            jax.ShapeDtypeStruct((2, 4, 2, 16, 256), BF16),
            jax.ShapeDtypeStruct((2, 8, 4, 16, 256), F32),
            jax.ShapeDtypeStruct((2, 4, 2, 16, 256), F32),
        ],
        in_specs=[VMEM] * 3,
        out_specs=[VMEM] * 3,
        compiler_params=params(FINE_MIB),
        cost_estimate=cost(4096 * 3456 * 256 * 2, 8 << 20),
        name="fine_middle",
    )(own, w, b)


def fine_sides_kernel(own, xlo, xhi, w, b, mid, eacc, epool):
    def planes(side, dx, z, n, rows):
        if side == 0 and dx == 0:
            return jnp.concatenate([xlo[z : z + n, rows][:, None], own[z : z + n, 0:1, rows]], 1)
        if side == 1 and dx == 2:
            return jnp.concatenate([own[z : z + n, 7:8, rows], xhi[z : z + n, rows][:, None]], 1)
        first = dx - 1 if side == 0 else 5 + dx
        return own[z : z + n, first : first + 2, rows]

    for side in (0, 1):
        taps = [
            planes(side, dx, dz, 8, slice(dy * 16, dy * 16 + 96)).reshape(1536, 128)
            for dz in range(3)
            for dx in range(3)
            for dy in range(3)
        ]
        acc = dot(jnp.concatenate(taps, -1), w[...])
        acc = acc.reshape(4, 2, 2, 6, 16, 256).max(axis=(1, 2))
        epool[0, :, side] = acc[:, 0]
        epool[1, :, side] = acc[:, 5]
        for y in (0, 1):
            inner = jnp.maximum(acc[:, 1 + 2 * y], acc[:, 2 + 2 * y])
            mid[y, :, side] = leaky(inner + b[...]).astype(BF16)
    for e in (0, 1):
        taps = [
            jnp.concatenate(
                [
                    planes(side, dx, dz, 8, slice((6 * e + k) * 16, (6 * e + k + 1) * 16)).reshape(256, 128)
                    for side in (0, 1)
                ],
                0,
            )
            for dz in range(3)
            for dx in range(3)
            for k in (0, 1)
        ]
        eacc[e] = dot(jnp.concatenate(taps, -1), edge_rows(w, e)).reshape(2, 8, 2, 16, 256)


def fine_sides(own, xlo, xhi, w, b):
    return pl.pallas_call(
        fine_sides_kernel,
        out_shape=[
            jax.ShapeDtypeStruct((2, 4, 2, 16, 256), BF16),
            jax.ShapeDtypeStruct((2, 2, 8, 2, 16, 256), F32),
            jax.ShapeDtypeStruct((2, 4, 2, 16, 256), F32),
        ],
        in_specs=[VMEM] * 5,
        out_specs=[VMEM] * 3,
        compiler_params=params(FINE_MIB),
        cost_estimate=cost(4096 * 3456 * 256 * 2, 8 << 20),
        name="fine_sides",
    )(own, xlo, xhi, w, b)


def fine_last_kernel(odd, got_a, got_b, w, b, mid_m, eacc_m, epool_m, mid_s, eacc_s, epool_s, out):
    p = swap_rows()

    def emit(y, plane):
        out[:, pl.ds(pl.multiple_of(y * 16, 16), 16)] = (
            dot(p, plane.reshape(256, 256)).astype(BF16).reshape(16, 16, 256)
        )

    for y in (0, 1):
        emit(1 + y, jnp.concatenate([mid_s[y, :, 0:1], mid_m[y], mid_s[y, :, 1:2]], 1))
    for got, e in ((got_a, odd[0]), (got_b, 1 - odd[0])):
        taps = [got[dz : dz + 8, dx : dx + 8].reshape(1024, 128) for dz in range(3) for dx in range(3)]
        acc = dot(jnp.concatenate(taps, -1), w[:, pl.ds(2 * e, 1)].reshape(1152, 256))
        acc = acc.reshape(8, 8, 16, 256)
        one = pl.ds(e, 1)
        inner = (acc[:, 2:6] + eacc_m[one][0]).reshape(4, 2, 2, 2, 16, 256).max(axis=(1, 3))
        inner = jnp.maximum(inner, epool_m[one][0])
        outer = jnp.stack([acc[:, 0:2], acc[:, 6:8]], 0) + eacc_s[one][0]
        outer = outer.reshape(2, 4, 2, 2, 16, 256).max(axis=(2, 3))
        known = epool_s[one][0]
        first = jnp.maximum(outer[0], known[:, 0])[:, None]
        last = jnp.maximum(outer[1], known[:, 1])[:, None]
        plane = jnp.concatenate([first, inner, last], 1)
        emit(3 * e, leaky(plane + b[...]).astype(BF16))


def fine_last(odd, got_a, got_b, w, b, middle, sides):
    return pl.pallas_call(
        fine_last_kernel,
        out_shape=jax.ShapeDtypeStruct((16, 64, 256), BF16),
        in_specs=[pl.BlockSpec(memory_space=pltpu.SMEM)] + [VMEM] * 10,
        out_specs=VMEM,
        compiler_params=params(24),
        cost_estimate=cost(2 * 2048 * 1152 * 256, 6 << 20),
        name="fine_last",
    )(odd, got_a, got_b, w, b, *middle, *sides)


def deep_first_kernel(got, pad, w, out, xs):
    for y in range(4):
        plane = got[:, y * 16 : y * 16 + 16].reshape(256, 256)
        xs[y] = dot(pad[...], plane).astype(BF16).reshape(6, 6, 16, 256)
    for first, size, dys in ((1, 2, (0, 1, 2)), (0, 1, (1, 2)), (3, 1, (0, 1))):
        taps = [
            xs[first + dy - 1 : first + dy - 1 + size, dz : dz + 4, dx : dx + 4].reshape(256 * size, 256)
            for dz in range(3)
            for dx in range(3)
            for dy in dys
        ]
        rows = [w[t, dy] for t in range(9) for dy in dys]
        acc = dot(jnp.concatenate(taps, -1), jnp.concatenate(rows, 0))
        out[first : first + size] = acc.reshape(size, 4, 4, 16, 256)


def deep_first(got, pad, w):
    return pl.pallas_call(
        deep_first_kernel,
        out_shape=jax.ShapeDtypeStruct((4, 4, 4, 16, 256), F32),
        in_specs=[VMEM] * 3,
        out_specs=VMEM,
        scratch_shapes=[pltpu.VMEM((4, 6, 6, 16, 256), BF16)],
        compiler_params=params(40),
        cost_estimate=cost(2 * 1024 * 6912 * 256, 6 << 20),
        name="deep_first",
    )(got, pad, w)


def deep_last_kernel(odd, got_a, got_b, pad, w, b, acc_in, out, ys, full, turned):
    p = swap_rows()
    for y in (1, 2):
        full[:, :, y] = leaky(acc_in[y] + b[...]).astype(BF16)
    for k, (got, e) in enumerate(((got_a, odd[0]), (got_b, 1 - odd[0]))):
        ys[k] = dot(pad[...], got[...].reshape(256, 256)).astype(BF16).reshape(6, 6, 16, 256)
        taps = [ys[k, dz : dz + 4, dx : dx + 4].reshape(256, 256) for dz in range(3) for dx in range(3)]
        acc = dot(jnp.concatenate(taps, -1), w[:, pl.ds(2 * e, 1)].reshape(2304, 256))
        acc = acc.reshape(4, 4, 16, 256) + acc_in[pl.ds(3 * e, 1)][0]
        full[:, :, pl.ds(3 * e, 1)] = leaky(acc + b[...]).astype(BF16)[:, :, None]
    planes = [dot(p, full[z].reshape(256, 256)).reshape(16, 16, 256) for z in range(4)]
    lane = lax.broadcasted_iota(jnp.int32, (128, 128), 1)
    for big in range(4):
        for z in (0, 2):
            rows = [planes[z + k][big * 4 : big * 4 + 4].reshape(64, 256) for k in (0, 1)]
            flipped = jnp.concatenate(rows, 0).T.reshape(8, 2, 16, 128)
            low = flipped[:, 0].reshape(128, 128)
            high = flipped[:, 1].reshape(128, 128)
            first = jnp.where(lane < 64, low, pltpu.roll(high, 64, 1))
            second = jnp.where(lane < 64, pltpu.roll(low, 64, 1), high)
            turned[big * 4 + z] = first.astype(BF16).reshape(8, 16, 128)
            turned[big * 4 + z + 1] = second.astype(BF16).reshape(8, 16, 128)
    for c in (0, 2, 4, 6):
        pair = [turned[:, c + k].reshape(256, 128) for k in (0, 1)]
        moved = dot(p, jnp.concatenate(pair, -1)).astype(BF16)
        for k in (0, 1):
            out[c + k] = moved[:, k * 128 : (k + 1) * 128]


def deep_last(odd, got_a, got_b, pad, w, b, acc):
    return pl.pallas_call(
        deep_last_kernel,
        out_shape=jax.ShapeDtypeStruct((8, 256, 128), BF16),
        in_specs=[pl.BlockSpec(memory_space=pltpu.SMEM)] + [VMEM] * 6,
        out_specs=VMEM,
        scratch_shapes=[
            pltpu.VMEM((2, 6, 6, 16, 256), BF16),
            pltpu.VMEM((4, 4, 4, 16, 256), BF16),
            pltpu.VMEM((16, 8, 16, 128), BF16),
        ],
        compiler_params=params(24),
        cost_estimate=cost(2 * 512 * 2304 * 256, 6 << 20),
        name="deep_last",
    )(odd, got_a, got_b, pad, w, b, acc)


def arrange_kernel(got, lanes, out):
    spread = dot(jnp.concatenate([got[c] for c in range(8)], -1), lanes[...]).astype(BF16)
    for h in range(2):
        for p in range(4):
            first = (h * 4 + p) * 128
            out[0, h * 16 : (h + 1) * 16, :, p * 128 : (p + 1) * 128] = spread[:, first : first + 128].reshape(
                16, 16, 128
            )


def arrange(got, lanes):
    return pl.pallas_call(
        arrange_kernel,
        out_shape=jax.ShapeDtypeStruct((1, 32, 16, 512), BF16),
        in_specs=[VMEM] * 2,
        out_specs=VMEM,
        compiler_params=params(16),
        cost_estimate=cost(2 * 256 * 1024 * 1024, 3 << 20),
        name="arrange",
    )(got, lanes)


def on_device(volume, fine_kernel, fine_bias, deep_kernel, deep_bias):
    odd = lax.axis_index("chan") % 2
    is_odd = odd == 1
    flag = odd.astype(jnp.int32).reshape(1)
    vol = volume.reshape(16, 8, 64, 128)

    def y_exchange(head, tail):
        got_a = swap_pairs(jnp.where(is_odd, tail, head), "chan", True)
        got_b = swap_pairs(jnp.where(is_odd, head, tail), "chan", False)
        return got_a, got_b

    tlo, thi = turn_faces(vol)
    zlo, zhi = shift(thi, "sample", 1), shift(tlo, "sample", -1)
    t1 = turn_rest(vol)
    own = jnp.concatenate([zlo[None], tlo[None], t1, thi[None], zhi[None]], 0)
    xlo, xhi = shift(own[:, 7], "space", 1), shift(own[:, 0], "space", -1)
    w = fine_kernel.reshape(3456, 256)
    b = fine_bias.reshape(1, 256)
    middle = fine_middle(own, w, b)

    def y_face(y):
        return jnp.concatenate([xlo[:, None], own, xhi[:, None]], 1)[:, :, y * 16 : y * 16 + 16]

    got_a, got_b = y_exchange(y_face(0), y_face(7))
    sides = fine_sides(own, xlo, xhi, w, b)
    send = fine_last(flag, got_a, got_b, fine_kernel.reshape(9, 3, 128, 256), b, middle, sides)
    got = lax.all_to_all(send, ("sample", "space"), split_axis=0, concat_axis=0, tiled=True)

    got_a, got_b = y_exchange(got[:, 0:16], got[:, 48:64])
    pad = jnp.asarray(pad_matrix(), BF16)
    dw = deep_kernel.reshape(9, 3, 256, 256)
    acc = deep_first(got, pad, dw)
    send = deep_last(flag, got_a, got_b, pad, dw, deep_bias.reshape(1, 256), acc)
    got = lax.all_to_all(send, "chan", split_axis=0, concat_axis=0, tiled=True)
    return arrange(got, jnp.asarray(lane_matrix(), BF16))


def solution(mesh):
    placed = (P(None, "sample", "space", "chan", None), P(), P(), P(), P())
    return jax.shard_map(
        on_device,
        mesh=mesh,
        in_specs=placed,
        out_specs=P(("sample", "space"), "chan", None, None),
        check_vma=False,
    )
```

```python
import jax
import jax.numpy as jnp
import numpy as np
from jax import lax
from jax.experimental import pallas as pl
from jax.experimental.pallas import tpu as pltpu
from jax.sharding import PartitionSpec as P

MIB = 1 << 20
FINE_MIB = 36
BF16 = jnp.bfloat16
F32 = jnp.float32
VMEM = pl.BlockSpec(memory_space=pltpu.VMEM)
ANY = pl.BlockSpec(memory_space=pl.ANY)


def lane_matrix():
    src = np.arange(1024).reshape(8, 8, 4, 4)
    dst = src.transpose(1, 2, 0, 3).reshape(-1)
    m = np.zeros((1024, 1024), np.float32)
    m[dst, np.arange(1024)] = 1
    return m


def pad_matrix():
    m = np.zeros((6, 6, 16, 256), np.float32)
    for i in range(6):
        for j in range(6):
            for big in range(4):
                for p in range(4):
                    z, x = (4 * big + i - 1) % 16, (4 * p + j - 1) % 16
                    m[i, j, big * 4 + p, ((z // 4) * 4 + x // 4) * 16 + (z % 4) * 4 + x % 4] = 1
    return m.reshape(576, 256)


def params(mib):
    return pltpu.CompilerParams(vmem_limit_bytes=mib * MIB)


def cost(flops, moved):
    return pl.CostEstimate(flops=flops, bytes_accessed=moved, transcendentals=0)


def leaky(value):
    return jnp.where(value >= 0, value, 0.3 * value)


def dot(a, b):
    return jnp.dot(a, b, preferred_element_type=F32)


def swap_rows():
    i = lax.broadcasted_iota(jnp.int32, (256, 256), 0)
    j = lax.broadcasted_iota(jnp.int32, (256, 256), 1)
    hit = ((i >> 4) == (j & 15)) & ((i & 15) == (j >> 4))
    return jnp.where(hit, 1.0, 0.0).astype(BF16)


def shift(value, axis, step):
    n = lax.axis_size(axis)
    return lax.ppermute(value, axis, [(i, (i + step) % n) for i in range(n)])


def swap_pairs(value, axis, odd):
    n = lax.axis_size(axis)
    pairs = []
    for i in range(n):
        up = (i % 2 == 1) if odd else (i % 2 == 0)
        pairs.append((i, (i + 1) % n if up else (i - 1) % n))
    return lax.ppermute(value, axis, pairs)


def turn(p, slab, put):
    for j in (0, 2):
        halves = [slab[:, (j + k) * 16 : (j + k) * 16 + 16].reshape(256, 128) for k in (0, 1)]
        turned = dot(p, jnp.concatenate(halves, -1)).astype(BF16)
        for k in (0, 1):
            put(2 * (j + k), turned[:, k * 128 : (k + 1) * 128].reshape(2, 128, 128))


def turn_faces_kernel(vol, lo, hi, buf, sem):
    copies = [pltpu.make_async_copy(vol.at[:, z], buf.at[i], sem.at[i]) for i, z in ((0, 0), (1, 7))]
    for c in copies:
        c.start()
    p = swap_rows()
    for i, out in ((0, lo), (1, hi)):
        copies[i].wait()

        def put(x, value, out=out):
            out[x : x + 2] = value

        turn(p, buf[i], put)


def turn_faces(vol):
    return pl.pallas_call(
        turn_faces_kernel,
        out_shape=[jax.ShapeDtypeStruct((8, 128, 128), BF16)] * 2,
        in_specs=[ANY],
        out_specs=[VMEM, VMEM],
        scratch_shapes=[pltpu.VMEM((2, 16, 64, 128), BF16), pltpu.SemaphoreType.DMA((2,))],
        compiler_params=params(60),
        cost_estimate=cost(2 * 2048 * 256 * 256, 1 << 20),
        name="turn_faces",
    )(vol)


def turn_rest_kernel(vol, out):
    def put(x, value):
        out[0, x : x + 2] = value

    turn(swap_rows(), vol[:, 0], put)


def turn_rest(vol):
    return pl.pallas_call(
        turn_rest_kernel,
        grid=(6,),
        out_shape=jax.ShapeDtypeStruct((6, 8, 128, 128), BF16),
        in_specs=[pl.BlockSpec((16, 1, 64, 128), lambda i: (0, i + 1, 0, 0))],
        out_specs=pl.BlockSpec((1, 8, 128, 128), lambda i: (i, 0, 0, 0)),
        compiler_params=params(8),
        cost_estimate=cost(2 * 6144 * 256 * 256, 3 << 20),
        name="turn_rest",
    )(vol)


def edge_rows(w, e):
    first = 128 * (1 - e)
    return jnp.concatenate([w[t * 384 + first : t * 384 + first + 256] for t in range(9)], 0)


def fine_middle_kernel(own, w, b, mid, eacc, epool):
    def step(i, carry):
        taps = [
            own[pl.ds(4 * i + dz, 4), 1 + dx : 5 + dx, dy * 16 : dy * 16 + 96].reshape(1536, 128)
            for dz in range(3)
            for dx in range(3)
            for dy in range(3)
        ]
        acc = dot(jnp.concatenate(taps, -1), w[...])
        acc = acc.reshape(2, 2, 2, 2, 6, 16, 256).max(axis=(1, 3))
        epool[0, pl.ds(2 * i, 2)] = acc[:, :, 0]
        epool[1, pl.ds(2 * i, 2)] = acc[:, :, 5]
        for y in (0, 1):
            inner = jnp.maximum(acc[:, :, 1 + 2 * y], acc[:, :, 2 + 2 * y])
            mid[y, pl.ds(2 * i, 2)] = leaky(inner + b[...]).astype(BF16)
        return carry

    lax.fori_loop(0, 2, step, 0)
    for e in (0, 1):
        taps = [
            own[dz : dz + 8, 1 + dx : 5 + dx, (6 * e + k) * 16 : (6 * e + k + 1) * 16].reshape(512, 128)
            for dz in range(3)
            for dx in range(3)
            for k in (0, 1)
        ]
        eacc[e] = dot(jnp.concatenate(taps, -1), edge_rows(w, e)).reshape(8, 4, 16, 256)


def fine_middle(own, w, b):
    return pl.pallas_call(
        fine_middle_kernel,
        out_shape=[
            jax.ShapeDtypeStruct((2, 4, 2, 16, 256), BF16),
            jax.ShapeDtypeStruct((2, 8, 4, 16, 256), F32),
            jax.ShapeDtypeStruct((2, 4, 2, 16, 256), F32),
        ],
        in_specs=[VMEM] * 3,
        out_specs=[VMEM] * 3,
        compiler_params=params(FINE_MIB),
        cost_estimate=cost(4096 * 3456 * 256 * 2, 8 << 20),
        name="fine_middle",
    )(own, w, b)


def fine_sides_kernel(own, xlo, xhi, w, b, mid, eacc, epool):
    def planes(side, dx, z, n, rows):
        if side == 0 and dx == 0:
            return jnp.concatenate([xlo[z : z + n, rows][:, None], own[z : z + n, 0:1, rows]], 1)
        if side == 1 and dx == 2:
            return jnp.concatenate([own[z : z + n, 7:8, rows], xhi[z : z + n, rows][:, None]], 1)
        first = dx - 1 if side == 0 else 5 + dx
        return own[z : z + n, first : first + 2, rows]

    for side in (0, 1):
        taps = [
            planes(side, dx, dz, 8, slice(dy * 16, dy * 16 + 96)).reshape(1536, 128)
            for dz in range(3)
            for dx in range(3)
            for dy in range(3)
        ]
        acc = dot(jnp.concatenate(taps, -1), w[...])
        acc = acc.reshape(4, 2, 2, 6, 16, 256).max(axis=(1, 2))
        epool[0, :, side] = acc[:, 0]
        epool[1, :, side] = acc[:, 5]
        for y in (0, 1):
            inner = jnp.maximum(acc[:, 1 + 2 * y], acc[:, 2 + 2 * y])
            mid[y, :, side] = leaky(inner + b[...]).astype(BF16)
    for e in (0, 1):
        taps = [
            jnp.concatenate(
                [
                    planes(side, dx, dz, 8, slice((6 * e + k) * 16, (6 * e + k + 1) * 16)).reshape(256, 128)
                    for side in (0, 1)
                ],
                0,
            )
            for dz in range(3)
            for dx in range(3)
            for k in (0, 1)
        ]
        eacc[e] = dot(jnp.concatenate(taps, -1), edge_rows(w, e)).reshape(2, 8, 2, 16, 256)


def fine_sides(own, xlo, xhi, w, b):
    return pl.pallas_call(
        fine_sides_kernel,
        out_shape=[
            jax.ShapeDtypeStruct((2, 4, 2, 16, 256), BF16),
            jax.ShapeDtypeStruct((2, 2, 8, 2, 16, 256), F32),
            jax.ShapeDtypeStruct((2, 4, 2, 16, 256), F32),
        ],
        in_specs=[VMEM] * 5,
        out_specs=[VMEM] * 3,
        compiler_params=params(FINE_MIB),
        cost_estimate=cost(4096 * 3456 * 256 * 2, 8 << 20),
        name="fine_sides",
    )(own, xlo, xhi, w, b)


def fine_last_kernel(odd, got_a, got_b, rim_a, rim_b, w, b, mid_m, eacc_m, epool_m, mid_s, eacc_s, epool_s, out, ys):
    p = swap_rows()

    def emit(y, plane):
        out[:, pl.ds(pl.multiple_of(y * 16, 16), 16)] = (
            dot(p, plane.reshape(256, 256)).astype(BF16).reshape(16, 16, 256)
        )

    for y in (0, 1):
        emit(1 + y, jnp.concatenate([mid_s[y, :, 0:1], mid_m[y], mid_s[y, :, 1:2]], 1))
    for k, (got, rim, e) in enumerate(((got_a, rim_a, odd[0]), (got_b, rim_b, 1 - odd[0]))):
        ys[k, 1:9, 1:9] = got[...]
        ys[k, 0] = rim[0:10]
        ys[k, 9] = rim[10:20]
        ys[k, 1:9, 0] = rim[20:28]
        ys[k, 1:9, 9] = rim[28:36]
        taps = [ys[k, dz : dz + 8, dx : dx + 8].reshape(1024, 128) for dz in range(3) for dx in range(3)]
        acc = dot(jnp.concatenate(taps, -1), w[:, pl.ds(2 * e, 1)].reshape(1152, 256))
        acc = acc.reshape(8, 8, 16, 256)
        one = pl.ds(e, 1)
        inner = (acc[:, 2:6] + eacc_m[one][0]).reshape(4, 2, 2, 2, 16, 256).max(axis=(1, 3))
        inner = jnp.maximum(inner, epool_m[one][0])
        outer = jnp.stack([acc[:, 0:2], acc[:, 6:8]], 0) + eacc_s[one][0]
        outer = outer.reshape(2, 4, 2, 2, 16, 256).max(axis=(2, 3))
        known = epool_s[one][0]
        first = jnp.maximum(outer[0], known[:, 0])[:, None]
        last = jnp.maximum(outer[1], known[:, 1])[:, None]
        plane = jnp.concatenate([first, inner, last], 1)
        emit(3 * e, leaky(plane + b[...]).astype(BF16))


def fine_last(odd, faces, rims, w, b, middle, sides):
    return pl.pallas_call(
        fine_last_kernel,
        out_shape=jax.ShapeDtypeStruct((16, 64, 256), BF16),
        in_specs=[pl.BlockSpec(memory_space=pltpu.SMEM)] + [VMEM] * 12,
        out_specs=VMEM,
        scratch_shapes=[pltpu.VMEM((2, 10, 10, 16, 128), BF16)],
        compiler_params=params(24),
        cost_estimate=cost(2 * 2048 * 1152 * 256, 6 << 20),
        name="fine_last",
    )(odd, *faces, *rims, w, b, *middle, *sides)


def deep_first_kernel(got, pad, w, out, xs):
    for y in range(4):
        plane = got[:, y * 16 : y * 16 + 16].reshape(256, 256)
        xs[y] = dot(pad[...], plane).astype(BF16).reshape(6, 6, 16, 256)
    for first, size, dys in ((1, 2, (0, 1, 2)), (0, 1, (1, 2)), (3, 1, (0, 1))):
        taps = [
            xs[first + dy - 1 : first + dy - 1 + size, dz : dz + 4, dx : dx + 4].reshape(256 * size, 256)
            for dz in range(3)
            for dx in range(3)
            for dy in dys
        ]
        rows = [w[t, dy] for t in range(9) for dy in dys]
        acc = dot(jnp.concatenate(taps, -1), jnp.concatenate(rows, 0))
        out[first : first + size] = acc.reshape(size, 4, 4, 16, 256)


def deep_first(got, pad, w):
    return pl.pallas_call(
        deep_first_kernel,
        out_shape=jax.ShapeDtypeStruct((4, 4, 4, 16, 256), F32),
        in_specs=[VMEM] * 3,
        out_specs=VMEM,
        scratch_shapes=[pltpu.VMEM((4, 6, 6, 16, 256), BF16)],
        compiler_params=params(40),
        cost_estimate=cost(2 * 1024 * 6912 * 256, 6 << 20),
        name="deep_first",
    )(got, pad, w)


def deep_last_kernel(odd, got_a, got_b, pad, w, b, acc_in, out, ys, full, turned):
    p = swap_rows()
    for y in (1, 2):
        full[:, :, y] = leaky(acc_in[y] + b[...]).astype(BF16)
    for k, (got, e) in enumerate(((got_a, odd[0]), (got_b, 1 - odd[0]))):
        ys[k] = dot(pad[...], got[...].reshape(256, 256)).astype(BF16).reshape(6, 6, 16, 256)
        taps = [ys[k, dz : dz + 4, dx : dx + 4].reshape(256, 256) for dz in range(3) for dx in range(3)]
        acc = dot(jnp.concatenate(taps, -1), w[:, pl.ds(2 * e, 1)].reshape(2304, 256))
        acc = acc.reshape(4, 4, 16, 256) + acc_in[pl.ds(3 * e, 1)][0]
        full[:, :, pl.ds(3 * e, 1)] = leaky(acc + b[...]).astype(BF16)[:, :, None]
    planes = [dot(p, full[z].reshape(256, 256)).reshape(16, 16, 256) for z in range(4)]
    lane = lax.broadcasted_iota(jnp.int32, (128, 128), 1)
    for big in range(4):
        for z in (0, 2):
            rows = [planes[z + k][big * 4 : big * 4 + 4].reshape(64, 256) for k in (0, 1)]
            flipped = jnp.concatenate(rows, 0).T.reshape(8, 2, 16, 128)
            low = flipped[:, 0].reshape(128, 128)
            high = flipped[:, 1].reshape(128, 128)
            first = jnp.where(lane < 64, low, pltpu.roll(high, 64, 1))
            second = jnp.where(lane < 64, pltpu.roll(low, 64, 1), high)
            turned[big * 4 + z] = first.astype(BF16).reshape(8, 16, 128)
            turned[big * 4 + z + 1] = second.astype(BF16).reshape(8, 16, 128)
    for c in (0, 2, 4, 6):
        pair = [turned[:, c + k].reshape(256, 128) for k in (0, 1)]
        moved = dot(p, jnp.concatenate(pair, -1)).astype(BF16)
        for k in (0, 1):
            out[c + k] = moved[:, k * 128 : (k + 1) * 128]


def deep_last(odd, got_a, got_b, pad, w, b, acc):
    return pl.pallas_call(
        deep_last_kernel,
        out_shape=jax.ShapeDtypeStruct((8, 256, 128), BF16),
        in_specs=[pl.BlockSpec(memory_space=pltpu.SMEM)] + [VMEM] * 6,
        out_specs=VMEM,
        scratch_shapes=[
            pltpu.VMEM((2, 6, 6, 16, 256), BF16),
            pltpu.VMEM((4, 4, 4, 16, 256), BF16),
            pltpu.VMEM((16, 8, 16, 128), BF16),
        ],
        compiler_params=params(24),
        cost_estimate=cost(2 * 512 * 2304 * 256, 6 << 20),
        name="deep_last",
    )(odd, got_a, got_b, pad, w, b, acc)


def arrange_kernel(got, lanes, out):
    spread = dot(jnp.concatenate([got[c] for c in range(8)], -1), lanes[...]).astype(BF16)
    for h in range(2):
        for p in range(4):
            first = (h * 4 + p) * 128
            out[0, h * 16 : (h + 1) * 16, :, p * 128 : (p + 1) * 128] = spread[:, first : first + 128].reshape(
                16, 16, 128
            )


def arrange(got, lanes):
    return pl.pallas_call(
        arrange_kernel,
        out_shape=jax.ShapeDtypeStruct((1, 32, 16, 512), BF16),
        in_specs=[VMEM] * 2,
        out_specs=VMEM,
        compiler_params=params(16),
        cost_estimate=cost(2 * 256 * 1024 * 1024, 3 << 20),
        name="arrange",
    )(got, lanes)


def on_device(volume, fine_kernel, fine_bias, deep_kernel, deep_bias):
    odd = lax.axis_index("chan") % 2
    is_odd = odd == 1
    flag = odd.astype(jnp.int32).reshape(1)
    vol = volume.reshape(16, 8, 64, 128)

    def y_exchange(head, tail):
        got_a = swap_pairs(jnp.where(is_odd, tail, head), "chan", True)
        got_b = swap_pairs(jnp.where(is_odd, head, tail), "chan", False)
        return got_a, got_b

    tlo, thi = turn_faces(vol)
    zlo, zhi = shift(thi, "sample", 1), shift(tlo, "sample", -1)
    t1 = turn_rest(vol)
    block = jnp.concatenate([tlo[None], t1, thi[None]], 0)
    faces = y_exchange(block[:, :, 0:16], block[:, :, 112:128])
    own = jnp.concatenate([zlo[None], block, zhi[None]], 0)
    xlo, xhi = shift(own[:, 7], "space", 1), shift(own[:, 0], "space", -1)
    w = fine_kernel.reshape(3456, 256)
    b = fine_bias.reshape(1, 256)
    middle = fine_middle(own, w, b)


    def rim(y):
        rows = slice(y * 16, y * 16 + 16)
        ends = [jnp.concatenate([xlo[z : z + 1, rows], own[z, :, rows], xhi[z : z + 1, rows]], 0) for z in (0, 9)]
        return jnp.concatenate(ends + [xlo[1:9, rows], xhi[1:9, rows]], 0)

    rims = y_exchange(rim(0), rim(7))
    sides = fine_sides(own, xlo, xhi, w, b)
    send = fine_last(flag, faces, rims, fine_kernel.reshape(9, 3, 128, 256), b, middle, sides)
    got = lax.all_to_all(send, ("sample", "space"), split_axis=0, concat_axis=0, tiled=True)

    got_a, got_b = y_exchange(got[:, 0:16], got[:, 48:64])
    pad = jnp.asarray(pad_matrix(), BF16)
    dw = deep_kernel.reshape(9, 3, 256, 256)
    acc = deep_first(got, pad, dw)
    send = deep_last(flag, got_a, got_b, pad, dw, deep_bias.reshape(1, 256), acc)
    got = lax.all_to_all(send, "chan", split_axis=0, concat_axis=0, tiled=True)
    return arrange(got, jnp.asarray(lane_matrix(), BF16))


def solution(mesh):
    placed = (P(None, "sample", "space", "chan", None), P(), P(), P(), P())
    return jax.shard_map(
        on_device,
        mesh=mesh,
        in_specs=placed,
        out_specs=P(("sample", "space"), "chan", None, None),
        check_vma=False,
    )
```

```python
import jax
import jax.numpy as jnp
import numpy as np
from jax import lax
from jax.experimental import pallas as pl
from jax.experimental.pallas import tpu as pltpu
from jax.sharding import PartitionSpec as P

MIB = 1 << 20
FINE_MIB = 36
BF16 = jnp.bfloat16
F32 = jnp.float32
VMEM = pl.BlockSpec(memory_space=pltpu.VMEM)
ANY = pl.BlockSpec(memory_space=pl.ANY)


def lane_matrix():
    src = np.arange(1024).reshape(8, 8, 4, 4)
    dst = src.transpose(1, 2, 0, 3).reshape(-1)
    m = np.zeros((1024, 1024), np.float32)
    m[dst, np.arange(1024)] = 1
    return m


def pad_matrix():
    m = np.zeros((6, 6, 16, 256), np.float32)
    for i in range(6):
        for j in range(6):
            for big in range(4):
                for p in range(4):
                    z, x = (4 * big + i - 1) % 16, (4 * p + j - 1) % 16
                    m[i, j, big * 4 + p, ((z // 4) * 4 + x // 4) * 16 + (z % 4) * 4 + x % 4] = 1
    return m.reshape(576, 256)


def params(mib):
    return pltpu.CompilerParams(vmem_limit_bytes=mib * MIB)


def cost(flops, moved):
    return pl.CostEstimate(flops=flops, bytes_accessed=moved, transcendentals=0)


def leaky(value):
    return jnp.where(value >= 0, value, 0.3 * value)


def dot(a, b):
    return jnp.dot(a, b, preferred_element_type=F32)


def swap_rows():
    i = lax.broadcasted_iota(jnp.int32, (256, 256), 0)
    j = lax.broadcasted_iota(jnp.int32, (256, 256), 1)
    hit = ((i >> 4) == (j & 15)) & ((i & 15) == (j >> 4))
    return jnp.where(hit, 1.0, 0.0).astype(BF16)


def shift(value, axis, step):
    n = lax.axis_size(axis)
    return lax.ppermute(value, axis, [(i, (i + step) % n) for i in range(n)])


def swap_pairs(value, axis, odd):
    n = lax.axis_size(axis)
    pairs = []
    for i in range(n):
        up = (i % 2 == 1) if odd else (i % 2 == 0)
        pairs.append((i, (i + 1) % n if up else (i - 1) % n))
    return lax.ppermute(value, axis, pairs)


def turn(p, slab, put):
    for j in (0, 2):
        halves = [slab[:, (j + k) * 16 : (j + k) * 16 + 16].reshape(256, 128) for k in (0, 1)]
        turned = dot(p, jnp.concatenate(halves, -1)).astype(BF16)
        for k in (0, 1):
            put(2 * (j + k), turned[:, k * 128 : (k + 1) * 128].reshape(2, 128, 128))


def turn_faces_kernel(vol, lo, hi):
    p = swap_rows()
    for z, out in ((0, lo), (7, hi)):

        def put(x, value, out=out):
            out[x : x + 2] = value

        turn(p, vol[:, z], put)


def turn_faces(vol):
    return pl.pallas_call(
        turn_faces_kernel,
        out_shape=[jax.ShapeDtypeStruct((8, 128, 128), BF16)] * 2,
        in_specs=[VMEM],
        out_specs=[VMEM, VMEM],
        compiler_params=params(12),
        cost_estimate=cost(2 * 2048 * 256 * 256, 1 << 20),
        name="turn_faces",
    )(vol)


def turn_rest_kernel(vol, out):
    p = swap_rows()
    for z in range(1, 7):

        def put(x, value, z=z):
            out[z - 1, x : x + 2] = value

        turn(p, vol[:, z], put)


def turn_rest(vol):
    return pl.pallas_call(
        turn_rest_kernel,
        out_shape=jax.ShapeDtypeStruct((6, 8, 128, 128), BF16),
        in_specs=[VMEM],
        out_specs=VMEM,
        compiler_params=params(12),
        cost_estimate=cost(2 * 6144 * 256 * 256, 3 << 20),
        name="turn_rest",
    )(vol)


def edge_rows(w, e):
    first = 128 * (1 - e)
    return jnp.concatenate([w[t * 384 + first : t * 384 + first + 256] for t in range(9)], 0)


def inner_cells(planes, w, b, mid, epool):
    taps = [
        planes(dz, dx, slice(dy * 16, dy * 16 + 96)).reshape(1536, 128)
        for dz in range(3)
        for dx in range(3)
        for dy in range(3)
    ]
    acc = dot(jnp.concatenate(taps, -1), w[...])
    acc = acc.reshape(2, 2, 2, 2, 6, 16, 256).max(axis=(1, 3))
    epool[0] = acc[:, :, 0]
    epool[1] = acc[:, :, 5]
    for y in (0, 1):
        inner = jnp.maximum(acc[:, :, 1 + 2 * y], acc[:, :, 2 + 2 * y])
        mid[y] = leaky(inner + b[...]).astype(BF16)


INNER_OUT = [
    jax.ShapeDtypeStruct((2, 2, 2, 16, 256), BF16),
    jax.ShapeDtypeStruct((2, 2, 2, 16, 256), F32),
]


def fine_inner_kernel(block, w, b, mid, epool):
    def planes(dz, dx, rows):
        return block[1 + dz : 5 + dz, 1 + dx : 5 + dx, rows]

    inner_cells(planes, w, b, mid, epool)


def fine_inner(block, w, b):
    return pl.pallas_call(
        fine_inner_kernel,
        out_shape=INNER_OUT,
        in_specs=[VMEM] * 3,
        out_specs=[VMEM] * 2,
        compiler_params=params(FINE_MIB),
        cost_estimate=cost(1536 * 3456 * 256 * 2, 5 << 20),
        name="fine_inner",
    )(block, w, b)


def fine_outer_kernel(own, w, b, mid, epool, eacc):
    def planes(dz, dx, rows):
        return jnp.concatenate([own[z + dz : z + dz + 2, 1 + dx : 5 + dx, rows] for z in (0, 6)], 0)

    inner_cells(planes, w, b, mid, epool)
    for e in (0, 1):
        taps = [
            own[dz : dz + 8, 1 + dx : 5 + dx, (6 * e + k) * 16 : (6 * e + k + 1) * 16].reshape(512, 128)
            for dz in range(3)
            for dx in range(3)
            for k in (0, 1)
        ]
        eacc[e] = dot(jnp.concatenate(taps, -1), edge_rows(w, e)).reshape(8, 4, 16, 256)


def fine_outer(own, w, b):
    return pl.pallas_call(
        fine_outer_kernel,
        out_shape=INNER_OUT + [jax.ShapeDtypeStruct((2, 8, 4, 16, 256), F32)],
        in_specs=[VMEM] * 3,
        out_specs=[VMEM] * 3,
        compiler_params=params(FINE_MIB),
        cost_estimate=cost(2560 * 3456 * 256 * 2, 7 << 20),
        name="fine_outer",
    )(own, w, b)


def fine_faces_kernel(odd, got_a, got_b, w, eacc, out, ys):
    ys[...] = jnp.zeros_like(ys)
    for k, (got, e) in enumerate(((got_a, odd[0]), (got_b, 1 - odd[0]))):
        ys[k, 1:9, 1:9] = got[...]
        taps = [ys[k, dz : dz + 8, dx : dx + 8].reshape(1024, 128) for dz in range(3) for dx in range(3)]
        acc = dot(jnp.concatenate(taps, -1), w[:, pl.ds(2 * e, 1)].reshape(1152, 256))
        acc = acc.reshape(8, 8, 16, 256)
        one = pl.ds(e, 1)
        out[one, :, 0:2] = acc[None, :, 0:2]
        out[one, :, 6:8] = acc[None, :, 6:8]
        out[one, :, 2:6] = acc[None, :, 2:6] + eacc[one]


def fine_faces(odd, faces, w, eacc):
    return pl.pallas_call(
        fine_faces_kernel,
        out_shape=jax.ShapeDtypeStruct((2, 8, 8, 16, 256), F32),
        in_specs=[pl.BlockSpec(memory_space=pltpu.SMEM)] + [VMEM] * 4,
        out_specs=VMEM,
        scratch_shapes=[pltpu.VMEM((2, 10, 10, 16, 128), BF16)],
        compiler_params=params(20),
        cost_estimate=cost(2 * 2048 * 1152 * 256, 6 << 20),
        name="fine_faces",
    )(odd, *faces, w, eacc)


def fine_sides_kernel(own, xlo, xhi, w, b, mid, eacc, epool):
    def planes(side, dx, z, n, rows):
        if side == 0 and dx == 0:
            return jnp.concatenate([xlo[z : z + n, rows][:, None], own[z : z + n, 0:1, rows]], 1)
        if side == 1 and dx == 2:
            return jnp.concatenate([own[z : z + n, 7:8, rows], xhi[z : z + n, rows][:, None]], 1)
        first = dx - 1 if side == 0 else 5 + dx
        return own[z : z + n, first : first + 2, rows]

    for side in (0, 1):
        taps = [
            planes(side, dx, dz, 8, slice(dy * 16, dy * 16 + 96)).reshape(1536, 128)
            for dz in range(3)
            for dx in range(3)
            for dy in range(3)
        ]
        acc = dot(jnp.concatenate(taps, -1), w[...])
        acc = acc.reshape(4, 2, 2, 6, 16, 256).max(axis=(1, 2))
        epool[0, :, side] = acc[:, 0]
        epool[1, :, side] = acc[:, 5]
        for y in (0, 1):
            inner = jnp.maximum(acc[:, 1 + 2 * y], acc[:, 2 + 2 * y])
            mid[y, :, side] = leaky(inner + b[...]).astype(BF16)
    for e in (0, 1):
        taps = [
            jnp.concatenate(
                [
                    planes(side, dx, dz, 8, slice((6 * e + k) * 16, (6 * e + k + 1) * 16)).reshape(256, 128)
                    for side in (0, 1)
                ],
                0,
            )
            for dz in range(3)
            for dx in range(3)
            for k in (0, 1)
        ]
        eacc[e] = dot(jnp.concatenate(taps, -1), edge_rows(w, e)).reshape(2, 8, 2, 16, 256)


def fine_sides(own, xlo, xhi, w, b):
    return pl.pallas_call(
        fine_sides_kernel,
        out_shape=[
            jax.ShapeDtypeStruct((2, 4, 2, 16, 256), BF16),
            jax.ShapeDtypeStruct((2, 2, 8, 2, 16, 256), F32),
            jax.ShapeDtypeStruct((2, 4, 2, 16, 256), F32),
        ],
        in_specs=[VMEM] * 5,
        out_specs=[VMEM] * 3,
        compiler_params=params(FINE_MIB),
        cost_estimate=cost(4096 * 3456 * 256 * 2, 8 << 20),
        name="fine_sides",
    )(own, xlo, xhi, w, b)


def fine_last_kernel(odd, rim_a, rim_b, w, b, facc, mid_i, epool_i, mid_o, epool_o, mid_s, eacc_s, epool_s, out, sums):
    p = swap_rows()

    def emit(y, plane):
        out[:, pl.ds(pl.multiple_of(y * 16, 16), 16)] = (
            dot(p, plane.reshape(256, 256)).astype(BF16).reshape(16, 16, 256)
        )

    def whole(sides, outer, inner):
        middle = jnp.concatenate([outer[0:1], inner, outer[1:2]], 0)
        return jnp.concatenate([sides[:, 0:1], middle, sides[:, 1:2]], 1)

    for y in (0, 1):
        emit(1 + y, whole(mid_s[y], mid_o[y], mid_i[y]))
    zero = jnp.zeros((1, 16, 128), BF16)
    for k, (rim, e) in enumerate(((rim_a, odd[0]), (rim_b, 1 - odd[0]))):
        one = pl.ds(e, 1)
        acc = sums.at[k]
        acc[:, 2:6] = facc[one, :, 2:6][0]
        acc[:, 0:2] = facc[one, :, 0:2][0] + eacc_s[one, 0][0]
        acc[:, 6:8] = facc[one, :, 6:8][0] + eacc_s[one, 1][0]

        def side(cells, taps):
            left = jnp.concatenate([cells[t : t + 8].reshape(128, 128) for t in range(3)], -1)
            rows = jnp.concatenate([w[t, pl.ds(2 * e, 1)][0] for t in taps], 0)
            return dot(left, rows).reshape(8, 16, 256)

        acc[0] += side(rim[0:10], (0, 1, 2))
        acc[7] += side(rim[10:20], (6, 7, 8))
        acc[:, 0] += side(jnp.concatenate([zero, rim[20:28], zero], 0), (0, 3, 6))
        acc[:, 7] += side(jnp.concatenate([zero, rim[28:36], zero], 0), (2, 5, 8))
        plane = acc[...].reshape(4, 2, 4, 2, 16, 256).max(axis=(1, 3))
        known = whole(
            jnp.stack([epool_s[one, :, x][0] for x in (0, 1)], 1), epool_o[one][0], epool_i[one][0]
        )
        emit(3 * e, leaky(jnp.maximum(plane, known) + b[...]).astype(BF16))


def fine_last(odd, rims, w, b, facc, inner, outer, sides):
    return pl.pallas_call(
        fine_last_kernel,
        out_shape=jax.ShapeDtypeStruct((16, 64, 256), BF16),
        in_specs=[pl.BlockSpec(memory_space=pltpu.SMEM)] + [VMEM] * 12,
        out_specs=VMEM,
        scratch_shapes=[pltpu.VMEM((2, 8, 8, 16, 256), F32)],
        compiler_params=params(20),
        cost_estimate=cost(2 * 1024 * 384 * 256, 6 << 20),
        name="fine_last",
    )(odd, *rims, w, b, facc, *inner, *outer, *sides)


def deep_first_kernel(got, pad, w, out, xs):
    for y in range(4):
        plane = got[:, y * 16 : y * 16 + 16].reshape(256, 256)
        xs[y] = dot(pad[...], plane).astype(BF16).reshape(6, 6, 16, 256)
    for first, size, dys in ((1, 2, (0, 1, 2)), (0, 1, (1, 2)), (3, 1, (0, 1))):
        taps = [
            xs[first + dy - 1 : first + dy - 1 + size, dz : dz + 4, dx : dx + 4].reshape(256 * size, 256)
            for dz in range(3)
            for dx in range(3)
            for dy in dys
        ]
        rows = [w[t, dy] for t in range(9) for dy in dys]
        acc = dot(jnp.concatenate(taps, -1), jnp.concatenate(rows, 0))
        out[first : first + size] = acc.reshape(size, 4, 4, 16, 256)


def deep_first(got, pad, w):
    return pl.pallas_call(
        deep_first_kernel,
        out_shape=jax.ShapeDtypeStruct((4, 4, 4, 16, 256), F32),
        in_specs=[VMEM] * 3,
        out_specs=VMEM,
        scratch_shapes=[pltpu.VMEM((4, 6, 6, 16, 256), BF16)],
        compiler_params=params(40),
        cost_estimate=cost(2 * 1024 * 6912 * 256, 6 << 20),
        name="deep_first",
    )(got, pad, w)


def deep_last_kernel(odd, got_a, got_b, pad, w, b, acc_in, out, ys, full, turned):
    p = swap_rows()
    for y in (1, 2):
        full[:, :, y] = leaky(acc_in[y] + b[...]).astype(BF16)
    for k, (got, e) in enumerate(((got_a, odd[0]), (got_b, 1 - odd[0]))):
        ys[k] = dot(pad[...], got[...].reshape(256, 256)).astype(BF16).reshape(6, 6, 16, 256)
        taps = [ys[k, dz : dz + 4, dx : dx + 4].reshape(256, 256) for dz in range(3) for dx in range(3)]
        acc = dot(jnp.concatenate(taps, -1), w[:, pl.ds(2 * e, 1)].reshape(2304, 256))
        acc = acc.reshape(4, 4, 16, 256) + acc_in[pl.ds(3 * e, 1)][0]
        full[:, :, pl.ds(3 * e, 1)] = leaky(acc + b[...]).astype(BF16)[:, :, None]
    planes = [dot(p, full[z].reshape(256, 256)).reshape(16, 16, 256) for z in range(4)]
    lane = lax.broadcasted_iota(jnp.int32, (128, 128), 1)
    for big in range(4):
        for z in (0, 2):
            rows = [planes[z + k][big * 4 : big * 4 + 4].reshape(64, 256) for k in (0, 1)]
            flipped = jnp.concatenate(rows, 0).T.reshape(8, 2, 16, 128)
            low = flipped[:, 0].reshape(128, 128)
            high = flipped[:, 1].reshape(128, 128)
            first = jnp.where(lane < 64, low, pltpu.roll(high, 64, 1))
            second = jnp.where(lane < 64, pltpu.roll(low, 64, 1), high)
            turned[big * 4 + z] = first.astype(BF16).reshape(8, 16, 128)
            turned[big * 4 + z + 1] = second.astype(BF16).reshape(8, 16, 128)
    for c in (0, 2, 4, 6):
        pair = [turned[:, c + k].reshape(256, 128) for k in (0, 1)]
        moved = dot(p, jnp.concatenate(pair, -1)).astype(BF16)
        for k in (0, 1):
            out[c + k] = moved[:, k * 128 : (k + 1) * 128]


def deep_last(odd, got_a, got_b, pad, w, b, acc):
    return pl.pallas_call(
        deep_last_kernel,
        out_shape=jax.ShapeDtypeStruct((8, 256, 128), BF16),
        in_specs=[pl.BlockSpec(memory_space=pltpu.SMEM)] + [VMEM] * 6,
        out_specs=VMEM,
        scratch_shapes=[
            pltpu.VMEM((2, 6, 6, 16, 256), BF16),
            pltpu.VMEM((4, 4, 4, 16, 256), BF16),
            pltpu.VMEM((16, 8, 16, 128), BF16),
        ],
        compiler_params=params(24),
        cost_estimate=cost(2 * 512 * 2304 * 256, 6 << 20),
        name="deep_last",
    )(odd, got_a, got_b, pad, w, b, acc)


def arrange_kernel(got, lanes, out):
    spread = dot(jnp.concatenate([got[c] for c in range(8)], -1), lanes[...]).astype(BF16)
    for h in range(2):
        for p in range(4):
            first = (h * 4 + p) * 128
            out[0, h * 16 : (h + 1) * 16, :, p * 128 : (p + 1) * 128] = spread[:, first : first + 128].reshape(
                16, 16, 128
            )


def arrange(got, lanes):
    return pl.pallas_call(
        arrange_kernel,
        out_shape=jax.ShapeDtypeStruct((1, 32, 16, 512), BF16),
        in_specs=[VMEM] * 2,
        out_specs=VMEM,
        compiler_params=params(16),
        cost_estimate=cost(2 * 256 * 1024 * 1024, 3 << 20),
        name="arrange",
    )(got, lanes)


def on_device(volume, fine_kernel, fine_bias, deep_kernel, deep_bias):
    odd = lax.axis_index("chan") % 2
    is_odd = odd == 1
    flag = odd.astype(jnp.int32).reshape(1)
    vol = volume.reshape(16, 8, 64, 128)

    def y_exchange(head, tail):
        got_a = swap_pairs(jnp.where(is_odd, tail, head), "chan", True)
        got_b = swap_pairs(jnp.where(is_odd, head, tail), "chan", False)
        return got_a, got_b

    tlo, thi = turn_faces(vol)
    zlo, zhi = shift(thi, "sample", 1), shift(tlo, "sample", -1)
    t1 = turn_rest(vol)
    block = jnp.concatenate([tlo[None], t1, thi[None]], 0)
    faces = y_exchange(block[:, :, 0:16], block[:, :, 112:128])
    own = jnp.concatenate([zlo[None], block, zhi[None]], 0)
    xlo, xhi = shift(own[:, 7], "space", 1), shift(own[:, 0], "space", -1)
    w = fine_kernel.reshape(3456, 256)
    b = fine_bias.reshape(1, 256)
    w9 = fine_kernel.reshape(9, 3, 128, 256)
    inner = fine_inner(block, w, b)
    mid, epool, eacc = fine_outer(own, w, b)
    facc = fine_faces(flag, faces, w9, eacc)


    def rim(y):
        rows = slice(y * 16, y * 16 + 16)
        ends = [jnp.concatenate([xlo[z : z + 1, rows], own[z, :, rows], xhi[z : z + 1, rows]], 0) for z in (0, 9)]
        return jnp.concatenate(ends + [xlo[1:9, rows], xhi[1:9, rows]], 0)

    rims = y_exchange(rim(0), rim(7))
    sides = fine_sides(own, xlo, xhi, w, b)
    send = fine_last(flag, rims, w9, b, facc, inner, (mid, epool), sides)
    got = lax.all_to_all(send, ("sample", "space"), split_axis=0, concat_axis=0, tiled=True)

    got_a, got_b = y_exchange(got[:, 0:16], got[:, 48:64])
    pad = jnp.asarray(pad_matrix(), BF16)
    dw = deep_kernel.reshape(9, 3, 256, 256)
    acc = deep_first(got, pad, dw)
    send = deep_last(flag, got_a, got_b, pad, dw, deep_bias.reshape(1, 256), acc)
    got = lax.all_to_all(send, "chan", split_axis=0, concat_axis=0, tiled=True)
    return arrange(got, jnp.asarray(lane_matrix(), BF16))


def solution(mesh):
    placed = (P(None, "sample", "space", "chan", None), P(), P(), P(), P())
    return jax.shard_map(
        on_device,
        mesh=mesh,
        in_specs=placed,
        out_specs=P(("sample", "space"), "chan", None, None),
        check_vma=False,
    )
```

```python
import jax
import jax.numpy as jnp
import numpy as np
from jax import lax
from jax.experimental import pallas as pl
from jax.experimental.pallas import tpu as pltpu
from jax.sharding import PartitionSpec as P

MIB = 1 << 20
FINE_MIB = 36
BF16 = jnp.bfloat16
F32 = jnp.float32
VMEM = pl.BlockSpec(memory_space=pltpu.VMEM)
ANY = pl.BlockSpec(memory_space=pl.ANY)


def lane_matrix():
    src = np.arange(1024).reshape(8, 8, 4, 4)
    dst = src.transpose(1, 2, 0, 3).reshape(-1)
    m = np.zeros((1024, 1024), np.float32)
    m[dst, np.arange(1024)] = 1
    return m


def pad_matrix():
    m = np.zeros((6, 6, 16, 256), np.float32)
    for i in range(6):
        for j in range(6):
            for big in range(4):
                for p in range(4):
                    z, x = (4 * big + i - 1) % 16, (4 * p + j - 1) % 16
                    m[i, j, big * 4 + p, ((z // 4) * 4 + x // 4) * 16 + (z % 4) * 4 + x % 4] = 1
    return m.reshape(576, 256)


def params(mib):
    return pltpu.CompilerParams(vmem_limit_bytes=mib * MIB)


def cost(flops, moved):
    return pl.CostEstimate(flops=flops, bytes_accessed=moved, transcendentals=0)


def leaky(value):
    return jnp.where(value >= 0, value, 0.3 * value)


def dot(a, b):
    return jnp.dot(a, b, preferred_element_type=F32)


def swap_rows():
    i = lax.broadcasted_iota(jnp.int32, (256, 256), 0)
    j = lax.broadcasted_iota(jnp.int32, (256, 256), 1)
    hit = ((i >> 4) == (j & 15)) & ((i & 15) == (j >> 4))
    return jnp.where(hit, 1.0, 0.0).astype(BF16)


def shift(value, axis, step):
    n = lax.axis_size(axis)
    return lax.ppermute(value, axis, [(i, (i + step) % n) for i in range(n)])


def swap_pairs(value, axis, odd):
    n = lax.axis_size(axis)
    pairs = []
    for i in range(n):
        up = (i % 2 == 1) if odd else (i % 2 == 0)
        pairs.append((i, (i + 1) % n if up else (i - 1) % n))
    return lax.ppermute(value, axis, pairs)


def turn(p, slab, put):
    for j in (0, 2):
        halves = [slab[:, (j + k) * 16 : (j + k) * 16 + 16].reshape(256, 128) for k in (0, 1)]
        turned = dot(p, jnp.concatenate(halves, -1)).astype(BF16)
        for k in (0, 1):
            put(2 * (j + k), turned[:, k * 128 : (k + 1) * 128].reshape(2, 128, 128))


def turn_all_kernel(vol, block, lo, hi):
    p = swap_rows()
    for z in (0, 7, 1, 2, 3, 4, 5, 6):

        def put(x, value, z=z):
            block[z, x : x + 2] = value
            if z == 0:
                lo[x : x + 2] = value
            if z == 7:
                hi[x : x + 2] = value

        turn(p, vol[:, z], put)


def turn_all(vol):
    face = jax.ShapeDtypeStruct((8, 128, 128), BF16)
    return pl.pallas_call(
        turn_all_kernel,
        out_shape=[jax.ShapeDtypeStruct((8, 8, 128, 128), BF16), face, face],
        in_specs=[VMEM],
        out_specs=[VMEM] * 3,
        compiler_params=params(12),
        cost_estimate=cost(2 * 8192 * 256 * 256, 4 << 20),
        name="turn_all",
    )(vol)


def pool_inner(acc, mid, epool):
    parts = [acc[:, 0:1], jnp.maximum(acc[:, 1:2], acc[:, 2:3]), jnp.maximum(acc[:, 3:4], acc[:, 4:5]), acc[:, 5:6]]
    acc = jnp.concatenate(parts, 1)
    epool[0] = acc[:, :, 0]
    epool[1] = acc[:, :, 5]
    for y in (0, 1):
        mid[y] = jnp.maximum(acc[:, :, 1 + 2 * y], acc[:, :, 2 + 2 * y])


def tap_rows(planes, dys, first, count):
    return [
        planes(dz, dx, slice((first + dy) * 16, (first + dy + count) * 16))
        for dz in range(3)
        for dx in range(3)
        for dy in dys
    ]


def inner_cells(planes, cells, w, mid, epool):
    taps = [t.reshape(cells * 96, 128) for t in tap_rows(planes, (0, 1, 2), 0, 6)]
    acc = dot(jnp.concatenate(taps, -1), w[...])
    pool_inner(acc.reshape(cells // 12, 2, 6, 6, 16, 256).max(axis=1), mid, epool)


def edge_rows(w, e):
    first = 128 * (1 - e)
    return jnp.concatenate([w[t * 384 + first : t * 384 + first + 256] for t in range(9)], 0)


def edge_cells(planes, cells, w, eacc):
    for e in (0, 1):
        taps = [t.reshape(cells * 16, 128) for t in tap_rows(planes, (0, 1), 6 * e, 1)]
        acc = dot(jnp.concatenate(taps, -1), edge_rows(w, e))
        eacc[e] = acc.reshape(eacc.shape[1:])


def pooled_f32(pairs):
    return jax.ShapeDtypeStruct((2, pairs, 4, 16, 256), F32)


def fine_call(kernel, outs, name, cells, operands):
    return pl.pallas_call(
        kernel,
        out_shape=outs,
        in_specs=[VMEM] * len(operands),
        out_specs=[VMEM] * len(outs),
        compiler_params=params(FINE_MIB),
        cost_estimate=cost(cells * 16 * 3456 * 256 * 2, 5 << 20),
        name=name,
    )(*operands)


def fine_inner_kernel(block, w, mid, epool, eacc):
    def planes(dz, dx, rows):
        return block[1 + dz : 5 + dz, dx : 6 + dx, rows]

    inner_cells(planes, 24, w, mid, epool)
    edge_cells(planes, 24, w, eacc)


def fine_inner(block, w):
    outs = [pooled_f32(2), pooled_f32(2), jax.ShapeDtypeStruct((2, 4, 6, 16, 256), F32)]
    return fine_call(fine_inner_kernel, outs, "fine_inner", 184, (block, w))


def low_planes(zlo, block):
    def planes(dz, dx, rows):
        if dz == 0:
            return jnp.concatenate([zlo[dx : 6 + dx, rows][None], block[0:1, dx : 6 + dx, rows]], 0)
        return block[dz - 1 : dz + 1, dx : 6 + dx, rows]

    return planes


def high_planes(block, zhi):
    def planes(dz, dx, rows):
        if dz == 2:
            return jnp.concatenate([block[7:8, dx : 6 + dx, rows], zhi[dx : 6 + dx, rows][None]], 0)
        return block[5 + dz : 7 + dz, dx : 6 + dx, rows]

    return planes


def fine_low_kernel(zlo, block, w, mid, epool):
    inner_cells(low_planes(zlo, block), 12, w, mid, epool)


def fine_low(zlo, block, w):
    return fine_call(fine_low_kernel, [pooled_f32(1), pooled_f32(1)], "fine_low", 76, (zlo, block, w))


def fine_high_kernel(zlo, block, zhi, w, mid, epool, eacc):
    low, high = low_planes(zlo, block), high_planes(block, zhi)
    inner_cells(high, 12, w, mid, epool)

    def planes(dz, dx, rows):
        return jnp.concatenate([low(dz, dx, rows), high(dz, dx, rows)], 0)

    edge_cells(planes, 24, w, eacc)


def fine_high(zlo, block, zhi, w):
    outs = [pooled_f32(1), pooled_f32(1), jax.ShapeDtypeStruct((2, 4, 6, 16, 256), F32)]
    return fine_call(fine_high_kernel, outs, "fine_high", 112, (zlo, block, zhi, w))


def emitter(p, out, b):
    def emit(y, plane):
        cells = leaky(plane + b[...]).astype(BF16).reshape(256, 256)
        out[:, pl.ds(y * 16 if isinstance(y, int) else pl.multiple_of(y * 16, 16), 16)] = (
            dot(p, cells).astype(BF16).reshape(16, 16, 256)
        )

    return emit


def fine_sides_kernel(
    xlo, xhi, zlo, block, zhi, w, b, mid_i, epool_i, mid_l, epool_l, mid_h, epool_h, outm, epool, eacc
):
    def column(x, dz, rows):
        if dz == 0:
            return jnp.concatenate([zlo[x : x + 1, rows], block[0:7, x, rows]], 0)
        if dz == 1:
            return block[0:8, x, rows]
        return jnp.concatenate([block[1:8, x, rows], zhi[x : x + 1, rows]], 0)

    def planes(dz, dx, rows):
        first = xlo[dz : dz + 8, rows] if dx == 0 else column(dx - 1, dz, rows)
        second = xhi[dz : dz + 8, rows] if dx == 2 else column(6 + dx, dz, rows)
        return jnp.stack([first, second], 1)

    taps = [t.reshape(1536, 128) for t in tap_rows(planes, (0, 1, 2), 0, 6)]
    acc = dot(jnp.concatenate(taps, -1), w[...]).reshape(4, 2, 2, 6, 16, 256).max(axis=1)

    def whole(sides, low, inner, high):
        plane = jnp.concatenate([low, inner, high], 0)
        first = jnp.maximum(plane[:, 0:1], sides[:, 0:1])
        last = jnp.maximum(plane[:, 3:4], sides[:, 1:2])
        return jnp.concatenate([first, plane[:, 1:3], last], 1)

    for e in (0, 1):
        epool[e] = whole(acc[:, :, 5 * e], epool_l[e], epool_i[e], epool_h[e])
    emit = emitter(swap_rows(), outm, b)
    for y in (0, 1):
        inner = jnp.maximum(acc[:, :, 1 + 2 * y], acc[:, :, 2 + 2 * y])
        emit(y, whole(inner, mid_l[y], mid_i[y], mid_h[y]))
    edge_cells(planes, 16, w, eacc)


def fine_sides(*operands):
    outs = [
        jax.ShapeDtypeStruct((16, 32, 256), BF16),
        pooled_f32(4),
        jax.ShapeDtypeStruct((2, 8, 2, 16, 256), F32),
    ]
    return fine_call(fine_sides_kernel, outs, "fine_sides", 124, operands)


def fine_faces_kernel(odd, got_a, got_b, w, eacc_i, eacc_o, out, ys):
    ys[...] = jnp.zeros_like(ys)
    for k, (got, e) in enumerate(((got_a, odd[0]), (got_b, 1 - odd[0]))):
        ys[k, 1:9, 1:9] = got[...]
        taps = [ys[k, dz : dz + 8, dx : dx + 8].reshape(1024, 128) for dz in range(3) for dx in range(3)]
        acc = dot(jnp.concatenate(taps, -1), w[:, pl.ds(2 * e, 1)].reshape(1152, 256))
        acc = acc.reshape(8, 8, 16, 256)
        one = pl.ds(e, 1)
        out[one, :, 0] = acc[None, :, 0]
        out[one, :, 7] = acc[None, :, 7]
        out[one, 0:2, 1:7] = acc[None, 0:2, 1:7] + eacc_o[one, 0:2]
        out[one, 2:6, 1:7] = acc[None, 2:6, 1:7] + eacc_i[one]
        out[one, 6:8, 1:7] = acc[None, 6:8, 1:7] + eacc_o[one, 2:4]


def fine_faces(odd, faces, w, eacc_i, eacc_o):
    return pl.pallas_call(
        fine_faces_kernel,
        out_shape=jax.ShapeDtypeStruct((2, 8, 8, 16, 256), F32),
        in_specs=[pl.BlockSpec(memory_space=pltpu.SMEM)] + [VMEM] * 5,
        out_specs=VMEM,
        scratch_shapes=[pltpu.VMEM((2, 10, 10, 16, 128), BF16)],
        compiler_params=params(20),
        cost_estimate=cost(2 * 2048 * 1152 * 256, 6 << 20),
        name="fine_faces",
    )(odd, *faces, w, eacc_i, eacc_o)


def fine_last_kernel(odd, zlo, zhi, xlo, xhi, w, b, facc, outm, epool, eacc, out, sums):
    emit = emitter(swap_rows(), out, b)
    out[:, 16:48] = outm[...]
    zero = jnp.zeros((1, 16, 128), BF16)
    for k, e in enumerate((odd[0], 1 - odd[0])):
        one = pl.ds(e, 1)
        acc = sums.at[k]
        acc[:, 1:7] = facc[one, :, 1:7][0]
        acc[:, 0] = facc[one, :, 0][0] + eacc[one, :, 0][0]
        acc[:, 7] = facc[one, :, 7][0] + eacc[one, :, 1][0]

        def side(cells, taps):
            cells = jnp.concatenate(cells, 0)
            left = jnp.concatenate([cells[t : t + 8].reshape(128, 128) for t in range(3)], -1)
            rows = jnp.concatenate([w[t, pl.ds(2 * e, 1)][0] for t in taps], 0)
            return dot(left, rows).reshape(8, 16, 256)

        c, z = 10 * k, 8 * k
        acc[0] += side([xlo[c : c + 1], zlo[z : z + 8], xhi[c : c + 1]], (0, 1, 2))
        acc[7] += side([xlo[c + 9 : c + 10], zhi[z : z + 8], xhi[c + 9 : c + 10]], (6, 7, 8))
        acc[:, 0] += side([zero, xlo[c + 1 : c + 9], zero], (0, 3, 6))
        acc[:, 7] += side([zero, xhi[c + 1 : c + 9], zero], (2, 5, 8))
        plane = acc[...].reshape(4, 2, 4, 2, 16, 256).max(axis=(1, 3))
        emit(3 * e, jnp.maximum(plane, epool[one][0]))


def fine_last(odd, strips, w, b, facc, sides):
    return pl.pallas_call(
        fine_last_kernel,
        out_shape=jax.ShapeDtypeStruct((16, 64, 256), BF16),
        in_specs=[pl.BlockSpec(memory_space=pltpu.SMEM)] + [VMEM] * 10,
        out_specs=VMEM,
        scratch_shapes=[pltpu.VMEM((2, 8, 8, 16, 256), F32)],
        compiler_params=params(20),
        cost_estimate=cost(2 * 1024 * 384 * 256, 6 << 20),
        name="fine_last",
    )(odd, *strips, w, b, facc, *sides)


def deep_first_kernel(got, pad, w, out, xs):
    for y in range(4):
        plane = got[:, y * 16 : y * 16 + 16].reshape(256, 256)
        xs[y] = dot(pad[...], plane).astype(BF16).reshape(6, 6, 16, 256)
    for first, size, dys in ((1, 2, (0, 1, 2)), (0, 1, (1, 2)), (3, 1, (0, 1))):
        taps = [
            xs[first + dy - 1 : first + dy - 1 + size, dz : dz + 4, dx : dx + 4].reshape(256 * size, 256)
            for dz in range(3)
            for dx in range(3)
            for dy in dys
        ]
        rows = [w[t, dy] for t in range(9) for dy in dys]
        acc = dot(jnp.concatenate(taps, -1), jnp.concatenate(rows, 0))
        out[first : first + size] = acc.reshape(size, 4, 4, 16, 256)


def deep_first(got, pad, w):
    return pl.pallas_call(
        deep_first_kernel,
        out_shape=jax.ShapeDtypeStruct((4, 4, 4, 16, 256), F32),
        in_specs=[VMEM] * 3,
        out_specs=VMEM,
        scratch_shapes=[pltpu.VMEM((4, 6, 6, 16, 256), BF16)],
        compiler_params=params(40),
        cost_estimate=cost(2 * 1024 * 6912 * 256, 6 << 20),
        name="deep_first",
    )(got, pad, w)


def deep_last_kernel(odd, got_a, got_b, pad, w, b, acc_in, out, ys, full, turned):
    p = swap_rows()
    for y in (1, 2):
        full[:, :, y] = leaky(acc_in[y] + b[...]).astype(BF16)
    for k, (got, e) in enumerate(((got_a, odd[0]), (got_b, 1 - odd[0]))):
        ys[k] = dot(pad[...], got[...].reshape(256, 256)).astype(BF16).reshape(6, 6, 16, 256)
        taps = [ys[k, dz : dz + 4, dx : dx + 4].reshape(256, 256) for dz in range(3) for dx in range(3)]
        acc = dot(jnp.concatenate(taps, -1), w[:, pl.ds(2 * e, 1)].reshape(2304, 256))
        acc = acc.reshape(4, 4, 16, 256) + acc_in[pl.ds(3 * e, 1)][0]
        full[:, :, pl.ds(3 * e, 1)] = leaky(acc + b[...]).astype(BF16)[:, :, None]
    planes = [dot(p, full[z].reshape(256, 256)).reshape(16, 16, 256) for z in range(4)]
    lane = lax.broadcasted_iota(jnp.int32, (128, 128), 1)
    for big in range(4):
        for z in (0, 2):
            rows = [planes[z + k][big * 4 : big * 4 + 4].reshape(64, 256) for k in (0, 1)]
            flipped = jnp.concatenate(rows, 0).T.reshape(8, 2, 16, 128)
            low = flipped[:, 0].reshape(128, 128)
            high = flipped[:, 1].reshape(128, 128)
            first = jnp.where(lane < 64, low, pltpu.roll(high, 64, 1))
            second = jnp.where(lane < 64, pltpu.roll(low, 64, 1), high)
            turned[big * 4 + z] = first.astype(BF16).reshape(8, 16, 128)
            turned[big * 4 + z + 1] = second.astype(BF16).reshape(8, 16, 128)
    for c in (0, 2, 4, 6):
        pair = [turned[:, c + k].reshape(256, 128) for k in (0, 1)]
        moved = dot(p, jnp.concatenate(pair, -1)).astype(BF16)
        for k in (0, 1):
            out[c + k] = moved[:, k * 128 : (k + 1) * 128]


def deep_last(odd, got_a, got_b, pad, w, b, acc):
    return pl.pallas_call(
        deep_last_kernel,
        out_shape=jax.ShapeDtypeStruct((8, 256, 128), BF16),
        in_specs=[pl.BlockSpec(memory_space=pltpu.SMEM)] + [VMEM] * 6,
        out_specs=VMEM,
        scratch_shapes=[
            pltpu.VMEM((2, 6, 6, 16, 256), BF16),
            pltpu.VMEM((4, 4, 4, 16, 256), BF16),
            pltpu.VMEM((16, 8, 16, 128), BF16),
        ],
        compiler_params=params(24),
        cost_estimate=cost(2 * 512 * 2304 * 256, 6 << 20),
        name="deep_last",
    )(odd, got_a, got_b, pad, w, b, acc)


def arrange_kernel(got, lanes, out):
    spread = dot(jnp.concatenate([got[c] for c in range(8)], -1), lanes[...]).astype(BF16)
    for h in range(2):
        for p in range(4):
            first = (h * 4 + p) * 128
            out[0, h * 16 : (h + 1) * 16, :, p * 128 : (p + 1) * 128] = spread[:, first : first + 128].reshape(
                16, 16, 128
            )


def arrange(got, lanes):
    return pl.pallas_call(
        arrange_kernel,
        out_shape=jax.ShapeDtypeStruct((1, 32, 16, 512), BF16),
        in_specs=[VMEM] * 2,
        out_specs=VMEM,
        compiler_params=params(16),
        cost_estimate=cost(2 * 256 * 1024 * 1024, 3 << 20),
        name="arrange",
    )(got, lanes)


def on_device(volume, fine_kernel, fine_bias, deep_kernel, deep_bias):
    odd = lax.axis_index("chan") % 2
    is_odd = odd == 1
    flag = odd.astype(jnp.int32).reshape(1)
    vol = volume.reshape(16, 8, 64, 128)

    def y_exchange(head, tail):
        got_a = swap_pairs(jnp.where(is_odd, tail, head), "chan", True)
        got_b = swap_pairs(jnp.where(is_odd, head, tail), "chan", False)
        return got_a, got_b

    block, tlo, thi = turn_all(vol)
    zlo, zhi = shift(thi, "sample", 1), shift(tlo, "sample", -1)
    got_a, got_b = y_exchange(block[:, :, 0:16], block[:, :, 112:128])
    w = fine_kernel.reshape(3456, 256)
    w9 = fine_kernel.reshape(9, 3, 128, 256)
    b = fine_bias.reshape(1, 256)
    mid_i, epool_i, eacc_i = fine_inner(block, w)

    def x_face(x):
        return jnp.concatenate([zlo[x : x + 1], block[:, x], zhi[x : x + 1]], 0)

    xlo, xhi = shift(x_face(7), "space", 1), shift(x_face(0), "space", -1)
    mid_h, epool_h, eacc_o = fine_high(zlo, block, zhi, w)
    got_a, got_b, epool_h = lax.optimization_barrier((got_a, got_b, epool_h))
    rzlo = shift(jnp.concatenate([got_a[7], got_b[7]], 0), "sample", 1)
    rzhi = shift(jnp.concatenate([got_a[0], got_b[0]], 0), "sample", -1)
    mid_l, epool_l = fine_low(zlo, block, w)
    facc = fine_faces(flag, (got_a, got_b), w9, eacc_i, eacc_o)

    def rim(x):
        return jnp.concatenate(
            [rzlo[x : x + 1], got_a[:, x], rzhi[x : x + 1], rzlo[8 + x : 9 + x], got_b[:, x], rzhi[8 + x : 9 + x]], 0
        )

    rxlo, rxhi = shift(rim(7), "space", 1), shift(rim(0), "space", -1)
    sides = fine_sides(xlo, xhi, zlo, block, zhi, w, b, mid_i, epool_i, mid_l, epool_l, mid_h, epool_h)
    send = fine_last(flag, (rzlo, rzhi, rxlo, rxhi), w9, b, facc, sides)
    got = lax.all_to_all(send, ("sample", "space"), split_axis=0, concat_axis=0, tiled=True)

    got_a, got_b = y_exchange(got[:, 0:16], got[:, 48:64])
    pad = jnp.asarray(pad_matrix(), BF16)
    dw = deep_kernel.reshape(9, 3, 256, 256)
    acc = deep_first(got, pad, dw)
    send = deep_last(flag, got_a, got_b, pad, dw, deep_bias.reshape(1, 256), acc)
    got = lax.all_to_all(send, "chan", split_axis=0, concat_axis=0, tiled=True)
    return arrange(got, jnp.asarray(lane_matrix(), BF16))


def solution(mesh):
    placed = (P(None, "sample", "space", "chan", None), P(), P(), P(), P())
    return jax.shard_map(
        on_device,
        mesh=mesh,
        in_specs=placed,
        out_specs=P(("sample", "space"), "chan", None, None),
        check_vma=False,
    )
```

```python
import jax
import jax.numpy as jnp
import numpy as np
from jax import lax
from jax.experimental import pallas as pl
from jax.experimental.pallas import tpu as pltpu
from jax.sharding import PartitionSpec as P

MIB = 1 << 20
FINE_MIB = 36
BF16 = jnp.bfloat16
F32 = jnp.float32
VMEM = pl.BlockSpec(memory_space=pltpu.VMEM)
ANY = pl.BlockSpec(memory_space=pl.ANY)


def lane_matrix():
    src = np.arange(1024).reshape(8, 8, 4, 4)
    dst = src.transpose(1, 2, 0, 3).reshape(-1)
    m = np.zeros((1024, 1024), np.float32)
    m[dst, np.arange(1024)] = 1
    return m


def pad_matrix():
    m = np.zeros((6, 6, 16, 256), np.float32)
    for i in range(6):
        for j in range(6):
            for big in range(4):
                for p in range(4):
                    z, x = (4 * big + i - 1) % 16, (4 * p + j - 1) % 16
                    m[i, j, big * 4 + p, ((z // 4) * 4 + x // 4) * 16 + (z % 4) * 4 + x % 4] = 1
    return m.reshape(576, 256)


def params(mib):
    return pltpu.CompilerParams(vmem_limit_bytes=mib * MIB)


def cost(flops, moved):
    return pl.CostEstimate(flops=flops, bytes_accessed=moved, transcendentals=0)


def leaky(value):
    return jnp.where(value >= 0, value, 0.3 * value)


def dot(a, b):
    return jnp.dot(a, b, preferred_element_type=F32)


def swap_rows():
    i = lax.broadcasted_iota(jnp.int32, (256, 256), 0)
    j = lax.broadcasted_iota(jnp.int32, (256, 256), 1)
    hit = ((i >> 4) == (j & 15)) & ((i & 15) == (j >> 4))
    return jnp.where(hit, 1.0, 0.0).astype(BF16)


def shift(value, axis, step):
    n = lax.axis_size(axis)
    return lax.ppermute(value, axis, [(i, (i + step) % n) for i in range(n)])


def swap_pairs(value, axis, odd):
    n = lax.axis_size(axis)
    pairs = []
    for i in range(n):
        up = (i % 2 == 1) if odd else (i % 2 == 0)
        pairs.append((i, (i + 1) % n if up else (i - 1) % n))
    return lax.ppermute(value, axis, pairs)


def turn(p, slab, put):
    for j in (0, 2):
        halves = [slab[:, (j + k) * 16 : (j + k) * 16 + 16].reshape(256, 128) for k in (0, 1)]
        turned = dot(p, jnp.concatenate(halves, -1)).astype(BF16)
        for k in (0, 1):
            put(2 * (j + k), turned[:, k * 128 : (k + 1) * 128].reshape(2, 128, 128))


def turn_faces_kernel(vol, lo, hi, rest):
    p = swap_rows()
    for z, out in ((0, lo), (7, hi)):

        def put(x, value, out=out):
            out[x : x + 2] = value

        turn(p, vol[:, z], put)
    rest[...] = vol[:, 1:7]


def turn_faces(vol):
    face = jax.ShapeDtypeStruct((8, 128, 128), BF16)
    return pl.pallas_call(
        turn_faces_kernel,
        out_shape=[face, face, jax.ShapeDtypeStruct((16, 6, 64, 128), BF16)],
        in_specs=[VMEM],
        out_specs=[VMEM] * 3,
        compiler_params=params(12),
        cost_estimate=cost(2 * 2048 * 256 * 256, 4 << 20),
        name="turn_faces",
    )(vol)


def turn_rest_kernel(rest, lo, hi, block):
    p = swap_rows()
    block[0] = lo[...]
    block[7] = hi[...]
    for z in range(1, 7):

        def put(x, value, z=z):
            block[z, x : x + 2] = value

        turn(p, rest[:, z - 1], put)


def turn_rest(rest, lo, hi):
    return pl.pallas_call(
        turn_rest_kernel,
        out_shape=jax.ShapeDtypeStruct((8, 8, 128, 128), BF16),
        in_specs=[VMEM] * 3,
        out_specs=VMEM,
        compiler_params=params(12),
        cost_estimate=cost(2 * 6144 * 256 * 256, 4 << 20),
        name="turn_rest",
    )(rest, lo, hi)


def pool_inner(acc, z, mid, epool):
    parts = [acc[:, 0:1], jnp.maximum(acc[:, 1:2], acc[:, 2:3]), jnp.maximum(acc[:, 3:4], acc[:, 4:5]), acc[:, 5:6]]
    acc = jnp.concatenate(parts, 1)
    for i in range(acc.shape[0]):
        epool[0, z[i]] = acc[i, :, 0]
        epool[1, z[i]] = acc[i, :, 5]
        for y in (0, 1):
            mid[y, z[i]] = jnp.maximum(acc[i, :, 1 + 2 * y], acc[i, :, 2 + 2 * y])


def tap_rows(planes, dys, first, count):
    return [
        planes(dz, dx, slice((first + dy) * 16, (first + dy + count) * 16))
        for dz in range(3)
        for dx in range(3)
        for dy in dys
    ]


def inner_cells(planes, w):
    taps = [t.reshape(1152, 128) for t in tap_rows(planes, (0, 1, 2), 0, 6)]
    return dot(jnp.concatenate(taps, -1), w[...]).reshape(2, 6, 6, 16, 256)


def edge_rows(w, e):
    first = 128 * (1 - e)
    return jnp.concatenate([w[t * 384 + first : t * 384 + first + 256] for t in range(9)], 0)


def edge_cells(planes, cells, w, eacc):
    for e in (0, 1):
        taps = [t.reshape(cells * 16, 128) for t in tap_rows(planes, (0, 1), 6 * e, 1)]
        acc = dot(jnp.concatenate(taps, -1), edge_rows(w, e))
        eacc[e] = acc.reshape(eacc.shape[1:])


def pooled_f32(pairs):
    return jax.ShapeDtypeStruct((2, pairs, 4, 16, 256), F32)


def fine_call(kernel, outs, name, cells, operands, moved=5 << 20):
    return pl.pallas_call(
        kernel,
        out_shape=outs,
        in_specs=[VMEM] * len(operands),
        out_specs=[VMEM] * len(outs),
        compiler_params=params(FINE_MIB),
        cost_estimate=cost(cells * 16 * 3456 * 256 * 2, moved),
        name=name,
    )(*operands)


def fine_inner_kernel(block, w, mid, epool, eacc):
    def ends(dz, dx, rows):
        return jnp.concatenate([block[z + dz : z + dz + 1, dx : 6 + dx, rows] for z in (0, 5)], 0)

    pool_inner(inner_cells(ends, w), (0, 3), mid, epool)
    for z in (1, 2):

        def pair(dz, dx, rows, z=z):
            return block[2 * z - 1 + dz : 2 * z + 1 + dz, dx : 6 + dx, rows]

        acc = inner_cells(pair, w)
        pool_inner(jnp.maximum(acc[0:1], acc[1:2]), (z,), mid, epool)

    def planes(dz, dx, rows):
        return block[dz : 6 + dz, dx : 6 + dx, rows]

    edge_cells(planes, 36, w, eacc)


def fine_inner(block, w):
    outs = [pooled_f32(4), pooled_f32(4), jax.ShapeDtypeStruct((2, 6, 6, 16, 256), F32)]
    return fine_call(fine_inner_kernel, outs, "fine_inner", 270, (block, w))


def fine_ends_kernel(zlo, block, zhi, w, mid, epool, eacc):
    def planes(dz, dx, rows):
        low = zlo[dx : 6 + dx, rows] if dz == 0 else block[dz - 1, dx : 6 + dx, rows]
        high = zhi[dx : 6 + dx, rows] if dz == 2 else block[6 + dz, dx : 6 + dx, rows]
        return jnp.stack([low, high], 0)

    pool_inner(inner_cells(planes, w), (0, 1), mid, epool)
    edge_cells(planes, 12, w, eacc)


def fine_ends(zlo, block, zhi, w):
    outs = [pooled_f32(2), pooled_f32(2), jax.ShapeDtypeStruct((2, 2, 6, 16, 256), F32)]
    return fine_call(fine_ends_kernel, outs, "fine_ends", 90, (zlo, block, zhi, w))


def emitter(p, out, b):
    def emit(y, plane):
        cells = leaky(plane + b[...]).astype(BF16).reshape(256, 256)
        out[:, pl.ds(y * 16 if isinstance(y, int) else pl.multiple_of(y * 16, 16), 16)] = (
            dot(p, cells).astype(BF16).reshape(16, 16, 256)
        )

    return emit


def fine_sides_kernel(
    xlo, xhi, zlo, block, zhi, w, b, mid_i, epool_i, mid_z, epool_z, outm, epool, eacc
):
    def column(x, dz, rows):
        if dz == 0:
            return jnp.concatenate([zlo[x : x + 1, rows], block[0:7, x, rows]], 0)
        if dz == 1:
            return block[0:8, x, rows]
        return jnp.concatenate([block[1:8, x, rows], zhi[x : x + 1, rows]], 0)

    def planes(dz, dx, rows):
        first = xlo[dz : dz + 8, rows] if dx == 0 else column(dx - 1, dz, rows)
        second = xhi[dz : dz + 8, rows] if dx == 2 else column(6 + dx, dz, rows)
        return jnp.stack([first, second], 1)

    taps = [t.reshape(1536, 128) for t in tap_rows(planes, (0, 1, 2), 0, 6)]
    acc = dot(jnp.concatenate(taps, -1), w[...]).reshape(4, 2, 2, 6, 16, 256).max(axis=1)

    def whole(sides, inner, ends):
        low = jnp.maximum(inner[0:1], ends[0:1])
        high = jnp.maximum(inner[3:4], ends[1:2])
        plane = jnp.concatenate([low, inner[1:3], high], 0)
        first = jnp.maximum(plane[:, 0:1], sides[:, 0:1])
        last = jnp.maximum(plane[:, 3:4], sides[:, 1:2])
        return jnp.concatenate([first, plane[:, 1:3], last], 1)

    for e in (0, 1):
        epool[e] = whole(acc[:, :, 5 * e], epool_i[e], epool_z[e])
    emit = emitter(swap_rows(), outm, b)
    for y in (0, 1):
        inner = jnp.maximum(acc[:, :, 1 + 2 * y], acc[:, :, 2 + 2 * y])
        emit(y, whole(inner, mid_i[y], mid_z[y]))
    edge_cells(planes, 16, w, eacc)


def fine_sides(*operands):
    outs = [
        jax.ShapeDtypeStruct((16, 32, 256), BF16),
        pooled_f32(4),
        jax.ShapeDtypeStruct((2, 8, 2, 16, 256), F32),
    ]
    return fine_call(fine_sides_kernel, outs, "fine_sides", 124, operands)


def fine_faces_kernel(odd, got_a, got_b, w, eacc_i, eacc_z, out, ys):
    ys[...] = jnp.zeros_like(ys)
    for k, (got, e) in enumerate(((got_a, odd[0]), (got_b, 1 - odd[0]))):
        ys[k, 1:9, 1:9] = got[...]
        taps = [ys[k, dz : dz + 8, dx : dx + 8].reshape(1024, 128) for dz in range(3) for dx in range(3)]
        acc = dot(jnp.concatenate(taps, -1), w[:, pl.ds(2 * e, 1)].reshape(1152, 256))
        acc = acc.reshape(8, 8, 16, 256)
        one = pl.ds(e, 1)
        out[one, :, 0] = acc[None, :, 0]
        out[one, :, 7] = acc[None, :, 7]
        out[one, 0, 1:7] = acc[None, 0, 1:7] + eacc_z[one, 0]
        out[one, 1:7, 1:7] = acc[None, 1:7, 1:7] + eacc_i[one]
        out[one, 7, 1:7] = acc[None, 7, 1:7] + eacc_z[one, 1]


def fine_faces(odd, faces, w, eacc_i, eacc_z):
    return pl.pallas_call(
        fine_faces_kernel,
        out_shape=jax.ShapeDtypeStruct((2, 8, 8, 16, 256), F32),
        in_specs=[pl.BlockSpec(memory_space=pltpu.SMEM)] + [VMEM] * 5,
        out_specs=VMEM,
        scratch_shapes=[pltpu.VMEM((2, 10, 10, 16, 128), BF16)],
        compiler_params=params(20),
        cost_estimate=cost(2 * 2048 * 1152 * 256, 6 << 20),
        name="fine_faces",
    )(odd, *faces, w, eacc_i, eacc_z)


def fine_last_kernel(odd, zlo, zhi, xlo, xhi, w, b, facc, outm, epool, eacc, out, sums):
    emit = emitter(swap_rows(), out, b)
    out[:, 16:48] = outm[...]
    zero = jnp.zeros((1, 16, 128), BF16)
    for k, e in enumerate((odd[0], 1 - odd[0])):
        one = pl.ds(e, 1)
        acc = sums.at[k]
        acc[:, 1:7] = facc[one, :, 1:7][0]
        acc[:, 0] = facc[one, :, 0][0] + eacc[one, :, 0][0]
        acc[:, 7] = facc[one, :, 7][0] + eacc[one, :, 1][0]

        def side(cells, taps):
            cells = jnp.concatenate(cells, 0)
            left = jnp.concatenate([cells[t : t + 8].reshape(128, 128) for t in range(3)], -1)
            rows = jnp.concatenate([w[t, pl.ds(2 * e, 1)][0] for t in taps], 0)
            return dot(left, rows).reshape(8, 16, 256)

        c, z = 10 * k, 8 * k
        acc[0] += side([xlo[c : c + 1], zlo[z : z + 8], xhi[c : c + 1]], (0, 1, 2))
        acc[7] += side([xlo[c + 9 : c + 10], zhi[z : z + 8], xhi[c + 9 : c + 10]], (6, 7, 8))
        acc[:, 0] += side([zero, xlo[c + 1 : c + 9], zero], (0, 3, 6))
        acc[:, 7] += side([zero, xhi[c + 1 : c + 9], zero], (2, 5, 8))
        plane = acc[...].reshape(4, 2, 4, 2, 16, 256).max(axis=(1, 3))
        emit(3 * e, jnp.maximum(plane, epool[one][0]))


def fine_last(odd, strips, w, b, facc, sides):
    return pl.pallas_call(
        fine_last_kernel,
        out_shape=jax.ShapeDtypeStruct((16, 64, 256), BF16),
        in_specs=[pl.BlockSpec(memory_space=pltpu.SMEM)] + [VMEM] * 10,
        out_specs=VMEM,
        scratch_shapes=[pltpu.VMEM((2, 8, 8, 16, 256), F32)],
        compiler_params=params(20),
        cost_estimate=cost(2 * 1024 * 384 * 256, 6 << 20),
        name="fine_last",
    )(odd, *strips, w, b, facc, *sides)


def deep_first_kernel(got, pad, w, out, xs):
    for y in range(4):
        plane = got[:, y * 16 : y * 16 + 16].reshape(256, 256)
        xs[y] = dot(pad[...], plane).astype(BF16).reshape(6, 6, 16, 256)
    for first, size, dys in ((1, 2, (0, 1, 2)), (0, 1, (1, 2)), (3, 1, (0, 1))):
        taps = [
            xs[first + dy - 1 : first + dy - 1 + size, dz : dz + 4, dx : dx + 4].reshape(256 * size, 256)
            for dz in range(3)
            for dx in range(3)
            for dy in dys
        ]
        rows = [w[t, dy] for t in range(9) for dy in dys]
        acc = dot(jnp.concatenate(taps, -1), jnp.concatenate(rows, 0))
        out[first : first + size] = acc.reshape(size, 4, 4, 16, 256)


def deep_first(got, pad, w):
    return pl.pallas_call(
        deep_first_kernel,
        out_shape=jax.ShapeDtypeStruct((4, 4, 4, 16, 256), F32),
        in_specs=[VMEM] * 3,
        out_specs=VMEM,
        scratch_shapes=[pltpu.VMEM((4, 6, 6, 16, 256), BF16)],
        compiler_params=params(40),
        cost_estimate=cost(2 * 1024 * 6912 * 256, 6 << 20),
        name="deep_first",
    )(got, pad, w)


def deep_last_kernel(odd, got_a, got_b, pad, w, b, acc_in, out, ys, full, turned):
    p = swap_rows()
    for y in (1, 2):
        full[:, :, y] = leaky(acc_in[y] + b[...]).astype(BF16)
    for k, (got, e) in enumerate(((got_a, odd[0]), (got_b, 1 - odd[0]))):
        ys[k] = dot(pad[...], got[...].reshape(256, 256)).astype(BF16).reshape(6, 6, 16, 256)
        taps = [ys[k, dz : dz + 4, dx : dx + 4].reshape(256, 256) for dz in range(3) for dx in range(3)]
        acc = dot(jnp.concatenate(taps, -1), w[:, pl.ds(2 * e, 1)].reshape(2304, 256))
        acc = acc.reshape(4, 4, 16, 256) + acc_in[pl.ds(3 * e, 1)][0]
        full[:, :, pl.ds(3 * e, 1)] = leaky(acc + b[...]).astype(BF16)[:, :, None]
    planes = [dot(p, full[z].reshape(256, 256)).reshape(16, 16, 256) for z in range(4)]
    lane = lax.broadcasted_iota(jnp.int32, (128, 128), 1)
    for big in range(4):
        for z in (0, 2):
            rows = [planes[z + k][big * 4 : big * 4 + 4].reshape(64, 256) for k in (0, 1)]
            flipped = jnp.concatenate(rows, 0).T.reshape(8, 2, 16, 128)
            low = flipped[:, 0].reshape(128, 128)
            high = flipped[:, 1].reshape(128, 128)
            first = jnp.where(lane < 64, low, pltpu.roll(high, 64, 1))
            second = jnp.where(lane < 64, pltpu.roll(low, 64, 1), high)
            turned[big * 4 + z] = first.astype(BF16).reshape(8, 16, 128)
            turned[big * 4 + z + 1] = second.astype(BF16).reshape(8, 16, 128)
    for c in (0, 2, 4, 6):
        pair = [turned[:, c + k].reshape(256, 128) for k in (0, 1)]
        moved = dot(p, jnp.concatenate(pair, -1)).astype(BF16)
        for k in (0, 1):
            out[c + k] = moved[:, k * 128 : (k + 1) * 128]


def deep_last(odd, got_a, got_b, pad, w, b, acc):
    return pl.pallas_call(
        deep_last_kernel,
        out_shape=jax.ShapeDtypeStruct((8, 256, 128), BF16),
        in_specs=[pl.BlockSpec(memory_space=pltpu.SMEM)] + [VMEM] * 6,
        out_specs=VMEM,
        scratch_shapes=[
            pltpu.VMEM((2, 6, 6, 16, 256), BF16),
            pltpu.VMEM((4, 4, 4, 16, 256), BF16),
            pltpu.VMEM((16, 8, 16, 128), BF16),
        ],
        compiler_params=params(24),
        cost_estimate=cost(2 * 512 * 2304 * 256, 6 << 20),
        name="deep_last",
    )(odd, got_a, got_b, pad, w, b, acc)


def arrange_kernel(got, lanes, out):
    spread = dot(jnp.concatenate([got[c] for c in range(8)], -1), lanes[...]).astype(BF16)
    for h in range(2):
        for p in range(4):
            first = (h * 4 + p) * 128
            out[0, h * 16 : (h + 1) * 16, :, p * 128 : (p + 1) * 128] = spread[:, first : first + 128].reshape(
                16, 16, 128
            )


def arrange(got, lanes):
    return pl.pallas_call(
        arrange_kernel,
        out_shape=jax.ShapeDtypeStruct((1, 32, 16, 512), BF16),
        in_specs=[VMEM] * 2,
        out_specs=VMEM,
        compiler_params=params(16),
        cost_estimate=cost(2 * 256 * 1024 * 1024, 3 << 20),
        name="arrange",
    )(got, lanes)


def on_device(volume, fine_kernel, fine_bias, deep_kernel, deep_bias):
    odd = lax.axis_index("chan") % 2
    is_odd = odd == 1
    flag = odd.astype(jnp.int32).reshape(1)
    vol = volume.reshape(16, 8, 64, 128)

    def y_exchange(head, tail):
        got_a = swap_pairs(jnp.where(is_odd, tail, head), "chan", True)
        got_b = swap_pairs(jnp.where(is_odd, head, tail), "chan", False)
        return got_a, got_b

    tlo, thi, rest = turn_faces(vol)
    zlo, zhi = shift(thi, "sample", 1), shift(tlo, "sample", -1)
    block = turn_rest(rest, tlo, thi)
    got_a, got_b = y_exchange(block[:, :, 0:16], block[:, :, 112:128])
    w = fine_kernel.reshape(3456, 256)
    w9 = fine_kernel.reshape(9, 3, 128, 256)
    b = fine_bias.reshape(1, 256)
    mid_i, epool_i, eacc_i = fine_inner(block, w)

    def x_face(x):
        return jnp.concatenate([zlo[x : x + 1], block[:, x], zhi[x : x + 1]], 0)

    xlo, xhi = shift(x_face(7), "space", 1), shift(x_face(0), "space", -1)
    mid_z, epool_z, eacc_z = fine_ends(zlo, block, zhi, w)
    rzlo = shift(jnp.concatenate([got_a[7], got_b[7]], 0), "sample", 1)
    rzhi = shift(jnp.concatenate([got_a[0], got_b[0]], 0), "sample", -1)
    facc = fine_faces(flag, (got_a, got_b), w9, eacc_i, eacc_z)
    def rim(x):
        return jnp.concatenate(
            [rzlo[x : x + 1], got_a[:, x], rzhi[x : x + 1], rzlo[8 + x : 9 + x], got_b[:, x], rzhi[8 + x : 9 + x]], 0
        )

    rxlo, rxhi = shift(rim(7), "space", 1), shift(rim(0), "space", -1)
    sides = fine_sides(xlo, xhi, zlo, block, zhi, w, b, mid_i, epool_i, mid_z, epool_z)
    send = fine_last(flag, (rzlo, rzhi, rxlo, rxhi), w9, b, facc, sides)
    got = lax.all_to_all(send, ("sample", "space"), split_axis=0, concat_axis=0, tiled=True)

    got_a, got_b = y_exchange(got[:, 0:16], got[:, 48:64])
    pad = jnp.asarray(pad_matrix(), BF16)
    dw = deep_kernel.reshape(9, 3, 256, 256)
    acc = deep_first(got, pad, dw)
    send = deep_last(flag, got_a, got_b, pad, dw, deep_bias.reshape(1, 256), acc)
    got = lax.all_to_all(send, "chan", split_axis=0, concat_axis=0, tiled=True)
    return arrange(got, jnp.asarray(lane_matrix(), BF16))


def solution(mesh):
    placed = (P(None, "sample", "space", "chan", None), P(), P(), P(), P())
    return jax.shard_map(
        on_device,
        mesh=mesh,
        in_specs=placed,
        out_specs=P(("sample", "space"), "chan", None, None),
        check_vma=False,
    )
```

```python
import jax
import jax.numpy as jnp
import numpy as np
from jax import lax
from jax.experimental import pallas as pl
from jax.experimental.pallas import tpu as pltpu
from jax.sharding import PartitionSpec as P

MIB = 1 << 20
FINE_MIB = 36
BF16 = jnp.bfloat16
F32 = jnp.float32
VMEM = pl.BlockSpec(memory_space=pltpu.VMEM)
ANY = pl.BlockSpec(memory_space=pl.ANY)


def lane_matrix():
    src = np.arange(1024).reshape(8, 8, 4, 4)
    dst = src.transpose(1, 2, 0, 3).reshape(-1)
    m = np.zeros((1024, 1024), np.float32)
    m[dst, np.arange(1024)] = 1
    return m


def pad_matrix():
    m = np.zeros((6, 6, 16, 256), np.float32)
    for i in range(6):
        for j in range(6):
            for big in range(4):
                for p in range(4):
                    z, x = (4 * big + i - 1) % 16, (4 * p + j - 1) % 16
                    m[i, j, big * 4 + p, ((z // 4) * 4 + x // 4) * 16 + (z % 4) * 4 + x % 4] = 1
    return m.reshape(576, 256)


def params(mib):
    return pltpu.CompilerParams(vmem_limit_bytes=mib * MIB)


def cost(flops, moved):
    return pl.CostEstimate(flops=flops, bytes_accessed=moved, transcendentals=0)


def leaky(value):
    return jnp.where(value >= 0, value, 0.3 * value)


def dot(a, b):
    return jnp.dot(a, b, preferred_element_type=F32)


def swap_rows():
    i = lax.broadcasted_iota(jnp.int32, (256, 256), 0)
    j = lax.broadcasted_iota(jnp.int32, (256, 256), 1)
    hit = ((i >> 4) == (j & 15)) & ((i & 15) == (j >> 4))
    return jnp.where(hit, 1.0, 0.0).astype(BF16)


def shift(value, axis, step):
    n = lax.axis_size(axis)
    return lax.ppermute(value, axis, [(i, (i + step) % n) for i in range(n)])


def swap_pairs(value, axis, odd):
    n = lax.axis_size(axis)
    pairs = []
    for i in range(n):
        up = (i % 2 == 1) if odd else (i % 2 == 0)
        pairs.append((i, (i + 1) % n if up else (i - 1) % n))
    return lax.ppermute(value, axis, pairs)


def turn(p, slab, put):
    for j in (0, 2):
        halves = [slab[:, (j + k) * 16 : (j + k) * 16 + 16].reshape(256, 128) for k in (0, 1)]
        turned = dot(p, jnp.concatenate(halves, -1)).astype(BF16)
        for k in (0, 1):
            put(2 * (j + k), turned[:, k * 128 : (k + 1) * 128].reshape(2, 128, 128))


def turn_all_kernel(vol, block, lo, hi):
    p = swap_rows()
    for z in (0, 7, 1, 2, 3, 4, 5, 6):

        def put(x, value, z=z):
            block[z, x : x + 2] = value
            if z == 0:
                lo[x : x + 2] = value
            if z == 7:
                hi[x : x + 2] = value

        turn(p, vol[:, z], put)


def turn_all(vol):
    face = jax.ShapeDtypeStruct((8, 128, 128), BF16)
    return pl.pallas_call(
        turn_all_kernel,
        out_shape=[jax.ShapeDtypeStruct((8, 8, 128, 128), BF16), face, face],
        in_specs=[VMEM],
        out_specs=[VMEM] * 3,
        compiler_params=params(12),
        cost_estimate=cost(2 * 8192 * 256 * 256, 4 << 20),
        name="turn_all",
    )(vol)


def pool_inner(acc, z, mid, epool):
    parts = [acc[:, 0:1], jnp.maximum(acc[:, 1:2], acc[:, 2:3]), jnp.maximum(acc[:, 3:4], acc[:, 4:5]), acc[:, 5:6]]
    acc = jnp.concatenate(parts, 1)
    for i in range(acc.shape[0]):
        epool[0, z[i]] = acc[i, :, 0]
        epool[1, z[i]] = acc[i, :, 5]
        for y in (0, 1):
            mid[y, z[i]] = jnp.maximum(acc[i, :, 1 + 2 * y], acc[i, :, 2 + 2 * y])


def tap_rows(planes, dys, first, count):
    return [
        planes(dz, dx, slice((first + dy) * 16, (first + dy + count) * 16))
        for dz in range(3)
        for dx in range(3)
        for dy in dys
    ]


def inner_cells(planes, w):
    taps = [t.reshape(1152, 128) for t in tap_rows(planes, (0, 1, 2), 0, 6)]
    return dot(jnp.concatenate(taps, -1), w[...]).reshape(2, 6, 6, 16, 256)


def edge_rows(w, e):
    first = 128 * (1 - e)
    return jnp.concatenate([w[t * 384 + first : t * 384 + first + 256] for t in range(9)], 0)


def edge_cells(planes, cells, w, eacc):
    for e in (0, 1):
        taps = [t.reshape(cells * 16, 128) for t in tap_rows(planes, (0, 1), 6 * e, 1)]
        acc = dot(jnp.concatenate(taps, -1), edge_rows(w, e))
        eacc[e] = acc.reshape(eacc.shape[1:])


def pooled_f32(pairs):
    return jax.ShapeDtypeStruct((2, pairs, 4, 16, 256), F32)


def fine_call(kernel, outs, name, cells, operands, moved=5 << 20):
    return pl.pallas_call(
        kernel,
        out_shape=outs,
        in_specs=[VMEM] * len(operands),
        out_specs=[VMEM] * len(outs),
        compiler_params=params(FINE_MIB),
        cost_estimate=cost(cells * 16 * 3456 * 256 * 2, moved),
        name=name,
    )(*operands)


def fine_inner_kernel(block, w, mid, epool, eacc):
    def ends(dz, dx, rows):
        return jnp.concatenate([block[z + dz : z + dz + 1, dx : 6 + dx, rows] for z in (0, 5)], 0)

    pool_inner(inner_cells(ends, w), (0, 3), mid, epool)
    for z in (1, 2):

        def pair(dz, dx, rows, z=z):
            return block[2 * z - 1 + dz : 2 * z + 1 + dz, dx : 6 + dx, rows]

        acc = inner_cells(pair, w)
        pool_inner(jnp.maximum(acc[0:1], acc[1:2]), (z,), mid, epool)

    def planes(dz, dx, rows):
        return block[dz : 6 + dz, dx : 6 + dx, rows]

    edge_cells(planes, 36, w, eacc)


def fine_inner(block, w):
    outs = [pooled_f32(4), pooled_f32(4), jax.ShapeDtypeStruct((2, 6, 6, 16, 256), F32)]
    return fine_call(fine_inner_kernel, outs, "fine_inner", 270, (block, w))


def fine_ends_kernel(zlo, block, zhi, w, mid, epool, eacc):
    def planes(dz, dx, rows):
        low = zlo[dx : 6 + dx, rows] if dz == 0 else block[dz - 1, dx : 6 + dx, rows]
        high = zhi[dx : 6 + dx, rows] if dz == 2 else block[6 + dz, dx : 6 + dx, rows]
        return jnp.stack([low, high], 0)

    pool_inner(inner_cells(planes, w), (0, 1), mid, epool)
    edge_cells(planes, 12, w, eacc)


def fine_ends(zlo, block, zhi, w):
    outs = [pooled_f32(2), pooled_f32(2), jax.ShapeDtypeStruct((2, 2, 6, 16, 256), F32)]
    return fine_call(fine_ends_kernel, outs, "fine_ends", 90, (zlo, block, zhi, w))


def emitter(p, out, b):
    def emit(y, plane):
        cells = leaky(plane + b[...]).astype(BF16).reshape(256, 256)
        out[:, pl.ds(y * 16 if isinstance(y, int) else pl.multiple_of(y * 16, 16), 16)] = (
            dot(p, cells).astype(BF16).reshape(16, 16, 256)
        )

    return emit


def fine_sides_kernel(
    xlo, xhi, zlo, block, zhi, w, b, mid_i, epool_i, mid_z, epool_z, outm, epool, eacc
):
    def column(x, dz, rows):
        if dz == 0:
            return jnp.concatenate([zlo[x : x + 1, rows], block[0:7, x, rows]], 0)
        if dz == 1:
            return block[0:8, x, rows]
        return jnp.concatenate([block[1:8, x, rows], zhi[x : x + 1, rows]], 0)

    def planes(dz, dx, rows):
        first = xlo[dz : dz + 8, rows] if dx == 0 else column(dx - 1, dz, rows)
        second = xhi[dz : dz + 8, rows] if dx == 2 else column(6 + dx, dz, rows)
        return jnp.stack([first, second], 1)

    taps = [t.reshape(1536, 128) for t in tap_rows(planes, (0, 1, 2), 0, 6)]
    acc = dot(jnp.concatenate(taps, -1), w[...]).reshape(4, 2, 2, 6, 16, 256).max(axis=1)

    def whole(sides, inner, ends):
        low = jnp.maximum(inner[0:1], ends[0:1])
        high = jnp.maximum(inner[3:4], ends[1:2])
        plane = jnp.concatenate([low, inner[1:3], high], 0)
        first = jnp.maximum(plane[:, 0:1], sides[:, 0:1])
        last = jnp.maximum(plane[:, 3:4], sides[:, 1:2])
        return jnp.concatenate([first, plane[:, 1:3], last], 1)

    for e in (0, 1):
        epool[e] = whole(acc[:, :, 5 * e], epool_i[e], epool_z[e])
    emit = emitter(swap_rows(), outm, b)
    for y in (0, 1):
        inner = jnp.maximum(acc[:, :, 1 + 2 * y], acc[:, :, 2 + 2 * y])
        emit(y, whole(inner, mid_i[y], mid_z[y]))
    edge_cells(planes, 16, w, eacc)


def fine_sides(*operands):
    outs = [
        jax.ShapeDtypeStruct((16, 32, 256), BF16),
        pooled_f32(4),
        jax.ShapeDtypeStruct((2, 8, 2, 16, 256), F32),
    ]
    return fine_call(fine_sides_kernel, outs, "fine_sides", 124, operands)


def fine_faces_kernel(odd, got_a, got_b, w, eacc_i, eacc_z, out, ys):
    ys[...] = jnp.zeros_like(ys)
    for k, (got, e) in enumerate(((got_a, odd[0]), (got_b, 1 - odd[0]))):
        ys[k, 1:9, 1:9] = got[...]
        taps = [ys[k, dz : dz + 8, dx : dx + 8].reshape(1024, 128) for dz in range(3) for dx in range(3)]
        acc = dot(jnp.concatenate(taps, -1), w[:, pl.ds(2 * e, 1)].reshape(1152, 256))
        acc = acc.reshape(8, 8, 16, 256)
        one = pl.ds(e, 1)
        out[one, :, 0] = acc[None, :, 0]
        out[one, :, 7] = acc[None, :, 7]
        out[one, 0, 1:7] = acc[None, 0, 1:7] + eacc_z[one, 0]
        out[one, 1:7, 1:7] = acc[None, 1:7, 1:7] + eacc_i[one]
        out[one, 7, 1:7] = acc[None, 7, 1:7] + eacc_z[one, 1]


def fine_faces(odd, faces, w, eacc_i, eacc_z):
    return pl.pallas_call(
        fine_faces_kernel,
        out_shape=jax.ShapeDtypeStruct((2, 8, 8, 16, 256), F32),
        in_specs=[pl.BlockSpec(memory_space=pltpu.SMEM)] + [VMEM] * 5,
        out_specs=VMEM,
        scratch_shapes=[pltpu.VMEM((2, 10, 10, 16, 128), BF16)],
        compiler_params=params(20),
        cost_estimate=cost(2 * 2048 * 1152 * 256, 6 << 20),
        name="fine_faces",
    )(odd, *faces, w, eacc_i, eacc_z)


def fine_last_kernel(odd, zlo, zhi, xlo, xhi, w, b, facc, outm, epool, eacc, out, sums):
    emit = emitter(swap_rows(), out, b)
    out[:, 16:48] = outm[...]
    zero = jnp.zeros((1, 16, 128), BF16)
    for k, e in enumerate((odd[0], 1 - odd[0])):
        one = pl.ds(e, 1)
        acc = sums.at[k]
        acc[:, 1:7] = facc[one, :, 1:7][0]
        acc[:, 0] = facc[one, :, 0][0] + eacc[one, :, 0][0]
        acc[:, 7] = facc[one, :, 7][0] + eacc[one, :, 1][0]

        def side(cells, taps):
            cells = jnp.concatenate(cells, 0)
            left = jnp.concatenate([cells[t : t + 8].reshape(128, 128) for t in range(3)], -1)
            rows = jnp.concatenate([w[t, pl.ds(2 * e, 1)][0] for t in taps], 0)
            return dot(left, rows).reshape(8, 16, 256)

        c, z = 10 * k, 8 * k
        acc[0] += side([xlo[c : c + 1], zlo[z : z + 8], xhi[c : c + 1]], (0, 1, 2))
        acc[7] += side([xlo[c + 9 : c + 10], zhi[z : z + 8], xhi[c + 9 : c + 10]], (6, 7, 8))
        acc[:, 0] += side([zero, xlo[c + 1 : c + 9], zero], (0, 3, 6))
        acc[:, 7] += side([zero, xhi[c + 1 : c + 9], zero], (2, 5, 8))
        plane = acc[...].reshape(4, 2, 4, 2, 16, 256).max(axis=(1, 3))
        emit(3 * e, jnp.maximum(plane, epool[one][0]))


def fine_last(odd, strips, w, b, facc, sides):
    return pl.pallas_call(
        fine_last_kernel,
        out_shape=jax.ShapeDtypeStruct((16, 64, 256), BF16),
        in_specs=[pl.BlockSpec(memory_space=pltpu.SMEM)] + [VMEM] * 10,
        out_specs=VMEM,
        scratch_shapes=[pltpu.VMEM((2, 8, 8, 16, 256), F32)],
        compiler_params=params(20),
        cost_estimate=cost(2 * 1024 * 384 * 256, 6 << 20),
        name="fine_last",
    )(odd, *strips, w, b, facc, *sides)


def deep_first_kernel(got, pad, w, out, xs):
    for y in range(4):
        plane = got[:, y * 16 : y * 16 + 16].reshape(256, 256)
        xs[y] = dot(pad[...], plane).astype(BF16).reshape(6, 6, 16, 256)
    for first, size, dys in ((1, 2, (0, 1, 2)), (0, 1, (1, 2)), (3, 1, (0, 1))):
        taps = [
            xs[first + dy - 1 : first + dy - 1 + size, dz : dz + 4, dx : dx + 4].reshape(256 * size, 256)
            for dz in range(3)
            for dx in range(3)
            for dy in dys
        ]
        rows = [w[t, dy] for t in range(9) for dy in dys]
        acc = dot(jnp.concatenate(taps, -1), jnp.concatenate(rows, 0))
        out[first : first + size] = acc.reshape(size, 4, 4, 16, 256)


def deep_first(got, pad, w):
    return pl.pallas_call(
        deep_first_kernel,
        out_shape=jax.ShapeDtypeStruct((4, 4, 4, 16, 256), F32),
        in_specs=[VMEM] * 3,
        out_specs=VMEM,
        scratch_shapes=[pltpu.VMEM((4, 6, 6, 16, 256), BF16)],
        compiler_params=params(40),
        cost_estimate=cost(2 * 1024 * 6912 * 256, 6 << 20),
        name="deep_first",
    )(got, pad, w)


def deep_last_kernel(odd, got_a, got_b, pad, w, b, acc_in, out, ys, full, turned):
    p = swap_rows()
    for y in (1, 2):
        full[:, :, y] = leaky(acc_in[y] + b[...]).astype(BF16)
    for k, (got, e) in enumerate(((got_a, odd[0]), (got_b, 1 - odd[0]))):
        ys[k] = dot(pad[...], got[...].reshape(256, 256)).astype(BF16).reshape(6, 6, 16, 256)
        taps = [ys[k, dz : dz + 4, dx : dx + 4].reshape(256, 256) for dz in range(3) for dx in range(3)]
        acc = dot(jnp.concatenate(taps, -1), w[:, pl.ds(2 * e, 1)].reshape(2304, 256))
        acc = acc.reshape(4, 4, 16, 256) + acc_in[pl.ds(3 * e, 1)][0]
        full[:, :, pl.ds(3 * e, 1)] = leaky(acc + b[...]).astype(BF16)[:, :, None]
    planes = [dot(p, full[z].reshape(256, 256)).reshape(16, 16, 256) for z in range(4)]
    lane = lax.broadcasted_iota(jnp.int32, (128, 128), 1)
    for big in range(4):
        for z in (0, 2):
            rows = [planes[z + k][big * 4 : big * 4 + 4].reshape(64, 256) for k in (0, 1)]
            flipped = jnp.concatenate(rows, 0).T.reshape(8, 2, 16, 128)
            low = flipped[:, 0].reshape(128, 128)
            high = flipped[:, 1].reshape(128, 128)
            first = jnp.where(lane < 64, low, pltpu.roll(high, 64, 1))
            second = jnp.where(lane < 64, pltpu.roll(low, 64, 1), high)
            turned[big * 4 + z] = first.astype(BF16).reshape(8, 16, 128)
            turned[big * 4 + z + 1] = second.astype(BF16).reshape(8, 16, 128)
    for c in (0, 2, 4, 6):
        pair = [turned[:, c + k].reshape(256, 128) for k in (0, 1)]
        moved = dot(p, jnp.concatenate(pair, -1)).astype(BF16)
        for k in (0, 1):
            out[c + k] = moved[:, k * 128 : (k + 1) * 128]


def deep_last(odd, got_a, got_b, pad, w, b, acc):
    return pl.pallas_call(
        deep_last_kernel,
        out_shape=jax.ShapeDtypeStruct((8, 256, 128), BF16),
        in_specs=[pl.BlockSpec(memory_space=pltpu.SMEM)] + [VMEM] * 6,
        out_specs=VMEM,
        scratch_shapes=[
            pltpu.VMEM((2, 6, 6, 16, 256), BF16),
            pltpu.VMEM((4, 4, 4, 16, 256), BF16),
            pltpu.VMEM((16, 8, 16, 128), BF16),
        ],
        compiler_params=params(24),
        cost_estimate=cost(2 * 512 * 2304 * 256, 6 << 20),
        name="deep_last",
    )(odd, got_a, got_b, pad, w, b, acc)


def arrange_kernel(got, lanes, out):
    spread = dot(jnp.concatenate([got[c] for c in range(8)], -1), lanes[...]).astype(BF16)
    for h in range(2):
        for p in range(4):
            first = (h * 4 + p) * 128
            out[0, h * 16 : (h + 1) * 16, :, p * 128 : (p + 1) * 128] = spread[:, first : first + 128].reshape(
                16, 16, 128
            )


def arrange(got, lanes):
    return pl.pallas_call(
        arrange_kernel,
        out_shape=jax.ShapeDtypeStruct((1, 32, 16, 512), BF16),
        in_specs=[VMEM] * 2,
        out_specs=VMEM,
        compiler_params=params(16),
        cost_estimate=cost(2 * 256 * 1024 * 1024, 3 << 20),
        name="arrange",
    )(got, lanes)


def on_device(volume, fine_kernel, fine_bias, deep_kernel, deep_bias):
    odd = lax.axis_index("chan") % 2
    is_odd = odd == 1
    flag = odd.astype(jnp.int32).reshape(1)
    vol = volume.reshape(16, 8, 64, 128)

    def y_exchange(head, tail):
        got_a = swap_pairs(jnp.where(is_odd, tail, head), "chan", True)
        got_b = swap_pairs(jnp.where(is_odd, head, tail), "chan", False)
        return got_a, got_b

    block, tlo, thi = turn_all(vol)
    zlo, zhi = shift(thi, "sample", 1), shift(tlo, "sample", -1)
    got_a, got_b = y_exchange(block[:, :, 0:16], block[:, :, 112:128])
    w = fine_kernel.reshape(3456, 256)
    w9 = fine_kernel.reshape(9, 3, 128, 256)
    b = fine_bias.reshape(1, 256)
    mid_i, epool_i, eacc_i = fine_inner(block, w)

    def x_face(x):
        return jnp.concatenate([zlo[x : x + 1], block[:, x], zhi[x : x + 1]], 0)

    xlo, xhi = shift(x_face(7), "space", 1), shift(x_face(0), "space", -1)
    mid_z, epool_z, eacc_z = fine_ends(zlo, block, zhi, w)
    rzlo = shift(jnp.concatenate([got_a[7], got_b[7]], 0), "sample", 1)
    rzhi = shift(jnp.concatenate([got_a[0], got_b[0]], 0), "sample", -1)
    facc = fine_faces(flag, (got_a, got_b), w9, eacc_i, eacc_z)
    def rim(x):
        return jnp.concatenate(
            [rzlo[x : x + 1], got_a[:, x], rzhi[x : x + 1], rzlo[8 + x : 9 + x], got_b[:, x], rzhi[8 + x : 9 + x]], 0
        )

    rxlo, rxhi = shift(rim(7), "space", 1), shift(rim(0), "space", -1)
    sides = fine_sides(xlo, xhi, zlo, block, zhi, w, b, mid_i, epool_i, mid_z, epool_z)
    send = fine_last(flag, (rzlo, rzhi, rxlo, rxhi), w9, b, facc, sides)
    got = lax.all_to_all(send, ("sample", "space"), split_axis=0, concat_axis=0, tiled=True)

    got_a, got_b = y_exchange(got[:, 0:16], got[:, 48:64])
    pad = jnp.asarray(pad_matrix(), BF16)
    dw = deep_kernel.reshape(9, 3, 256, 256)
    acc = deep_first(got, pad, dw)
    send = deep_last(flag, got_a, got_b, pad, dw, deep_bias.reshape(1, 256), acc)
    got = lax.all_to_all(send, "chan", split_axis=0, concat_axis=0, tiled=True)
    return arrange(got, jnp.asarray(lane_matrix(), BF16))


def solution(mesh):
    placed = (P(None, "sample", "space", "chan", None), P(), P(), P(), P())
    return jax.shard_map(
        on_device,
        mesh=mesh,
        in_specs=placed,
        out_specs=P(("sample", "space"), "chan", None, None),
        check_vma=False,
    )
```

```python
import jax
import jax.numpy as jnp
import numpy as np
from jax import lax
from jax.experimental import pallas as pl
from jax.experimental.pallas import tpu as pltpu
from jax.sharding import PartitionSpec as P

MIB = 1 << 20
FINE_MIB = 36
BF16 = jnp.bfloat16
F32 = jnp.float32
VMEM = pl.BlockSpec(memory_space=pltpu.VMEM)
ANY = pl.BlockSpec(memory_space=pl.ANY)


def lane_matrix():
    src = np.arange(512).reshape(8, 4, 4, 4)
    dst = src.transpose(1, 2, 0, 3).reshape(-1)
    m = np.zeros((512, 512), np.float32)
    m[dst, np.arange(512)] = 1
    return m


def pad_matrix():
    m = np.zeros((6, 6, 16, 256), np.float32)
    for i in range(6):
        for j in range(6):
            for big in range(4):
                for p in range(4):
                    z, x = (4 * big + i - 1) % 16, (4 * p + j - 1) % 16
                    m[i, j, big * 4 + p, ((z // 4) * 4 + x // 4) * 16 + (z % 4) * 4 + x % 4] = 1
    return m.reshape(576, 256)


def params(mib):
    return pltpu.CompilerParams(vmem_limit_bytes=mib * MIB)


def cost(flops, moved):
    return pl.CostEstimate(flops=flops, bytes_accessed=moved, transcendentals=0)


def leaky(value):
    return jnp.where(value >= 0, value, 0.3 * value)


def dot(a, b):
    return jnp.dot(a, b, preferred_element_type=F32)


def swap_rows():
    i = lax.broadcasted_iota(jnp.int32, (256, 256), 0)
    j = lax.broadcasted_iota(jnp.int32, (256, 256), 1)
    hit = ((i >> 4) == (j & 15)) & ((i & 15) == (j >> 4))
    return jnp.where(hit, 1.0, 0.0).astype(BF16)


def shift(value, axis, step):
    n = lax.axis_size(axis)
    return lax.ppermute(value, axis, [(i, (i + step) % n) for i in range(n)])


def swap_pairs(value, axis, odd):
    n = lax.axis_size(axis)
    pairs = []
    for i in range(n):
        up = (i % 2 == 1) if odd else (i % 2 == 0)
        pairs.append((i, (i + 1) % n if up else (i - 1) % n))
    return lax.ppermute(value, axis, pairs)


def turn(p, slab, put):
    for j in (0, 2):
        halves = [slab[:, (j + k) * 16 : (j + k) * 16 + 16].reshape(256, 128) for k in (0, 1)]
        turned = dot(p, jnp.concatenate(halves, -1)).astype(BF16)
        for k in (0, 1):
            put(2 * (j + k), turned[:, k * 128 : (k + 1) * 128].reshape(2, 128, 128))


def turn_all_kernel(vol, block, lo, hi):
    p = swap_rows()
    for z in (0, 7, 1, 2, 3, 4, 5, 6):

        def put(x, value, z=z):
            block[z, x : x + 2] = value
            if z == 0:
                lo[x : x + 2] = value
            if z == 7:
                hi[x : x + 2] = value

        turn(p, vol[:, z], put)


def turn_all(vol):
    face = jax.ShapeDtypeStruct((8, 128, 128), BF16)
    return pl.pallas_call(
        turn_all_kernel,
        out_shape=[jax.ShapeDtypeStruct((8, 8, 128, 128), BF16), face, face],
        in_specs=[VMEM],
        out_specs=[VMEM] * 3,
        compiler_params=params(12),
        cost_estimate=cost(2 * 8192 * 256 * 256, 4 << 20),
        name="turn_all",
    )(vol)


def pool_inner(acc, z, mid, epool):
    parts = [acc[:, 0:1], jnp.maximum(acc[:, 1:2], acc[:, 2:3]), jnp.maximum(acc[:, 3:4], acc[:, 4:5]), acc[:, 5:6]]
    acc = jnp.concatenate(parts, 1)
    for i in range(acc.shape[0]):
        epool[0, z[i]] = acc[i, :, 0]
        epool[1, z[i]] = acc[i, :, 5]
        for y in (0, 1):
            mid[y, z[i]] = jnp.maximum(acc[i, :, 1 + 2 * y], acc[i, :, 2 + 2 * y])


def tap_rows(planes, dys, first, count):
    return [
        planes(dz, dx, slice((first + dy) * 16, (first + dy + count) * 16))
        for dz in range(3)
        for dx in range(3)
        for dy in dys
    ]


def inner_cells(planes, w):
    taps = [t.reshape(1152, 128) for t in tap_rows(planes, (0, 1, 2), 0, 6)]
    return dot(jnp.concatenate(taps, -1), w[...]).reshape(2, 6, 6, 16, 256)


def edge_rows(w, e):
    first = 128 * (1 - e)
    return jnp.concatenate([w[t * 384 + first : t * 384 + first + 256] for t in range(9)], 0)


def edge_cells(planes, cells, w, eacc):
    for e in (0, 1):
        taps = [t.reshape(cells * 16, 128) for t in tap_rows(planes, (0, 1), 6 * e, 1)]
        acc = dot(jnp.concatenate(taps, -1), edge_rows(w, e))
        eacc[e] = acc.reshape(eacc.shape[1:])


def pooled_f32(pairs):
    return jax.ShapeDtypeStruct((2, pairs, 4, 16, 256), F32)


def fine_call(kernel, outs, name, cells, operands, moved=5 << 20):
    return pl.pallas_call(
        kernel,
        out_shape=outs,
        in_specs=[VMEM] * len(operands),
        out_specs=[VMEM] * len(outs),
        compiler_params=params(FINE_MIB),
        cost_estimate=cost(cells * 16 * 3456 * 256 * 2, moved),
        name=name,
    )(*operands)


def fine_inner_kernel(block, w, mid, epool, eacc):
    def ends(dz, dx, rows):
        return jnp.concatenate([block[z + dz : z + dz + 1, dx : 6 + dx, rows] for z in (0, 5)], 0)

    pool_inner(inner_cells(ends, w), (0, 3), mid, epool)
    for z in (1, 2):

        def pair(dz, dx, rows, z=z):
            return block[2 * z - 1 + dz : 2 * z + 1 + dz, dx : 6 + dx, rows]

        acc = inner_cells(pair, w)
        pool_inner(jnp.maximum(acc[0:1], acc[1:2]), (z,), mid, epool)

    def planes(dz, dx, rows):
        return block[dz : 6 + dz, dx : 6 + dx, rows]

    edge_cells(planes, 36, w, eacc)


def fine_inner(block, w):
    outs = [pooled_f32(4), pooled_f32(4), jax.ShapeDtypeStruct((2, 6, 6, 16, 256), F32)]
    return fine_call(fine_inner_kernel, outs, "fine_inner", 270, (block, w))


def fine_ends_kernel(zlo, block, zhi, w, mid, epool, eacc):
    def planes(dz, dx, rows):
        low = zlo[dx : 6 + dx, rows] if dz == 0 else block[dz - 1, dx : 6 + dx, rows]
        high = zhi[dx : 6 + dx, rows] if dz == 2 else block[6 + dz, dx : 6 + dx, rows]
        return jnp.stack([low, high], 0)

    pool_inner(inner_cells(planes, w), (0, 1), mid, epool)
    edge_cells(planes, 12, w, eacc)


def fine_ends(zlo, block, zhi, w):
    outs = [pooled_f32(2), pooled_f32(2), jax.ShapeDtypeStruct((2, 2, 6, 16, 256), F32)]
    return fine_call(fine_ends_kernel, outs, "fine_ends", 90, (zlo, block, zhi, w))


def emitter(p, out, b):
    def emit(y, plane):
        cells = leaky(plane + b[...]).astype(BF16).reshape(256, 256)
        out[:, pl.ds(y * 16 if isinstance(y, int) else pl.multiple_of(y * 16, 16), 16)] = (
            dot(p, cells).astype(BF16).reshape(16, 16, 256)
        )

    return emit


def fine_sides_kernel(
    xlo, xhi, zlo, block, zhi, w, b, mid_i, epool_i, mid_z, epool_z, outm, epool, eacc
):
    def column(x, dz, rows):
        if dz == 0:
            return jnp.concatenate([zlo[x : x + 1, rows], block[0:7, x, rows]], 0)
        if dz == 1:
            return block[0:8, x, rows]
        return jnp.concatenate([block[1:8, x, rows], zhi[x : x + 1, rows]], 0)

    def planes(dz, dx, rows):
        first = xlo[dz : dz + 8, rows] if dx == 0 else column(dx - 1, dz, rows)
        second = xhi[dz : dz + 8, rows] if dx == 2 else column(6 + dx, dz, rows)
        return jnp.stack([first, second], 1)

    taps = [t.reshape(1536, 128) for t in tap_rows(planes, (0, 1, 2), 0, 6)]
    acc = dot(jnp.concatenate(taps, -1), w[...]).reshape(4, 2, 2, 6, 16, 256).max(axis=1)

    def whole(sides, inner, ends):
        low = jnp.maximum(inner[0:1], ends[0:1])
        high = jnp.maximum(inner[3:4], ends[1:2])
        plane = jnp.concatenate([low, inner[1:3], high], 0)
        first = jnp.maximum(plane[:, 0:1], sides[:, 0:1])
        last = jnp.maximum(plane[:, 3:4], sides[:, 1:2])
        return jnp.concatenate([first, plane[:, 1:3], last], 1)

    for e in (0, 1):
        epool[e] = whole(acc[:, :, 5 * e], epool_i[e], epool_z[e])
    emit = emitter(swap_rows(), outm, b)
    for y in (0, 1):
        inner = jnp.maximum(acc[:, :, 1 + 2 * y], acc[:, :, 2 + 2 * y])
        emit(y, whole(inner, mid_i[y], mid_z[y]))
    edge_cells(planes, 16, w, eacc)


def fine_sides(*operands):
    outs = [
        jax.ShapeDtypeStruct((16, 32, 256), BF16),
        pooled_f32(4),
        jax.ShapeDtypeStruct((2, 8, 2, 16, 256), F32),
    ]
    return fine_call(fine_sides_kernel, outs, "fine_sides", 124, operands)


def fine_faces_kernel(odd, got_a, got_b, w, eacc_i, eacc_z, out, ys):
    ys[...] = jnp.zeros_like(ys)
    for k, (got, e) in enumerate(((got_a, odd[0]), (got_b, 1 - odd[0]))):
        ys[k, 1:9, 1:9] = got[...]
        taps = [ys[k, dz : dz + 8, dx : dx + 8].reshape(1024, 128) for dz in range(3) for dx in range(3)]
        acc = dot(jnp.concatenate(taps, -1), w[:, pl.ds(2 * e, 1)].reshape(1152, 256))
        acc = acc.reshape(8, 8, 16, 256)
        one = pl.ds(e, 1)
        out[one, :, 0] = acc[None, :, 0]
        out[one, :, 7] = acc[None, :, 7]
        out[one, 0, 1:7] = acc[None, 0, 1:7] + eacc_z[one, 0]
        out[one, 1:7, 1:7] = acc[None, 1:7, 1:7] + eacc_i[one]
        out[one, 7, 1:7] = acc[None, 7, 1:7] + eacc_z[one, 1]


def fine_faces(odd, faces, w, eacc_i, eacc_z):
    return pl.pallas_call(
        fine_faces_kernel,
        out_shape=jax.ShapeDtypeStruct((2, 8, 8, 16, 256), F32),
        in_specs=[pl.BlockSpec(memory_space=pltpu.SMEM)] + [VMEM] * 5,
        out_specs=VMEM,
        scratch_shapes=[pltpu.VMEM((2, 10, 10, 16, 128), BF16)],
        compiler_params=params(20),
        cost_estimate=cost(2 * 2048 * 1152 * 256, 6 << 20),
        name="fine_faces",
    )(odd, *faces, w, eacc_i, eacc_z)


def fine_last_kernel(odd, zlo, zhi, xlo, xhi, w, b, facc, outm, epool, eacc, out, sums):
    emit = emitter(swap_rows(), out, b)
    out[:, 16:48] = outm[...]
    zero = jnp.zeros((1, 16, 128), BF16)
    for k, e in enumerate((odd[0], 1 - odd[0])):
        one = pl.ds(e, 1)
        acc = sums.at[k]
        acc[:, 1:7] = facc[one, :, 1:7][0]
        acc[:, 0] = facc[one, :, 0][0] + eacc[one, :, 0][0]
        acc[:, 7] = facc[one, :, 7][0] + eacc[one, :, 1][0]

        def side(cells, taps):
            cells = jnp.concatenate(cells, 0)
            left = jnp.concatenate([cells[t : t + 8].reshape(128, 128) for t in range(3)], -1)
            rows = jnp.concatenate([w[t, pl.ds(2 * e, 1)][0] for t in taps], 0)
            return dot(left, rows).reshape(8, 16, 256)

        c, z = 10 * k, 8 * k
        acc[0] += side([xlo[c : c + 1], zlo[z : z + 8], xhi[c : c + 1]], (0, 1, 2))
        acc[7] += side([xlo[c + 9 : c + 10], zhi[z : z + 8], xhi[c + 9 : c + 10]], (6, 7, 8))
        acc[:, 0] += side([zero, xlo[c + 1 : c + 9], zero], (0, 3, 6))
        acc[:, 7] += side([zero, xhi[c + 1 : c + 9], zero], (2, 5, 8))
        plane = acc[...].reshape(4, 2, 4, 2, 16, 256).max(axis=(1, 3))
        emit(3 * e, jnp.maximum(plane, epool[one][0]))


def fine_last(odd, strips, w, b, facc, sides):
    return pl.pallas_call(
        fine_last_kernel,
        out_shape=jax.ShapeDtypeStruct((16, 64, 256), BF16),
        in_specs=[pl.BlockSpec(memory_space=pltpu.SMEM)] + [VMEM] * 10,
        out_specs=VMEM,
        scratch_shapes=[pltpu.VMEM((2, 8, 8, 16, 256), F32)],
        compiler_params=params(20),
        cost_estimate=cost(2 * 1024 * 384 * 256, 6 << 20),
        name="fine_last",
    )(odd, *strips, w, b, facc, *sides)


def deep_first_kernel(got, pad, w, out, xs):
    for y in range(4):
        plane = got[:, y * 16 : y * 16 + 16].reshape(256, 256)
        xs[y] = dot(pad[...], plane).astype(BF16).reshape(6, 6, 16, 256)

    def part(dy, first, size):
        taps = [
            xs[first : first + size, dz : dz + 4, dx : dx + 4].reshape(256 * size, 256)
            for dz in range(3)
            for dx in range(3)
        ]
        rows = [w[t, dy] for t in range(9)]
        acc = dot(jnp.concatenate(taps, -1), jnp.concatenate(rows, 0))
        return acc.reshape(size, 4, 4, 16, 256)

    out[...] = part(1, 0, 4)
    out[1:4] += part(0, 0, 3)
    out[0:3] += part(2, 1, 3)


def deep_first(got, pad, w):
    return pl.pallas_call(
        deep_first_kernel,
        out_shape=jax.ShapeDtypeStruct((4, 4, 4, 16, 256), F32),
        in_specs=[VMEM] * 3,
        out_specs=VMEM,
        scratch_shapes=[pltpu.VMEM((4, 6, 6, 16, 256), BF16)],
        compiler_params=params(40),
        cost_estimate=cost(2 * 1024 * 6912 * 256, 6 << 20),
        name="deep_first",
    )(got, pad, w)


def deep_last_kernel(odd, got_a, got_b, pad, w, b, acc_in, out, ys, full, turned):
    p = swap_rows()
    for y in (1, 2):
        full[:, :, y] = leaky(acc_in[y] + b[...]).astype(BF16)
    for k, (got, e) in enumerate(((got_a, odd[0]), (got_b, 1 - odd[0]))):
        ys[k] = dot(pad[...], got[...].reshape(256, 256)).astype(BF16).reshape(6, 6, 16, 256)
        taps = [ys[k, dz : dz + 4, dx : dx + 4].reshape(256, 256) for dz in range(3) for dx in range(3)]
        acc = dot(jnp.concatenate(taps, -1), w[:, pl.ds(2 * e, 1)].reshape(2304, 256))
        acc = acc.reshape(4, 4, 16, 256) + acc_in[pl.ds(3 * e, 1)][0]
        full[:, :, pl.ds(3 * e, 1)] = leaky(acc + b[...]).astype(BF16)[:, :, None]
    planes = [dot(p, full[z].reshape(256, 256)).reshape(16, 16, 256) for z in range(4)]
    lane = lax.broadcasted_iota(jnp.int32, (128, 128), 1)
    for big in range(4):
        for z in (0, 2):
            rows = [planes[z + k][big * 4 : big * 4 + 4].reshape(64, 256) for k in (0, 1)]
            flipped = jnp.concatenate(rows, 0).T.reshape(8, 2, 16, 128)
            low = flipped[:, 0].reshape(128, 128)
            high = flipped[:, 1].reshape(128, 128)
            first = jnp.where(lane < 64, low, pltpu.roll(high, 64, 1))
            second = jnp.where(lane < 64, pltpu.roll(low, 64, 1), high)
            turned[big * 4 + z] = first.astype(BF16).reshape(8, 16, 128)
            turned[big * 4 + z + 1] = second.astype(BF16).reshape(8, 16, 128)
    for c in (0, 2, 4, 6):
        pair = [turned[:, c + k].reshape(256, 128) for k in (0, 1)]
        moved = dot(p, jnp.concatenate(pair, -1)).astype(BF16)
        for k in (0, 1):
            out[c + k] = moved[:, k * 128 : (k + 1) * 128]


def deep_last(odd, got_a, got_b, pad, w, b, acc):
    return pl.pallas_call(
        deep_last_kernel,
        out_shape=jax.ShapeDtypeStruct((8, 256, 128), BF16),
        in_specs=[pl.BlockSpec(memory_space=pltpu.SMEM)] + [VMEM] * 6,
        out_specs=VMEM,
        scratch_shapes=[
            pltpu.VMEM((2, 6, 6, 16, 256), BF16),
            pltpu.VMEM((4, 4, 4, 16, 256), BF16),
            pltpu.VMEM((16, 8, 16, 128), BF16),
        ],
        compiler_params=params(24),
        cost_estimate=cost(2 * 512 * 2304 * 256, 6 << 20),
        name="deep_last",
    )(odd, got_a, got_b, pad, w, b, acc)


def arrange_kernel(got, lanes, out):
    lane = lax.broadcasted_iota(jnp.int32, (256, 128), 1)
    low, high = [], []
    for c in (0, 2, 4, 6):
        first, second = got[c].astype(F32), got[c + 1].astype(F32)
        low.append(jnp.where(lane < 64, first, pltpu.roll(second, 64, 1)).astype(BF16))
        high.append(jnp.where(lane < 64, pltpu.roll(first, 64, 1), second).astype(BF16))
    for h, half in enumerate((low, high)):
        spread = dot(jnp.concatenate(half, -1), lanes[...]).astype(BF16)
        out[0, h * 16 : (h + 1) * 16] = spread.reshape(16, 16, 512)


def arrange(got, lanes):
    return pl.pallas_call(
        arrange_kernel,
        out_shape=jax.ShapeDtypeStruct((1, 32, 16, 512), BF16),
        in_specs=[VMEM] * 2,
        out_specs=VMEM,
        compiler_params=params(16),
        cost_estimate=cost(2 * 512 * 512 * 512, 1 << 20),
        name="arrange",
    )(got, lanes)


def on_device(volume, fine_kernel, fine_bias, deep_kernel, deep_bias):
    odd = lax.axis_index("chan") % 2
    is_odd = odd == 1
    flag = odd.astype(jnp.int32).reshape(1)
    vol = volume.reshape(16, 8, 64, 128)

    def y_exchange(head, tail):
        got_a = swap_pairs(jnp.where(is_odd, tail, head), "chan", True)
        got_b = swap_pairs(jnp.where(is_odd, head, tail), "chan", False)
        return got_a, got_b

    block, tlo, thi = turn_all(vol)
    zlo, zhi = shift(thi, "sample", 1), shift(tlo, "sample", -1)
    got_a, got_b = y_exchange(block[:, :, 0:16], block[:, :, 112:128])
    w = fine_kernel.reshape(3456, 256)
    w9 = fine_kernel.reshape(9, 3, 128, 256)
    b = fine_bias.reshape(1, 256)
    mid_i, epool_i, eacc_i = fine_inner(block, w)

    def x_face(x):
        return jnp.concatenate([zlo[x : x + 1], block[:, x], zhi[x : x + 1]], 0)

    xlo, xhi = shift(x_face(7), "space", 1), shift(x_face(0), "space", -1)
    mid_z, epool_z, eacc_z = fine_ends(zlo, block, zhi, w)
    rzlo = shift(jnp.concatenate([got_a[7], got_b[7]], 0), "sample", 1)
    rzhi = shift(jnp.concatenate([got_a[0], got_b[0]], 0), "sample", -1)
    facc = fine_faces(flag, (got_a, got_b), w9, eacc_i, eacc_z)
    def rim(x):
        return jnp.concatenate(
            [rzlo[x : x + 1], got_a[:, x], rzhi[x : x + 1], rzlo[8 + x : 9 + x], got_b[:, x], rzhi[8 + x : 9 + x]], 0
        )

    rxlo, rxhi = shift(rim(7), "space", 1), shift(rim(0), "space", -1)
    sides = fine_sides(xlo, xhi, zlo, block, zhi, w, b, mid_i, epool_i, mid_z, epool_z)
    send = fine_last(flag, (rzlo, rzhi, rxlo, rxhi), w9, b, facc, sides)
    got = lax.all_to_all(send, ("sample", "space"), split_axis=0, concat_axis=0, tiled=True)

    got_a, got_b = y_exchange(got[:, 0:16], got[:, 48:64])
    pad = jnp.asarray(pad_matrix(), BF16)
    dw = deep_kernel.reshape(9, 3, 256, 256)
    acc = deep_first(got, pad, dw)
    send = deep_last(flag, got_a, got_b, pad, dw, deep_bias.reshape(1, 256), acc)
    got = lax.all_to_all(send, "chan", split_axis=0, concat_axis=0, tiled=True)
    return arrange(got, jnp.asarray(lane_matrix(), BF16))


def solution(mesh):
    placed = (P(None, "sample", "space", "chan", None), P(), P(), P(), P())
    return jax.shard_map(
        on_device,
        mesh=mesh,
        in_specs=placed,
        out_specs=P(("sample", "space"), "chan", None, None),
        check_vma=False,
    )
```

```python
import jax
import jax.numpy as jnp
import numpy as np
from jax import lax
from jax.experimental import pallas as pl
from jax.experimental.pallas import tpu as pltpu
from jax.sharding import PartitionSpec as P

MIB = 1 << 20
FINE_MIB = 36
BF16 = jnp.bfloat16
F32 = jnp.float32
VMEM = pl.BlockSpec(memory_space=pltpu.VMEM)
ANY = pl.BlockSpec(memory_space=pl.ANY)


def lane_matrix():
    src = np.arange(512).reshape(8, 4, 4, 4)
    dst = src.transpose(1, 2, 0, 3).reshape(-1)
    m = np.zeros((512, 512), np.float32)
    m[dst, np.arange(512)] = 1
    return m


def pad_matrix():
    m = np.zeros((6, 6, 16, 256), np.float32)
    for i in range(6):
        for j in range(6):
            for big in range(4):
                for p in range(4):
                    z, x = (4 * big + i - 1) % 16, (4 * p + j - 1) % 16
                    m[i, j, big * 4 + p, ((z // 4) * 4 + x // 4) * 16 + (z % 4) * 4 + x % 4] = 1
    return m.reshape(576, 256)


def params(mib):
    return pltpu.CompilerParams(vmem_limit_bytes=mib * MIB)


def cost(flops, moved):
    return pl.CostEstimate(flops=flops, bytes_accessed=moved, transcendentals=0)


def leaky(value):
    return jnp.where(value >= 0, value, 0.3 * value)


def dot(a, b):
    return jnp.dot(a, b, preferred_element_type=F32)


def swap_rows():
    i = lax.broadcasted_iota(jnp.int32, (256, 256), 0)
    j = lax.broadcasted_iota(jnp.int32, (256, 256), 1)
    hit = ((i >> 4) == (j & 15)) & ((i & 15) == (j >> 4))
    return jnp.where(hit, 1.0, 0.0).astype(BF16)


def shift(value, axis, step):
    n = lax.axis_size(axis)
    return lax.ppermute(value, axis, [(i, (i + step) % n) for i in range(n)])


def swap_pairs(value, axis, odd):
    n = lax.axis_size(axis)
    pairs = []
    for i in range(n):
        up = (i % 2 == 1) if odd else (i % 2 == 0)
        pairs.append((i, (i + 1) % n if up else (i - 1) % n))
    return lax.ppermute(value, axis, pairs)


def turn(p, slab, put):
    for j in (0, 2):
        halves = [slab[:, (j + k) * 16 : (j + k) * 16 + 16].reshape(256, 128) for k in (0, 1)]
        turned = dot(p, jnp.concatenate(halves, -1)).astype(BF16)
        for k in (0, 1):
            put(2 * (j + k), turned[:, k * 128 : (k + 1) * 128].reshape(2, 128, 128))


def turn_all_kernel(vol, block, lo, hi):
    p = swap_rows()
    for z in (0, 7, 1, 2, 3, 4, 5, 6):

        def put(x, value, z=z):
            block[z, x : x + 2] = value
            if z == 0:
                lo[x : x + 2] = value
            if z == 7:
                hi[x : x + 2] = value

        turn(p, vol[:, z], put)


def turn_all(vol):
    face = jax.ShapeDtypeStruct((8, 128, 128), BF16)
    return pl.pallas_call(
        turn_all_kernel,
        out_shape=[jax.ShapeDtypeStruct((8, 8, 128, 128), BF16), face, face],
        in_specs=[VMEM],
        out_specs=[VMEM] * 3,
        compiler_params=params(12),
        cost_estimate=cost(2 * 8192 * 256 * 256, 4 << 20),
        name="turn_all",
    )(vol)


def pool_inner(acc, z, mid, epool):
    parts = [acc[:, 0:1], jnp.maximum(acc[:, 1:2], acc[:, 2:3]), jnp.maximum(acc[:, 3:4], acc[:, 4:5]), acc[:, 5:6]]
    acc = jnp.concatenate(parts, 1)
    for i in range(acc.shape[0]):
        epool[0, z[i]] = acc[i, :, 0]
        epool[1, z[i]] = acc[i, :, 5]
        for y in (0, 1):
            mid[y, z[i]] = jnp.maximum(acc[i, :, 1 + 2 * y], acc[i, :, 2 + 2 * y])


def tap_rows(planes, dys, first, count):
    return [
        planes(dz, dx, slice((first + dy) * 16, (first + dy + count) * 16))
        for dz in range(3)
        for dx in range(3)
        for dy in dys
    ]


def inner_cells(planes, w):
    taps = [t.reshape(1152, 128) for t in tap_rows(planes, (0, 1, 2), 0, 6)]
    return dot(jnp.concatenate(taps, -1), w[...]).reshape(2, 6, 6, 16, 256)


def edge_rows(w, e):
    first = 128 * (1 - e)
    return jnp.concatenate([w[t * 384 + first : t * 384 + first + 256] for t in range(9)], 0)


def edge_cells(planes, cells, w, eacc):
    for e in (0, 1):
        taps = [t.reshape(cells * 16, 128) for t in tap_rows(planes, (0, 1), 6 * e, 1)]
        acc = dot(jnp.concatenate(taps, -1), edge_rows(w, e))
        eacc[e] = acc.reshape(eacc.shape[1:])


def pooled_f32(pairs):
    return jax.ShapeDtypeStruct((2, pairs, 4, 16, 256), F32)


def fine_call(kernel, outs, name, cells, operands, moved=5 << 20):
    return pl.pallas_call(
        kernel,
        out_shape=outs,
        in_specs=[VMEM] * len(operands),
        out_specs=[VMEM] * len(outs),
        compiler_params=params(FINE_MIB),
        cost_estimate=cost(cells * 16 * 3456 * 256 * 2, moved),
        name=name,
    )(*operands)


def fine_inner_kernel(block, w, mid, epool, eacc):
    def ends(dz, dx, rows):
        return jnp.concatenate([block[z + dz : z + dz + 1, dx : 6 + dx, rows] for z in (0, 5)], 0)

    pool_inner(inner_cells(ends, w), (0, 3), mid, epool)
    for z in (1, 2):

        def pair(dz, dx, rows, z=z):
            return block[2 * z - 1 + dz : 2 * z + 1 + dz, dx : 6 + dx, rows]

        acc = inner_cells(pair, w)
        pool_inner(jnp.maximum(acc[0:1], acc[1:2]), (z,), mid, epool)

    def planes(dz, dx, rows):
        return block[dz : 6 + dz, dx : 6 + dx, rows]

    edge_cells(planes, 36, w, eacc)


def fine_inner(block, w):
    outs = [pooled_f32(4), pooled_f32(4), jax.ShapeDtypeStruct((2, 6, 6, 16, 256), F32)]
    return fine_call(fine_inner_kernel, outs, "fine_inner", 270, (block, w))


def fine_ends_kernel(zlo, block, zhi, w, mid, epool, eacc):
    def planes(dz, dx, rows):
        low = zlo[dx : 6 + dx, rows] if dz == 0 else block[dz - 1, dx : 6 + dx, rows]
        high = zhi[dx : 6 + dx, rows] if dz == 2 else block[6 + dz, dx : 6 + dx, rows]
        return jnp.stack([low, high], 0)

    pool_inner(inner_cells(planes, w), (0, 1), mid, epool)
    edge_cells(planes, 12, w, eacc)


def fine_ends(zlo, block, zhi, w):
    outs = [pooled_f32(2), pooled_f32(2), jax.ShapeDtypeStruct((2, 2, 6, 16, 256), F32)]
    return fine_call(fine_ends_kernel, outs, "fine_ends", 90, (zlo, block, zhi, w))


def emitter(p, out, b):
    def emit(y, plane):
        cells = leaky(plane + b[...]).astype(BF16).reshape(256, 256)
        out[:, pl.ds(y * 16 if isinstance(y, int) else pl.multiple_of(y * 16, 16), 16)] = (
            dot(p, cells).astype(BF16).reshape(16, 16, 256)
        )

    return emit


def fine_sides_kernel(
    xlo, xhi, zlo, block, zhi, w, b, mid_i, epool_i, mid_z, epool_z, outm, epool, eacc
):
    def column(x, dz, rows):
        if dz == 0:
            return jnp.concatenate([zlo[x : x + 1, rows], block[0:7, x, rows]], 0)
        if dz == 1:
            return block[0:8, x, rows]
        return jnp.concatenate([block[1:8, x, rows], zhi[x : x + 1, rows]], 0)

    def planes(dz, dx, rows):
        first = xlo[dz : dz + 8, rows] if dx == 0 else column(dx - 1, dz, rows)
        second = xhi[dz : dz + 8, rows] if dx == 2 else column(6 + dx, dz, rows)
        return jnp.stack([first, second], 1)

    taps = [t.reshape(1536, 128) for t in tap_rows(planes, (0, 1, 2), 0, 6)]
    acc = dot(jnp.concatenate(taps, -1), w[...]).reshape(4, 2, 2, 6, 16, 256).max(axis=1)

    def whole(sides, inner, ends):
        low = jnp.maximum(inner[0:1], ends[0:1])
        high = jnp.maximum(inner[3:4], ends[1:2])
        plane = jnp.concatenate([low, inner[1:3], high], 0)
        first = jnp.maximum(plane[:, 0:1], sides[:, 0:1])
        last = jnp.maximum(plane[:, 3:4], sides[:, 1:2])
        return jnp.concatenate([first, plane[:, 1:3], last], 1)

    for e in (0, 1):
        epool[e] = whole(acc[:, :, 5 * e], epool_i[e], epool_z[e])
    emit = emitter(swap_rows(), outm, b)
    for y in (0, 1):
        inner = jnp.maximum(acc[:, :, 1 + 2 * y], acc[:, :, 2 + 2 * y])
        emit(y, whole(inner, mid_i[y], mid_z[y]))
    edge_cells(planes, 16, w, eacc)


def fine_sides(*operands):
    outs = [
        jax.ShapeDtypeStruct((16, 32, 256), BF16),
        pooled_f32(4),
        jax.ShapeDtypeStruct((2, 8, 2, 16, 256), F32),
    ]
    return fine_call(fine_sides_kernel, outs, "fine_sides", 124, operands)


def fine_faces_kernel(odd, got_a, got_b, w, eacc_i, eacc_z, out, ys):
    ys[...] = jnp.zeros_like(ys)
    for k, (got, e) in enumerate(((got_a, odd[0]), (got_b, 1 - odd[0]))):
        ys[k, 1:9, 1:9] = got[...]
        taps = [ys[k, dz : dz + 8, dx : dx + 8].reshape(1024, 128) for dz in range(3) for dx in range(3)]
        acc = dot(jnp.concatenate(taps, -1), w[:, pl.ds(2 * e, 1)].reshape(1152, 256))
        acc = acc.reshape(8, 8, 16, 256)
        one = pl.ds(e, 1)
        out[one, :, 0] = acc[None, :, 0]
        out[one, :, 7] = acc[None, :, 7]
        out[one, 0, 1:7] = acc[None, 0, 1:7] + eacc_z[one, 0]
        out[one, 1:7, 1:7] = acc[None, 1:7, 1:7] + eacc_i[one]
        out[one, 7, 1:7] = acc[None, 7, 1:7] + eacc_z[one, 1]


def fine_faces(odd, faces, w, eacc_i, eacc_z):
    return pl.pallas_call(
        fine_faces_kernel,
        out_shape=jax.ShapeDtypeStruct((2, 8, 8, 16, 256), F32),
        in_specs=[pl.BlockSpec(memory_space=pltpu.SMEM)] + [VMEM] * 5,
        out_specs=VMEM,
        scratch_shapes=[pltpu.VMEM((2, 10, 10, 16, 128), BF16)],
        compiler_params=params(20),
        cost_estimate=cost(2 * 2048 * 1152 * 256, 6 << 20),
        name="fine_faces",
    )(odd, *faces, w, eacc_i, eacc_z)


def fine_last_kernel(odd, zlo, zhi, xlo, xhi, w, b, facc, outm, epool, eacc, out, sums):
    emit = emitter(swap_rows(), out, b)
    out[:, 16:48] = outm[...]
    zero = jnp.zeros((1, 16, 128), BF16)
    for k, e in enumerate((odd[0], 1 - odd[0])):
        one = pl.ds(e, 1)
        acc = sums.at[k]
        acc[:, 1:7] = facc[one, :, 1:7][0]
        acc[:, 0] = facc[one, :, 0][0] + eacc[one, :, 0][0]
        acc[:, 7] = facc[one, :, 7][0] + eacc[one, :, 1][0]

        def side(cells, taps):
            cells = jnp.concatenate(cells, 0)
            left = jnp.concatenate([cells[t : t + 8].reshape(128, 128) for t in range(3)], -1)
            rows = jnp.concatenate([w[t, pl.ds(2 * e, 1)][0] for t in taps], 0)
            return dot(left, rows).reshape(8, 16, 256)

        c, z = 10 * k, 8 * k
        acc[0] += side([xlo[c : c + 1], zlo[z : z + 8], xhi[c : c + 1]], (0, 1, 2))
        acc[7] += side([xlo[c + 9 : c + 10], zhi[z : z + 8], xhi[c + 9 : c + 10]], (6, 7, 8))
        acc[:, 0] += side([zero, xlo[c + 1 : c + 9], zero], (0, 3, 6))
        acc[:, 7] += side([zero, xhi[c + 1 : c + 9], zero], (2, 5, 8))
        plane = acc[...].reshape(4, 2, 4, 2, 16, 256).max(axis=(1, 3))
        emit(3 * e, jnp.maximum(plane, epool[one][0]))


def fine_last(odd, strips, w, b, facc, sides):
    return pl.pallas_call(
        fine_last_kernel,
        out_shape=jax.ShapeDtypeStruct((16, 64, 256), BF16),
        in_specs=[pl.BlockSpec(memory_space=pltpu.SMEM)] + [VMEM] * 10,
        out_specs=VMEM,
        scratch_shapes=[pltpu.VMEM((2, 8, 8, 16, 256), F32)],
        compiler_params=params(20),
        cost_estimate=cost(2 * 1024 * 384 * 256, 6 << 20),
        name="fine_last",
    )(odd, *strips, w, b, facc, *sides)


def deep_first_kernel(got, pad, w, out, xs):
    for y in range(4):
        plane = got[:, y * 16 : y * 16 + 16].reshape(256, 256)
        xs[y] = dot(pad[...], plane).astype(BF16).reshape(6, 6, 16, 256)

    def part(dy, first, size):
        taps = [
            xs[first : first + size, dz : dz + 4, dx : dx + 4].reshape(256 * size, 256)
            for dz in range(3)
            for dx in range(3)
        ]
        rows = [w[t, dy] for t in range(9)]
        acc = dot(jnp.concatenate(taps, -1), jnp.concatenate(rows, 0))
        return acc.reshape(size, 4, 4, 16, 256)

    out[...] = part(1, 0, 4)
    out[1:4] += part(0, 0, 3)
    out[0:3] += part(2, 1, 3)


def deep_first(got, pad, w):
    return pl.pallas_call(
        deep_first_kernel,
        out_shape=jax.ShapeDtypeStruct((4, 4, 4, 16, 256), F32),
        in_specs=[VMEM] * 3,
        out_specs=VMEM,
        scratch_shapes=[pltpu.VMEM((4, 6, 6, 16, 256), BF16)],
        compiler_params=params(40),
        cost_estimate=cost(2 * 1024 * 6912 * 256, 6 << 20),
        name="deep_first",
    )(got, pad, w)


def deep_last_kernel(odd, got_a, got_b, pad, w, b, acc_in, out, ys, full, turned):
    p = swap_rows()
    for y in (1, 2):
        full[:, :, y] = leaky(acc_in[y] + b[...]).astype(BF16)
    for k, (got, e) in enumerate(((got_a, odd[0]), (got_b, 1 - odd[0]))):
        ys[k] = dot(pad[...], got[...].reshape(256, 256)).astype(BF16).reshape(6, 6, 16, 256)
        taps = [ys[k, dz : dz + 4, dx : dx + 4].reshape(256, 256) for dz in range(3) for dx in range(3)]
        acc = dot(jnp.concatenate(taps, -1), w[:, pl.ds(2 * e, 1)].reshape(2304, 256))
        acc = acc.reshape(4, 4, 16, 256) + acc_in[pl.ds(3 * e, 1)][0]
        full[:, :, pl.ds(3 * e, 1)] = leaky(acc + b[...]).astype(BF16)[:, :, None]
    planes = [dot(p, full[z].reshape(256, 256)).reshape(16, 16, 256) for z in range(4)]
    for k in range(8):
        big, z = k // 4, k % 4
        rows = [planes[z][b4 * 4 : b4 * 4 + 4].reshape(64, 256) for b4 in (big, big + 2)]
        turned[k] = jnp.concatenate(rows, 0).T.astype(BF16).reshape(8, 32, 128)
    i = lax.broadcasted_iota(jnp.int32, (256, 256), 0)
    j = lax.broadcasted_iota(jnp.int32, (256, 256), 1)
    q = jnp.where(((i >> 3) == (j & 31)) & ((i & 7) == (j >> 5)), 1.0, 0.0).astype(BF16)
    for c in (0, 2, 4, 6):
        pair = [turned[:, c + k].reshape(256, 128) for k in (0, 1)]
        moved = dot(q, jnp.concatenate(pair, -1)).astype(BF16)
        for k in (0, 1):
            out[c + k] = moved[:, k * 128 : (k + 1) * 128]


def deep_last(odd, got_a, got_b, pad, w, b, acc):
    return pl.pallas_call(
        deep_last_kernel,
        out_shape=jax.ShapeDtypeStruct((8, 256, 128), BF16),
        in_specs=[pl.BlockSpec(memory_space=pltpu.SMEM)] + [VMEM] * 6,
        out_specs=VMEM,
        scratch_shapes=[
            pltpu.VMEM((2, 6, 6, 16, 256), BF16),
            pltpu.VMEM((4, 4, 4, 16, 256), BF16),
            pltpu.VMEM((8, 8, 32, 128), BF16),
        ],
        compiler_params=params(24),
        cost_estimate=cost(2 * 512 * 2304 * 256, 6 << 20),
        name="deep_last",
    )(odd, got_a, got_b, pad, w, b, acc)


def arrange_kernel(got, lanes, out):
    lane = lax.broadcasted_iota(jnp.int32, (256, 128), 1)
    low, high = [], []
    for c in (0, 2, 4, 6):
        first, second = got[c].astype(F32), got[c + 1].astype(F32)
        low.append(jnp.where(lane < 64, first, pltpu.roll(second, 64, 1)).astype(BF16))
        high.append(jnp.where(lane < 64, pltpu.roll(first, 64, 1), second).astype(BF16))
    halves = [dot(jnp.concatenate(half, -1), lanes[...]).reshape(32, 8, 512) for half in (low, high)]
    out[0] = jnp.concatenate(halves, 1).astype(BF16)


def arrange(got, lanes):
    return pl.pallas_call(
        arrange_kernel,
        out_shape=jax.ShapeDtypeStruct((1, 32, 16, 512), BF16),
        in_specs=[VMEM] * 2,
        out_specs=VMEM,
        compiler_params=params(16),
        cost_estimate=cost(2 * 512 * 512 * 512, 1 << 20),
        name="arrange",
    )(got, lanes)


def on_device(volume, fine_kernel, fine_bias, deep_kernel, deep_bias):
    odd = lax.axis_index("chan") % 2
    is_odd = odd == 1
    flag = odd.astype(jnp.int32).reshape(1)
    vol = volume.reshape(16, 8, 64, 128)

    def y_exchange(head, tail):
        got_a = swap_pairs(jnp.where(is_odd, tail, head), "chan", True)
        got_b = swap_pairs(jnp.where(is_odd, head, tail), "chan", False)
        return got_a, got_b

    block, tlo, thi = turn_all(vol)
    zlo, zhi = shift(thi, "sample", 1), shift(tlo, "sample", -1)
    got_a, got_b = y_exchange(block[:, :, 0:16], block[:, :, 112:128])
    w = fine_kernel.reshape(3456, 256)
    w9 = fine_kernel.reshape(9, 3, 128, 256)
    b = fine_bias.reshape(1, 256)
    mid_i, epool_i, eacc_i = fine_inner(block, w)

    def x_face(x):
        return jnp.concatenate([zlo[x : x + 1], block[:, x], zhi[x : x + 1]], 0)

    xlo, xhi = shift(x_face(7), "space", 1), shift(x_face(0), "space", -1)
    mid_z, epool_z, eacc_z = fine_ends(zlo, block, zhi, w)
    rzlo = shift(jnp.concatenate([got_a[7], got_b[7]], 0), "sample", 1)
    rzhi = shift(jnp.concatenate([got_a[0], got_b[0]], 0), "sample", -1)
    facc = fine_faces(flag, (got_a, got_b), w9, eacc_i, eacc_z)
    def rim(x):
        return jnp.concatenate(
            [rzlo[x : x + 1], got_a[:, x], rzhi[x : x + 1], rzlo[8 + x : 9 + x], got_b[:, x], rzhi[8 + x : 9 + x]], 0
        )

    rxlo, rxhi = shift(rim(7), "space", 1), shift(rim(0), "space", -1)
    sides = fine_sides(xlo, xhi, zlo, block, zhi, w, b, mid_i, epool_i, mid_z, epool_z)
    send = fine_last(flag, (rzlo, rzhi, rxlo, rxhi), w9, b, facc, sides)
    got = lax.all_to_all(send, ("sample", "space"), split_axis=0, concat_axis=0, tiled=True)

    got_a, got_b = y_exchange(got[:, 0:16], got[:, 48:64])
    pad = jnp.asarray(pad_matrix(), BF16)
    dw = deep_kernel.reshape(9, 3, 256, 256)
    acc = deep_first(got, pad, dw)
    send = deep_last(flag, got_a, got_b, pad, dw, deep_bias.reshape(1, 256), acc)
    got = lax.all_to_all(send, "chan", split_axis=0, concat_axis=0, tiled=True)
    return arrange(got, jnp.asarray(lane_matrix(), BF16))


def solution(mesh):
    placed = (P(None, "sample", "space", "chan", None), P(), P(), P(), P())
    return jax.shard_map(
        on_device,
        mesh=mesh,
        in_specs=placed,
        out_specs=P(("sample", "space"), "chan", None, None),
        check_vma=False,
    )
```

```python
import jax
import jax.numpy as jnp
import numpy as np
from jax import lax
from jax.experimental import pallas as pl
from jax.experimental.pallas import tpu as pltpu
from jax.sharding import PartitionSpec as P

MIB = 1 << 20
FINE_MIB = 36
BF16 = jnp.bfloat16
F32 = jnp.float32
VMEM = pl.BlockSpec(memory_space=pltpu.VMEM)
ANY = pl.BlockSpec(memory_space=pl.ANY)


def lane_matrix():
    src = np.arange(512).reshape(8, 4, 4, 4)
    dst = src.transpose(1, 2, 0, 3).reshape(-1)
    m = np.zeros((512, 512), np.float32)
    m[dst, np.arange(512)] = 1
    return m


def pad_matrix():
    m = np.zeros((6, 6, 16, 256), np.float32)
    for i in range(6):
        for j in range(6):
            for big in range(4):
                for p in range(4):
                    z, x = (4 * big + i - 1) % 16, (4 * p + j - 1) % 16
                    m[i, j, big * 4 + p, ((z // 4) * 4 + x // 4) * 16 + (z % 4) * 4 + x % 4] = 1
    return m.reshape(576, 256)


def params(mib):
    return pltpu.CompilerParams(vmem_limit_bytes=mib * MIB)


def cost(flops, moved):
    return pl.CostEstimate(flops=flops, bytes_accessed=moved, transcendentals=0)


def leaky(value):
    return jnp.where(value >= 0, value, 0.3 * value)


def dot(a, b):
    return jnp.dot(a, b, preferred_element_type=F32)


def swap_rows():
    i = lax.broadcasted_iota(jnp.int32, (256, 256), 0)
    j = lax.broadcasted_iota(jnp.int32, (256, 256), 1)
    hit = ((i >> 4) == (j & 15)) & ((i & 15) == (j >> 4))
    return jnp.where(hit, 1.0, 0.0).astype(BF16)


def shift(value, axis, step):
    n = lax.axis_size(axis)
    return lax.ppermute(value, axis, [(i, (i + step) % n) for i in range(n)])


def swap_pairs(value, axis, odd):
    n = lax.axis_size(axis)
    pairs = []
    for i in range(n):
        up = (i % 2 == 1) if odd else (i % 2 == 0)
        pairs.append((i, (i + 1) % n if up else (i - 1) % n))
    return lax.ppermute(value, axis, pairs)


def turn(p, slab, put):
    for j in (0, 2):
        halves = [slab[:, (j + k) * 16 : (j + k) * 16 + 16].reshape(256, 128) for k in (0, 1)]
        turned = dot(p, jnp.concatenate(halves, -1)).astype(BF16)
        for k in (0, 1):
            put(2 * (j + k), turned[:, k * 128 : (k + 1) * 128].reshape(2, 128, 128))


def turn_all_kernel(vol, block, lo, hi):
    p = swap_rows()
    for z in (0, 7, 1, 2, 3, 4, 5, 6):

        def put(x, value, z=z):
            block[z, x : x + 2] = value
            if z == 0:
                lo[x : x + 2] = value
            if z == 7:
                hi[x : x + 2] = value

        turn(p, vol[:, z], put)


def turn_all(vol):
    face = jax.ShapeDtypeStruct((8, 128, 128), BF16)
    return pl.pallas_call(
        turn_all_kernel,
        out_shape=[jax.ShapeDtypeStruct((8, 8, 128, 128), BF16), face, face],
        in_specs=[VMEM],
        out_specs=[VMEM] * 3,
        compiler_params=params(12),
        cost_estimate=cost(2 * 8192 * 256 * 256, 4 << 20),
        name="turn_all",
    )(vol)


def pool_inner(acc, z, mid, epool):
    parts = [acc[:, 0:1], jnp.maximum(acc[:, 1:2], acc[:, 2:3]), jnp.maximum(acc[:, 3:4], acc[:, 4:5]), acc[:, 5:6]]
    acc = jnp.concatenate(parts, 1)
    for i in range(acc.shape[0]):
        epool[0, z[i]] = acc[i, :, 0]
        epool[1, z[i]] = acc[i, :, 5]
        for y in (0, 1):
            mid[y, z[i]] = jnp.maximum(acc[i, :, 1 + 2 * y], acc[i, :, 2 + 2 * y])


def tap_rows(planes, dys, first, count):
    return [
        planes(dz, dx, slice((first + dy) * 16, (first + dy + count) * 16))
        for dz in range(3)
        for dx in range(3)
        for dy in dys
    ]


def inner_cells(planes, w):
    taps = [t.reshape(1152, 128) for t in tap_rows(planes, (0, 1, 2), 0, 6)]
    return dot(jnp.concatenate(taps, -1), w[...]).reshape(2, 6, 6, 16, 256)


def edge_rows(w, e):
    first = 128 * (1 - e)
    return jnp.concatenate([w[t * 384 + first : t * 384 + first + 256] for t in range(9)], 0)


def edge_cells(planes, cells, w, eacc):
    for e in (0, 1):
        taps = [t.reshape(cells * 16, 128) for t in tap_rows(planes, (0, 1), 6 * e, 1)]
        acc = dot(jnp.concatenate(taps, -1), edge_rows(w, e))
        eacc[e] = acc.reshape(eacc.shape[1:])


def pooled_f32(pairs):
    return jax.ShapeDtypeStruct((2, pairs, 4, 16, 256), F32)


def fine_call(kernel, outs, name, cells, operands, moved=5 << 20):
    return pl.pallas_call(
        kernel,
        out_shape=outs,
        in_specs=[VMEM] * len(operands),
        out_specs=[VMEM] * len(outs),
        compiler_params=params(FINE_MIB),
        cost_estimate=cost(cells * 16 * 3456 * 256 * 2, moved),
        name=name,
    )(*operands)


def fine_inner_kernel(block, w, mid, epool, eacc):
    def ends(dz, dx, rows):
        return jnp.concatenate([block[z + dz : z + dz + 1, dx : 6 + dx, rows] for z in (0, 5)], 0)

    pool_inner(inner_cells(ends, w), (0, 3), mid, epool)
    for z in (1, 2):

        def pair(dz, dx, rows, z=z):
            return block[2 * z - 1 + dz : 2 * z + 1 + dz, dx : 6 + dx, rows]

        acc = inner_cells(pair, w)
        pool_inner(jnp.maximum(acc[0:1], acc[1:2]), (z,), mid, epool)

    def planes(dz, dx, rows):
        return block[dz : 6 + dz, dx : 6 + dx, rows]

    edge_cells(planes, 36, w, eacc)


def fine_inner(block, w):
    outs = [pooled_f32(4), pooled_f32(4), jax.ShapeDtypeStruct((2, 6, 6, 16, 256), F32)]
    return fine_call(fine_inner_kernel, outs, "fine_inner", 270, (block, w))


def fine_ends_kernel(zlo, block, zhi, w, mid, epool, eacc):
    def planes(dz, dx, rows):
        low = zlo[dx : 6 + dx, rows] if dz == 0 else block[dz - 1, dx : 6 + dx, rows]
        high = zhi[dx : 6 + dx, rows] if dz == 2 else block[6 + dz, dx : 6 + dx, rows]
        return jnp.stack([low, high], 0)

    pool_inner(inner_cells(planes, w), (0, 1), mid, epool)
    edge_cells(planes, 12, w, eacc)


def fine_ends(zlo, block, zhi, w):
    outs = [pooled_f32(2), pooled_f32(2), jax.ShapeDtypeStruct((2, 2, 6, 16, 256), F32)]
    return fine_call(fine_ends_kernel, outs, "fine_ends", 90, (zlo, block, zhi, w))


def emitter(p, out, b):
    def emit(y, plane):
        cells = leaky(plane + b[...]).astype(BF16).reshape(256, 256)
        out[:, pl.ds(y * 16 if isinstance(y, int) else pl.multiple_of(y * 16, 16), 16)] = (
            dot(p, cells).astype(BF16).reshape(16, 16, 256)
        )

    return emit


def fine_sides_kernel(
    xlo, xhi, zlo, block, zhi, w, b, mid_i, epool_i, mid_z, epool_z, outm, epool, eacc
):
    def column(x, dz, rows):
        if dz == 0:
            return jnp.concatenate([zlo[x : x + 1, rows], block[0:7, x, rows]], 0)
        if dz == 1:
            return block[0:8, x, rows]
        return jnp.concatenate([block[1:8, x, rows], zhi[x : x + 1, rows]], 0)

    def planes(dz, dx, rows):
        first = xlo[dz : dz + 8, rows] if dx == 0 else column(dx - 1, dz, rows)
        second = xhi[dz : dz + 8, rows] if dx == 2 else column(6 + dx, dz, rows)
        return jnp.stack([first, second], 1)

    taps = [t.reshape(1536, 128) for t in tap_rows(planes, (0, 1, 2), 0, 6)]
    acc = dot(jnp.concatenate(taps, -1), w[...]).reshape(4, 2, 2, 6, 16, 256).max(axis=1)

    def whole(sides, inner, ends):
        low = jnp.maximum(inner[0:1], ends[0:1])
        high = jnp.maximum(inner[3:4], ends[1:2])
        plane = jnp.concatenate([low, inner[1:3], high], 0)
        first = jnp.maximum(plane[:, 0:1], sides[:, 0:1])
        last = jnp.maximum(plane[:, 3:4], sides[:, 1:2])
        return jnp.concatenate([first, plane[:, 1:3], last], 1)

    for e in (0, 1):
        epool[e] = whole(acc[:, :, 5 * e], epool_i[e], epool_z[e])
    emit = emitter(swap_rows(), outm, b)
    for y in (0, 1):
        inner = jnp.maximum(acc[:, :, 1 + 2 * y], acc[:, :, 2 + 2 * y])
        emit(y, whole(inner, mid_i[y], mid_z[y]))
    edge_cells(planes, 16, w, eacc)


def fine_sides(*operands):
    outs = [
        jax.ShapeDtypeStruct((16, 32, 256), BF16),
        pooled_f32(4),
        jax.ShapeDtypeStruct((2, 8, 2, 16, 256), F32),
    ]
    return fine_call(fine_sides_kernel, outs, "fine_sides", 124, operands)


def fine_faces_kernel(odd, got_a, got_b, w, eacc_i, eacc_z, out, ys):
    ys[...] = jnp.zeros_like(ys)
    for k, (got, e) in enumerate(((got_a, odd[0]), (got_b, 1 - odd[0]))):
        ys[k, 1:9, 1:9] = got[...]
        taps = [ys[k, dz : dz + 8, dx : dx + 8].reshape(1024, 128) for dz in range(3) for dx in range(3)]
        acc = dot(jnp.concatenate(taps, -1), w[:, pl.ds(2 * e, 1)].reshape(1152, 256))
        acc = acc.reshape(8, 8, 16, 256)
        one = pl.ds(e, 1)
        out[one, :, 0] = acc[None, :, 0]
        out[one, :, 7] = acc[None, :, 7]
        out[one, 0, 1:7] = acc[None, 0, 1:7] + eacc_z[one, 0]
        out[one, 1:7, 1:7] = acc[None, 1:7, 1:7] + eacc_i[one]
        out[one, 7, 1:7] = acc[None, 7, 1:7] + eacc_z[one, 1]


def fine_faces(odd, faces, w, eacc_i, eacc_z):
    return pl.pallas_call(
        fine_faces_kernel,
        out_shape=jax.ShapeDtypeStruct((2, 8, 8, 16, 256), F32),
        in_specs=[pl.BlockSpec(memory_space=pltpu.SMEM)] + [VMEM] * 5,
        out_specs=VMEM,
        scratch_shapes=[pltpu.VMEM((2, 10, 10, 16, 128), BF16)],
        compiler_params=params(20),
        cost_estimate=cost(2 * 2048 * 1152 * 256, 6 << 20),
        name="fine_faces",
    )(odd, *faces, w, eacc_i, eacc_z)


def fine_last_kernel(odd, zlo, zhi, xlo, xhi, w, b, facc, outm, epool, eacc, out, sums):
    emit = emitter(swap_rows(), out, b)
    out[:, 16:48] = outm[...]
    zero = jnp.zeros((1, 16, 128), BF16)
    for k, e in enumerate((odd[0], 1 - odd[0])):
        one = pl.ds(e, 1)
        acc = sums.at[k]
        acc[:, 1:7] = facc[one, :, 1:7][0]
        acc[:, 0] = facc[one, :, 0][0] + eacc[one, :, 0][0]
        acc[:, 7] = facc[one, :, 7][0] + eacc[one, :, 1][0]

        def side(cells, taps):
            cells = jnp.concatenate(cells, 0)
            left = jnp.concatenate([cells[t : t + 8].reshape(128, 128) for t in range(3)], -1)
            rows = jnp.concatenate([w[t, pl.ds(2 * e, 1)][0] for t in taps], 0)
            return dot(left, rows).reshape(8, 16, 256)

        c, z = 10 * k, 8 * k
        acc[0] += side([xlo[c : c + 1], zlo[z : z + 8], xhi[c : c + 1]], (0, 1, 2))
        acc[7] += side([xlo[c + 9 : c + 10], zhi[z : z + 8], xhi[c + 9 : c + 10]], (6, 7, 8))
        acc[:, 0] += side([zero, xlo[c + 1 : c + 9], zero], (0, 3, 6))
        acc[:, 7] += side([zero, xhi[c + 1 : c + 9], zero], (2, 5, 8))
        plane = acc[...].reshape(4, 2, 4, 2, 16, 256).max(axis=(1, 3))
        emit(3 * e, jnp.maximum(plane, epool[one][0]))


def fine_last(odd, strips, w, b, facc, sides):
    return pl.pallas_call(
        fine_last_kernel,
        out_shape=jax.ShapeDtypeStruct((16, 64, 256), BF16),
        in_specs=[pl.BlockSpec(memory_space=pltpu.SMEM)] + [VMEM] * 10,
        out_specs=VMEM,
        scratch_shapes=[pltpu.VMEM((2, 8, 8, 16, 256), F32)],
        compiler_params=params(20),
        cost_estimate=cost(2 * 1024 * 384 * 256, 6 << 20),
        name="fine_last",
    )(odd, *strips, w, b, facc, *sides)


def deep_first_kernel(got, pad, w, out, xs):
    for y in range(4):
        plane = got[:, y * 16 : y * 16 + 16].reshape(256, 256)
        xs[y] = dot(pad[...], plane).astype(BF16).reshape(6, 6, 16, 256)

    def part(dy, first, size):
        taps = [
            xs[first : first + size, dz : dz + 4, dx : dx + 4].reshape(256 * size, 256)
            for dz in range(3)
            for dx in range(3)
        ]
        rows = [w[t, dy] for t in range(9)]
        acc = dot(jnp.concatenate(taps, -1), jnp.concatenate(rows, 0))
        return acc.reshape(size, 4, 4, 16, 256)

    out[...] = part(1, 0, 4)
    out[1:4] += part(0, 0, 3)
    out[0:3] += part(2, 1, 3)


def deep_first(got, pad, w):
    return pl.pallas_call(
        deep_first_kernel,
        out_shape=jax.ShapeDtypeStruct((4, 4, 4, 16, 256), F32),
        in_specs=[VMEM] * 3,
        out_specs=VMEM,
        scratch_shapes=[pltpu.VMEM((4, 6, 6, 16, 256), BF16)],
        compiler_params=params(40),
        cost_estimate=cost(2 * 1024 * 6912 * 256, 6 << 20),
        name="deep_first",
    )(got, pad, w)


def deep_last_kernel(odd, got_a, got_b, pad, w, b, acc_in, out, ys, full, turned):
    p = swap_rows()
    for y in (1, 2):
        full[:, :, y] = leaky(acc_in[y] + b[...]).astype(BF16)
    for k, (got, e) in enumerate(((got_a, odd[0]), (got_b, 1 - odd[0]))):
        ys[k] = dot(pad[...], got[...].reshape(256, 256)).astype(BF16).reshape(6, 6, 16, 256)
        taps = [ys[k, dz : dz + 4, dx : dx + 4].reshape(256, 256) for dz in range(3) for dx in range(3)]
        acc = dot(jnp.concatenate(taps, -1), w[:, pl.ds(2 * e, 1)].reshape(2304, 256))
        acc = acc.reshape(4, 4, 16, 256) + acc_in[pl.ds(3 * e, 1)][0]
        full[:, :, pl.ds(3 * e, 1)] = leaky(acc + b[...]).astype(BF16)[:, :, None]
    planes = [dot(p, full[z].reshape(256, 256)).reshape(16, 16, 256) for z in range(4)]
    for k in range(8):
        big, z = k // 4, k % 4
        rows = [planes[z][b4 * 4 : b4 * 4 + 4].reshape(64, 256) for b4 in (big, big + 2)]
        turned[k] = jnp.concatenate(rows, 0).astype(BF16).T.reshape(8, 32, 128)
    i = lax.broadcasted_iota(jnp.int32, (256, 256), 0)
    j = lax.broadcasted_iota(jnp.int32, (256, 256), 1)
    q = jnp.where(((i >> 3) == (j & 31)) & ((i & 7) == (j >> 5)), 1.0, 0.0).astype(BF16)
    for c in (0, 2, 4, 6):
        pair = [turned[:, c + k].reshape(256, 128) for k in (0, 1)]
        moved = dot(q, jnp.concatenate(pair, -1)).astype(BF16)
        for k in (0, 1):
            out[c + k] = moved[:, k * 128 : (k + 1) * 128]


def deep_last(odd, got_a, got_b, pad, w, b, acc):
    return pl.pallas_call(
        deep_last_kernel,
        out_shape=jax.ShapeDtypeStruct((8, 256, 128), BF16),
        in_specs=[pl.BlockSpec(memory_space=pltpu.SMEM)] + [VMEM] * 6,
        out_specs=VMEM,
        scratch_shapes=[
            pltpu.VMEM((2, 6, 6, 16, 256), BF16),
            pltpu.VMEM((4, 4, 4, 16, 256), BF16),
            pltpu.VMEM((8, 8, 32, 128), BF16),
        ],
        compiler_params=params(24),
        cost_estimate=cost(2 * 512 * 2304 * 256, 6 << 20),
        name="deep_last",
    )(odd, got_a, got_b, pad, w, b, acc)


def arrange_kernel(got, lanes, out):
    lane = lax.broadcasted_iota(jnp.int32, (256, 128), 1)
    low, high = [], []
    for c in (0, 2, 4, 6):
        first, second = got[c].astype(F32), got[c + 1].astype(F32)
        low.append(jnp.where(lane < 64, first, pltpu.roll(second, 64, 1)).astype(BF16))
        high.append(jnp.where(lane < 64, pltpu.roll(first, 64, 1), second).astype(BF16))
    halves = [dot(jnp.concatenate(half, -1), lanes[...]).reshape(32, 8, 512) for half in (low, high)]
    out[0] = jnp.concatenate(halves, 1).astype(BF16)


def arrange(got, lanes):
    return pl.pallas_call(
        arrange_kernel,
        out_shape=jax.ShapeDtypeStruct((1, 32, 16, 512), BF16),
        in_specs=[VMEM] * 2,
        out_specs=VMEM,
        compiler_params=params(16),
        cost_estimate=cost(2 * 512 * 512 * 512, 1 << 20),
        name="arrange",
    )(got, lanes)


def on_device(volume, fine_kernel, fine_bias, deep_kernel, deep_bias):
    odd = lax.axis_index("chan") % 2
    is_odd = odd == 1
    flag = odd.astype(jnp.int32).reshape(1)
    vol = volume.reshape(16, 8, 64, 128)

    def y_exchange(head, tail):
        got_a = swap_pairs(jnp.where(is_odd, tail, head), "chan", True)
        got_b = swap_pairs(jnp.where(is_odd, head, tail), "chan", False)
        return got_a, got_b

    block, tlo, thi = turn_all(vol)
    zlo, zhi = shift(thi, "sample", 1), shift(tlo, "sample", -1)
    got_a, got_b = y_exchange(block[:, :, 0:16], block[:, :, 112:128])
    w = fine_kernel.reshape(3456, 256)
    w9 = fine_kernel.reshape(9, 3, 128, 256)
    b = fine_bias.reshape(1, 256)
    mid_i, epool_i, eacc_i = fine_inner(block, w)

    def x_face(x):
        return jnp.concatenate([zlo[x : x + 1], block[:, x], zhi[x : x + 1]], 0)

    xlo, xhi = shift(x_face(7), "space", 1), shift(x_face(0), "space", -1)
    mid_z, epool_z, eacc_z = fine_ends(zlo, block, zhi, w)
    rzlo = shift(jnp.concatenate([got_a[7], got_b[7]], 0), "sample", 1)
    rzhi = shift(jnp.concatenate([got_a[0], got_b[0]], 0), "sample", -1)
    facc = fine_faces(flag, (got_a, got_b), w9, eacc_i, eacc_z)
    def rim(x):
        return jnp.concatenate(
            [rzlo[x : x + 1], got_a[:, x], rzhi[x : x + 1], rzlo[8 + x : 9 + x], got_b[:, x], rzhi[8 + x : 9 + x]], 0
        )

    rxlo, rxhi = shift(rim(7), "space", 1), shift(rim(0), "space", -1)
    sides = fine_sides(xlo, xhi, zlo, block, zhi, w, b, mid_i, epool_i, mid_z, epool_z)
    send = fine_last(flag, (rzlo, rzhi, rxlo, rxhi), w9, b, facc, sides)
    got = lax.all_to_all(send, ("sample", "space"), split_axis=0, concat_axis=0, tiled=True)

    got_a, got_b = y_exchange(got[:, 0:16], got[:, 48:64])
    pad = jnp.asarray(pad_matrix(), BF16)
    dw = deep_kernel.reshape(9, 3, 256, 256)
    acc = deep_first(got, pad, dw)
    send = deep_last(flag, got_a, got_b, pad, dw, deep_bias.reshape(1, 256), acc)
    got = lax.all_to_all(send, "chan", split_axis=0, concat_axis=0, tiled=True)
    return arrange(got, jnp.asarray(lane_matrix(), BF16))


def solution(mesh):
    placed = (P(None, "sample", "space", "chan", None), P(), P(), P(), P())
    return jax.shard_map(
        on_device,
        mesh=mesh,
        in_specs=placed,
        out_specs=P(("sample", "space"), "chan", None, None),
        check_vma=False,
    )
```
